32 devices in a mesh: group: 2 (over y), lon: 4 (over z), lat: 2 (over x), lev: 2 (over core).
Axes of the slice: x: 2, y: 2, z: 4, core: 2. Of those that a mesh axis runs over, the one named last changes fastest.
Arguments:
- fields: float32 [6, 64, 32, 512], P('lev', None, ('group', 'lat'), 'lon'), parts along dimension 2, may hold values from -6 to 6
- in_scale: float32 [6, 64], P('lev'), may hold values from 0.5 to 2
- out_scale: float32 [6, 64], P('lev'), may hold values from 0.3 to 1.5
- w_in: bfloat16 [256, 384], replicated, may hold values from -0.3125 to 0.3125
- w_mid: bfloat16 [3, 256, 256], replicated, may hold values from -0.375 to 0.375
- w_out: bfloat16 [384, 256], replicated, may hold values from -0.375 to 0.375
- storm_mask: int32 [32, 512], P(('group', 'lat'), 'lon'), parts along dimension 0, may hold values 0 or 1
- balance: int32 [32, 4], P(('group', 'lat')), parts along dimension 0, may hold values from -1 to 3, as said below
- substeps: int32 [64], replicated, may hold values from 1 to 3
- courant: float32 [2, 64], replicated, as said below
Outputs:
- advected: float32 [6, 64, 32, 512], P('lev', None, ('group', 'lat'), 'lon'), parts along dimension 2
The draws below stay inside these ranges and needn't reach their ends.
There are 2 independent parts, one for each index of `group`. The reference program is written for one: setup_inputs(seed, part) draws one part's arguments, and reference() takes and returns one part's arrays. A program takes and returns all parts, laid end to end along the dimension named above; an argument that names none is the same for every part. Nothing has to cross between parts.
Inputs may be any that keep to these rules, and one draw needn't show every extreme that they name: `balance`: entry (i, d) is -1, d, or a neighbour (d - 1) or (d + 1) modulo 4. Within the 8 rows of one latitude block, at most 2 spans of a block go to each neighbour, and every block computes at most 4 spans: those it keeps plus those it receives. |courant[k, l]| <= 0.95 * substeps[l].
All inputs are finite; a program needn't handle non-finite values. No bound on the sum of `storm_mask` on one device may be relied on, other than what follows from the above.
Results may differ from the reference program's by a relative error of at most 0.0019.
Values may be sent and summed in bfloat16 or wider, within the bound.
No kernel may reach another device: no remote copies, remote signals or barrier semaphores. Data moves between devices by JAX's collectives and lax.ppermute only.
A program may use at most 64 MiB of HBM per device.

```python
import math
import jax
import jax.numpy as jnp
from jax import lax

NTR = 6
LEVELS = 64
HID = 256
NMID = 3
SUBS = 3
CLON = 128
CLAT = 8
NLAT = 16
NLON = 512
N_LON = 4


def level_steps(key):
    key = jax.random.fold_in(key, 101)
    key_counts, key_top = jax.random.split(key)
    counts = jax.random.randint(key_counts, (LEVELS,), 1, SUBS + 1)
    top_level = jax.random.randint(key_top, (), 0, LEVELS)
    return jnp.where(jnp.arange(LEVELS) == top_level, SUBS, counts).astype(jnp.int32)


def draw_substeps(key, part):
    return level_steps(key)


def draw_courant(key, part):
    counts = level_steps(key).astype(jnp.float32)
    key = jax.random.fold_in(key, 5)
    key_size, key_sign = jax.random.split(key)
    magnitude = jax.random.uniform(key_size, (2, LEVELS), jnp.float32, 0.3, 0.95)
    signs = jnp.where(jax.random.bernoulli(key_sign, 0.5, (2, LEVELS)), 1.0, -1.0)
    return (signs * magnitude * counts[None, :]).astype(jnp.float32)


def draw_balance(key, part):
    key = jax.random.fold_in(key, 11)
    band_count = NLAT // CLAT
    slot_cap = CLAT // 4
    work_cap = CLAT // 2
    key_right, key_left, key_full, key_busy, key_slack, key_order = jax.random.split(key, 6)
    device_ids = jnp.arange(N_LON, dtype=jnp.int32)[None, :]
    sent_right = jax.random.randint(key_right, (band_count, N_LON), 0, slot_cap + 1)
    sent_left = jax.random.randint(key_left, (band_count, N_LON), 0, slot_cap + 1)
    full_device = jax.random.randint(key_full, (band_count, 1), 0, N_LON)
    sent_right = jnp.where(device_ids == full_device, slot_cap, sent_right)
    incoming = jnp.roll(sent_right, 1, axis=1) + jnp.roll(sent_left, -1, axis=1)
    room_left = work_cap - incoming
    busy_device = jax.random.randint(key_busy, (band_count, 1), 0, N_LON)
    slack = jax.random.randint(key_slack, (band_count, N_LON), 0, 2)
    kept_count = jnp.where(device_ids == busy_device, room_left, jnp.maximum(room_left - slack, 0))
    order_keys = jax.random.split(key_order, band_count * N_LON)
    orders = jax.vmap(lambda single: jax.random.permutation(single, CLAT))(order_keys)
    orders = jnp.transpose(orders.reshape(band_count, N_LON, CLAT), (0, 2, 1))
    kept_b = kept_count[:, None, :]
    left_b = sent_left[:, None, :]
    right_b = sent_right[:, None, :]
    owner = device_ids[:, None, :]
    target = jnp.where(orders < kept_b, owner, jnp.where(orders < kept_b + left_b, (owner - 1 + N_LON) % N_LON, jnp.where(orders < kept_b + left_b + right_b, (owner + 1) % N_LON, -1)))
    return target.reshape(NLAT, N_LON).astype(jnp.int32)


def touch_ends(values, key, low, largest):
    extent = values.shape
    spot = [jax.random.randint(jax.random.fold_in(key, axis), (), 0, extent[axis]) for axis in range(len(extent))]
    values = values.at[tuple(spot)].set(low)
    longest = extent.index(max(extent))
    spot[longest] = (spot[longest] + 1) % extent[longest]
    return values.at[tuple(spot)].set(largest)


def steps_of(key, shape, shards, least, high):
    level = 1.0
    for dim, shards_of in shards:
        steps = jax.random.uniform(jax.random.fold_in(jax.random.fold_in(key, 6), dim), (shards_of,), jnp.float32, least / len(shards), high / len(shards))
        level = level * jnp.repeat(jnp.exp(steps), shape[dim] // shards_of).reshape((-1,) + (1,) * (len(shape) - 1 - dim))
    return level


def gaussian(key, shape, spread, most, cuts=(), held_as=jnp.bfloat16):
    drawn = spread * jax.random.normal(key, shape, jnp.float32)
    if cuts:
        drawn = drawn * steps_of(key, shape, cuts, -0.22, 0.18)
    return jnp.clip(drawn, -most, most).astype(held_as)


def setup_inputs(seed: int = 0, part: int = 0) -> dict:
    key_list = jax.random.split(jax.random.key(seed), 11)
    part_keys = jax.random.split(jax.random.fold_in(key_list[10], part), 11)
    fields = gaussian(part_keys[0], (NTR, LEVELS, NLAT, NLON), 1.0, 6.0, ((0, 2), (2, 2), (3, 4)), jnp.float32)
    in_scale = jnp.clip(jnp.exp(math.log(2.0) - 1.3862944 * jax.random.uniform(key_list[1], (NTR, LEVELS), jnp.float32) ** steps_of(key_list[1], (NTR, LEVELS), ((0, 2),), -0.2, 0.2)), 0.5, 2.0)
    out_scale = jnp.clip(jnp.exp(math.log(1.5) - 1.60943787 * jax.random.uniform(key_list[2], (NTR, LEVELS), jnp.float32) ** steps_of(key_list[2], (NTR, LEVELS), ((0, 2),), -0.2, 0.2)), 0.3, 1.5)
    w_in = gaussian(key_list[3], (HID, NTR * LEVELS), (NTR * LEVELS) ** -0.5, 0.3125)
    w_mid = gaussian(key_list[4], (NMID, HID, HID), HID ** -0.5, 0.375)
    w_out = gaussian(key_list[5], (NTR * LEVELS, HID), HID ** -0.5, 0.375)
    storm_mask = touch_ends((jax.random.randint(part_keys[6], (NLAT, NLON), 0, 2) < 1).astype(jnp.int32), jax.random.fold_in(part_keys[6], 1), 0, 1)
    balance = draw_balance(jax.random.fold_in(jax.random.fold_in(key_list[10], part), 71), part)
    substeps = draw_substeps(jax.random.fold_in(key_list[10], 71), part)
    courant = draw_courant(jax.random.fold_in(key_list[10], 71), part)
    return {"fields": fields, "in_scale": in_scale, "out_scale": out_scale, "w_in": w_in, "w_mid": w_mid, "w_out": w_out, "storm_mask": storm_mask, "balance": balance, "substeps": substeps, "courant": courant}


def column_network(stacked, w_in, w_mid, w_out):
    hidden = jax.nn.silu(jnp.dot(w_in, stacked, preferred_element_type=jnp.float32)).astype(jnp.bfloat16)
    for layer in range(NMID):
        hidden = jax.nn.silu(jnp.dot(w_mid[layer], hidden, preferred_element_type=jnp.float32)).astype(jnp.bfloat16)
    return jnp.dot(w_out, hidden, preferred_element_type=jnp.float32).astype(jnp.bfloat16)


def donor_sweep(padded, step_lon, step_lat):
    east_lon = jnp.maximum(step_lon, 0.0)
    west_lon = jnp.minimum(step_lon, 0.0)
    flux_lon = east_lon * padded[..., :-1] + west_lon * padded[..., 1:]
    swept_lon = padded[..., 1:-1] - (flux_lon[..., 1:] - flux_lon[..., :-1])
    east_lat = jnp.maximum(step_lat, 0.0)
    west_lat = jnp.minimum(step_lat, 0.0)
    flux_lat = east_lat * swept_lon[..., :-1, :] + west_lat * swept_lon[..., 1:, :]
    return swept_lon[..., 1:-1, :] - (flux_lat[..., 1:, :] - flux_lat[..., :-1, :])


def reference(fields, in_scale, out_scale, w_in, w_mid, w_out, storm_mask, balance, substeps, courant):
    features = (fields * in_scale[:, :, None, None]).astype(jnp.bfloat16)

    def network_row(lat_row):
        stacked = lat_row.reshape(NTR * LEVELS, NLON)
        return column_network(stacked, w_in, w_mid, w_out).reshape(NTR, LEVELS, NLON)

    tendency = lax.map(network_row, jnp.moveaxis(features, 2, 0))
    tendency = jnp.moveaxis(tendency, 0, 2)
    convecting = jnp.repeat((balance >= 0).astype(jnp.int32), CLON, axis=1)
    active = (storm_mask * convecting).astype(jnp.float32)
    tracer_state = fields + out_scale[:, :, None, None] * tendency.astype(jnp.float32) * active[None, None]
    counts = substeps.astype(jnp.float32)
    for substep in range(SUBS):
        running = substeps > substep
        step_lon = jnp.where(running, courant[0] / counts, 0.0).reshape(1, LEVELS, 1, 1)
        step_lat = jnp.where(running, courant[1] / counts, 0.0).reshape(1, LEVELS, 1, 1)
        padded = jnp.concatenate([tracer_state[..., -1:], tracer_state, tracer_state[..., :1]], axis=3)
        padded = jnp.pad(padded, ((0, 0), (0, 0), (1, 1), (0, 0)))
        tracer_state = donor_sweep(padded, step_lon, step_lat)
    return tracer_state
```

```python
import functools

import jax
import jax.numpy as jnp
from jax import lax
from jax.experimental import pallas as pl
from jax.experimental.pallas import tpu as pltpu
from jax.sharding import PartitionSpec as P

W = 3
LANES = 128
EXTRA = 8
F32 = jnp.float32
BF16 = jnp.bfloat16
VMEM_LIMIT = 40 * 1024 * 1024


def lane_ids(rows):
    return lax.broadcasted_iota(jnp.int32, (rows, LANES), 1)


def turned(x, shift):
    if isinstance(shift, int):
        shift %= LANES
        if shift == 0:
            return x
    return pltpu.roll(x, shift, 1)


def silu(v):
    half = 0.5 * v
    return half + half * jnp.tanh(half)


def as_columns(scratch, parts):
    scratch[...] = jnp.zeros_like(scratch)
    at = 0
    for part in parts:
        scratch[at : at + part.shape[0], : part.shape[1]] = part
        at += part.shape[0]
    return scratch[...].T


def column(turned_rows, index, levels):
    return jnp.broadcast_to(turned_rows[:levels, index : index + 1], (levels, LANES))


def side_packs(edges):
    lane = lane_ids(edges[0].shape[0])
    east = lane % 6 < 3
    last = [jnp.where(east, e, 0.0) for e in edges]
    first = [jnp.where(east, 0.0, e) for e in edges]
    east_pack = last[0] + turned(last[1], 3) + turned(last[2], 48)
    west_pack = turned(first[0], -3) + first[1] + turned(first[2], 45)
    return east_pack, west_pack


def prepare_kernel(tracers, levels, rows, moves, fields, in_scale, storm, balance, features, keep, give, active, *rest):
    edge_rows, (scratch,) = rest[: len(moves)], rest[len(moves) :]
    lon, lat, lev = (lax.axis_index(name) for name in ("lon", "lat", "lev"))
    position = lax.broadcasted_iota(jnp.int32, balance.shape, 1)
    target = jnp.max(jnp.where(position == lon, balance[...], -1).astype(F32), axis=1, keepdims=True)
    mask = jnp.where(target >= 0.0, storm[...].astype(F32), 0.0)
    active[...] = mask
    scales = as_columns(scratch, [in_scale[...]])
    lane = lane_ids(levels)
    edges = []
    scale_lanes = jnp.zeros((levels, LANES), F32)
    for t in range(tracers):
        scale = column(scales, t, levels)
        scale_lanes = jnp.where(lane == 96 + t, scale, scale_lanes)
        pack = jnp.zeros((levels, LANES), F32)
        for i in range(rows):
            x = fields[pl.ds(t * levels * rows + i, levels, stride=rows), :]
            features[i, t * levels : (t + 1) * levels, :] = (x * scale).astype(BF16)
            pack = jnp.where((lane >= 6 * i) & (lane < 6 * i + 6), turned(x, 6 * i + W), pack)
        edges.append(pack)
    lane = lane_ids(1)
    mask_pack = jnp.zeros((1, LANES), F32)
    for i in range(rows):
        mask_pack = jnp.where((lane >= 6 * i) & (lane < 6 * i + 6), turned(active[i : i + 1, :], 6 * i + W), mask_pack)
    mask_pack = jnp.broadcast_to(mask_pack, (EXTRA, LANES))
    none = jnp.zeros_like(mask_pack)
    last_pack, first_pack = side_packs(edges)
    last_mask, first_mask = side_packs([mask_pack, none, none])
    head = lev == 0
    keep[:levels] = jnp.where(head, last_pack, first_pack) + scale_lanes
    give[:levels] = jnp.where(head, first_pack, last_pack) + scale_lanes
    keep[levels:] = jnp.where(head, last_mask, first_mask)
    give[levels:] = jnp.where(head, first_mask, last_mask)
    for move, out in zip(moves, edge_rows):
        start = first_row_sent(move, lat, rows)
        for r in range(W):
            for t in range(tracers):
                x = fields[pl.ds(t * levels * rows + start + r, levels, stride=rows), :]
                out[(r * tracers + t) * levels : (r * tracers + t + 1) * levels, :] = x
        tail = W * tracers * levels
        for r in range(W):
            out[tail + r : tail + r + 1, :] = active[pl.ds(start + r, 1), :]
        out[tail + W :, :] = jnp.zeros((EXTRA - W, LANES), F32)


def first_row_sent(move, lat, rows):
    if move == 0:
        return jnp.where(lat == 0, rows - W, 0)
    return rows - W if move > 0 else 0


def first_row_received(move, lat, rows):
    if move == 0:
        return jnp.where(lat == 0, 0, rows - W)
    return rows - W if move > 0 else 0


def network(x, w_in, w_mid, w_last):
    hidden = silu(jnp.dot(w_in, x, preferred_element_type=F32)).astype(BF16)
    for layer in range(len(w_mid)):
        hidden = silu(jnp.dot(w_mid[layer], hidden, preferred_element_type=F32)).astype(BF16)
    return jnp.dot(w_last, hidden, preferred_element_type=F32).astype(BF16)


def taps(step, count):
    first = jnp.abs(step)
    second = jnp.where(count > 1.5, first, 0.0)
    third = jnp.where(count > 2.5, first, 0.0)
    rest = [1.0 - a for a in (first, second, third)]
    return (
        rest[0] * rest[1] * rest[2],
        first * rest[1] * rest[2] + rest[0] * second * rest[2] + rest[0] * rest[1] * third,
        first * second * rest[2] + first * rest[1] * third + rest[0] * second * third,
        first * second * third,
    )


OUT_SCALE, LON, LON_SIGN, LAT, LAT_SIGN, EDGE, PLANES = 0, 3, 7, 8, 12, 13, 18


def write_weights(weights, scratch, out_scale, courant, substeps, levels):
    columns = as_columns(scratch, [out_scale[...], courant[...], substeps[...].astype(F32)])
    tracers = out_scale.shape[0]
    for t in range(tracers):
        weights[OUT_SCALE + t] = column(columns, t, levels)
    count = column(columns, tracers + 2, levels)
    lane = lane_ids(levels)
    place = lane % 6
    step = column(columns, tracers, levels) / count
    up = step > 0.0
    w = taps(step, count)
    weights[LON_SIGN] = jnp.where(up, 1.0, 0.0)
    for k in range(4):
        weights[LON + k] = jnp.where(
            up, jnp.where(lane >= k, w[k], 0.0), jnp.where(lane < LANES - (W - k), w[W - k], 0.0)
        )
    east = [jnp.where(up | (place > 2) | (place < d), 0.0, w[W - d]) for d in range(3)]
    west = [jnp.where(up & (place > 2) & (place + d < 6), w[W - d], 0.0) for d in range(3)]
    weights[EDGE] = east[0] + west[0]
    weights[EDGE + 1] = east[1]
    weights[EDGE + 2] = west[1]
    weights[EDGE + 3] = east[2]
    weights[EDGE + 4] = west[2]
    step = column(columns, tracers + 1, levels) / count
    up = step > 0.0
    w = taps(step, count)
    weights[LAT_SIGN] = jnp.where(up, 1.0, 0.0)
    for k in range(4):
        weights[LAT + k] = jnp.where(up, w[W - k], w[k])


def sweep_lon(q, weights, span):
    up = weights[LON_SIGN, span, :] > 0.5
    q = jnp.where(up, q, turned(q, -W))
    total = weights[LON, span, :] * q
    for k in range(1, 4):
        total += weights[LON + k, span, :] * turned(q, k)
    return total


def own_kernel(
    tracers, levels, rows, fields, mine, other, w_in, w_mid, w_out, out_scale, courant, substeps, active,
    swept, weights, x, tendency, scratch,
):
    lev = lax.axis_index("lev")
    width = tracers * levels
    write_weights(weights, scratch, out_scale, courant, substeps, levels)
    near = pl.ds(pl.multiple_of(lev * width, width), width)
    far = pl.ds(pl.multiple_of((1 - lev) * width, width), width)
    w_last = w_out[near, :]
    for i in range(rows):
        x[near, i * LANES : (i + 1) * LANES] = mine[i]
        x[far, i * LANES : (i + 1) * LANES] = other[i]
    step = 2 * LANES
    for j in range(0, rows * LANES, step):
        tendency[:, j : j + step] = network(x[:, j : j + step], w_in[...], w_mid, w_last)
    for t in range(tracers):
        for i in range(rows):
            for g in range(0, levels, 16):
                span = slice(g, g + 16)
                at = t * levels + g
                q = fields[pl.ds(at * rows + i, 16, stride=rows), :]
                moist = tendency[at : at + 16, i * LANES : (i + 1) * LANES].astype(F32)
                q = q + weights[OUT_SCALE + t, span, :] * moist * active[i : i + 1, :]
                swept[i, at : at + 16, :] = sweep_lon(q, weights, span)


def finish_kernel(tracers, levels, rows, moves, *refs):
    count = len(moves)
    swept, weights, w_in, w_mid, w_out, packs, ring, ring_other = refs[:8]
    corner, corner_other, edge, edge_other = (refs[8 + n * count : 8 + (n + 1) * count] for n in range(4))
    out, x, tendency, halo, mask_rows = refs[8 + 4 * count :]
    lat, lev = lax.axis_index("lat"), lax.axis_index("lev")
    width = tracers * levels
    block = levels + EXTRA
    head = lev == 0
    near = pl.ds(pl.multiple_of(lev * width, width), width)
    far = pl.ds(pl.multiple_of((1 - lev) * width, width), width)
    w_last = w_out[near, :]

    def sides(received, forwarded):
        own_r, other_r = received[:block], received[block:]
        other_f, own_f = forwarded[:block], forwarded[block:]
        return (
            (jnp.where(head, own_r, own_f), jnp.where(head, own_f, own_r)),
            (jnp.where(head, other_r, other_f), jnp.where(head, other_f, other_r)),
        )

    ring_sides = sides(ring, ring_other)
    corner_sides = [sides(c, f) for c, f in zip(corner, corner_other)]
    lane = lane_ids(levels)
    east = lane % 6 < 3

    def unpack(which, t, part):
        shift_east = (0, -3, -48)[t]
        shift_west = (3, 0, -45)[t]
        west_pack, east_pack = ring_sides[which]
        picked = east[: part.stop - part.start]
        value = jnp.where(picked, turned(east_pack[part], shift_east), turned(west_pack[part], shift_west))
        lane_part = lane[: part.stop - part.start]
        for n, move in enumerate(moves):
            west_pack, east_pack = corner_sides[n][which]
            base = 48 + 18 * n
            shift = base - 6 * first_row_received(move, lat, rows) + 2 * LANES
            far_value = jnp.where(
                picked, turned(east_pack[part], (shift + shift_east) % LANES), turned(west_pack[part], (shift + shift_west) % LANES)
            )
            value = jnp.where((lane_part >= base) & (lane_part < base + 18), far_value, value)
        return jnp.where(lane_part < 48 + 18 * count, value, 0.0)

    for which, place in ((0, near), (1, far)):
        start = lev * width if which == 0 else (1 - lev) * width
        source = edge if which == 0 else edge_other
        for t in range(tracers):
            scale = jnp.broadcast_to(packs[which * block : which * block + levels, 96 + t : 97 + t], (levels, LANES))
            to = pl.ds(pl.multiple_of(start + t * levels, levels), levels)
            value = unpack(which, t, slice(0, levels))
            if which == 0:
                halo[t] = value
            x[to, :LANES] = (value * scale).astype(BF16)
            for n in range(count):
                for r in range(W):
                    column_at = (1 + n * W + r) * LANES
                    value = source[n][(r * tracers + t) * levels : (r * tracers + t + 1) * levels, :]
                    x[to, column_at : column_at + LANES] = (value * scale).astype(BF16)
    mask_rows[...] = unpack(0, 0, slice(levels, block))
    total = (1 + W * count) * LANES
    step = 2 * LANES
    for j in range(0, total, step):
        stop = min(j + step, total)
        tendency[:, j:stop] = network(x[:, j:stop], w_in[...], w_mid, w_last)

    tail = W * tracers * levels
    lane = lane_ids(8)
    at_edge = (lane < W) | (lane >= LANES - W)
    southward = jnp.where(lat == 0, 0.0, 1.0)
    for t in range(tracers):
        for g in range(0, levels, 16):
            span = slice(g, g + 16)
            at = t * levels + g
            lane = lane_ids(16)
            at_edge = (lane < W) | (lane >= LANES - W)
            scale = weights[OUT_SCALE + t, span, :]
            up = weights[LAT_SIGN, span, :] > 0.5

            def physics(value, column_at, mask):
                return value + scale * tendency[at : at + 16, column_at : column_at + LANES].astype(F32) * mask

            sides_q = physics(halo[t, span, :], 0, mask_rows[0:1, :])
            if count == 2:
                sides_q = jnp.where(up | (lane < 48), sides_q, turned(sides_q, -18))
            fix = weights[EDGE, span, :] * sides_q
            for k, shift in ((1, 1), (2, -1), (3, 2), (4, -2)):
                fix += weights[EDGE + k, span, :] * turned(sides_q, shift)

            def fixed(value, first):
                return value + jnp.where(at_edge, turned(fix, LANES - W - first), 0.0)

            beyond = []
            for r in range(W):
                rows_q = [
                    physics(
                        edge[n][(r * tracers + t) * levels + g : (r * tracers + t) * levels + g + 16, :],
                        (1 + n * W + r) * LANES,
                        edge[n][tail + r : tail + r + 1, :],
                    )
                    for n in range(count)
                ]
                q = jnp.where(up, rows_q[0], rows_q[-1])
                q = fixed(sweep_lon(q, weights, span), 48 + 6 * r)
                if count == 1:
                    q = jnp.where(weights[LAT_SIGN, span, :] == southward, q, 0.0)
                beyond.append(q)
            inner = [fixed(swept[i, at : at + 16, :], 6 * i) for i in range(rows)]
            line = []
            for i in range(rows + W):
                above = beyond[i] if i < W else inner[i - W]
                below = inner[i] if i < rows else beyond[i - rows]
                line.append(jnp.where(up, above, below))
            for i in range(rows):
                value = weights[LAT, span, :] * line[i]
                for k in range(1, 4):
                    value += weights[LAT + k, span, :] * line[i + k]
                out[pl.ds(at * rows + i, 16, stride=rows), :] = value


def call(kernel, out_shape, scratch, flops, moved, name):
    return pl.pallas_call(
        kernel,
        out_shape=out_shape,
        scratch_shapes=scratch,
        compiler_params=pltpu.CompilerParams(vmem_limit_bytes=VMEM_LIMIT),
        cost_estimate=pl.CostEstimate(flops=flops, bytes_accessed=moved, transcendentals=0),
        name=name,
    )


def swap_cores(x):
    return lax.ppermute(x, "lev", [(0, 1), (1, 0)])


def routes(lon_count, lat_count, move, along_lon):
    pairs = []
    for i in range(lon_count):
        for j in range(lat_count):
            to_lat = 1 - j if move == 0 else j + (move or 0)
            if not 0 <= to_lat < lat_count:
                continue
            for k in range(2):
                to_lon = (i + (1 - 2 * k)) % lon_count if along_lon else i
                pairs.append((((i * lat_count) + j) * 2 + k, ((to_lon * lat_count) + to_lat) * 2 + k))
    return pairs


def send(x, move, along_lon):
    axes = ("lon", "lat", "lev")
    lon_count, lat_count = lax.axis_size("lon"), lax.axis_size("lat")
    if move is None:
        pairs = []
        for i in range(lon_count):
            for j in range(lat_count):
                for k in range(2):
                    to_lon = (i + (1 - 2 * k)) % lon_count
                    pairs.append(((i * lat_count + j) * 2 + k, (to_lon * lat_count + j) * 2 + k))
    else:
        pairs = routes(lon_count, lat_count, move, along_lon)
    return lax.ppermute(x, axes, pairs)


def on_device(fields, in_scale, out_scale, w_in, w_mid, w_out, storm_mask, balance, substeps, courant):
    tracers, levels, rows, columns = fields.shape
    width = tracers * levels
    moves = (0,) if lax.axis_size("lat") == 2 else (1, -1)
    count = len(moves)
    flat = fields.reshape(width * rows, columns)
    block = levels + EXTRA
    edge_shape = jax.ShapeDtypeStruct((W * width + EXTRA, columns), F32)
    pack_shape = jax.ShapeDtypeStruct((block, LANES), F32)
    features, keep, give, active, *edge_rows = call(
        functools.partial(prepare_kernel, tracers, levels, rows, moves),
        [jax.ShapeDtypeStruct((rows, width, columns), BF16), pack_shape, pack_shape,
         jax.ShapeDtypeStruct((rows, columns), F32)] + [edge_shape] * count,
        [pltpu.VMEM((8, LANES), F32)],
        10**6, 2 * 10**6, "prepare",
    )(flat, in_scale, storm_mask, balance)

    given = swap_cores(give)
    features_other = swap_cores(features)
    edge = [send(e, move, False) for e, move in zip(edge_rows, moves)]
    packs = jnp.concatenate([keep, given], axis=0)
    corner = [send(packs, move, True) for move in moves]
    ring = send(packs, None, True)

    swept, weights = call(
        functools.partial(own_kernel, tracers, levels, rows),
        [jax.ShapeDtypeStruct((rows, width, columns), F32), jax.ShapeDtypeStruct((PLANES, levels, LANES), F32)],
        [pltpu.VMEM((2 * width, rows * columns), BF16), pltpu.VMEM((width, rows * columns), BF16),
         pltpu.VMEM((8, LANES), F32)],
        10**9, 4 * 10**6, "own_columns",
    )(flat, features, features_other, w_in, w_mid, w_out, out_scale, courant, substeps.reshape(1, levels), active)

    ring_other = swap_cores(ring)
    corner_other = [swap_cores(c) for c in corner]
    edge_other = [swap_cores(e) for e in edge]
    total = (1 + W * count) * LANES
    out = call(
        functools.partial(finish_kernel, tracers, levels, rows, moves),
        jax.ShapeDtypeStruct((width * rows, columns), F32),
        [pltpu.VMEM((2 * width, total), BF16), pltpu.VMEM((width, total), BF16),
         pltpu.VMEM((tracers, levels, LANES), F32), pltpu.VMEM((EXTRA, LANES), F32)],
        10**9, 4 * 10**6, "finish",
    )(swept, weights, w_in, w_mid, w_out, packs, ring, ring_other, *corner, *corner_other, *edge, *edge_other)
    return out.reshape(fields.shape)


def solution(mesh):
    in_specs = (
        P("lev", None, ("group", "lat"), "lon"),
        P("lev", None),
        P("lev", None),
        P(),
        P(),
        P(),
        P(("group", "lat"), "lon"),
        P(("group", "lat"), None),
        P(),
        P(),
    )
    out_specs = P("lev", None, ("group", "lat"), "lon")
    return jax.shard_map(
        on_device, mesh=mesh, in_specs=in_specs, out_specs=out_specs, check_vma=False
    )
```

```python
import functools

import jax
import jax.numpy as jnp
from jax import lax
from jax.experimental import pallas as pl
from jax.experimental.pallas import tpu as pltpu
from jax.sharding import PartitionSpec as P

W = 3
LANES = 128
EXTRA = 8
F32 = jnp.float32
BF16 = jnp.bfloat16
GROUP = 32
HALF_GROUP = 16
VMEM_LIMIT = 40 * 1024 * 1024


def lane_ids(rows):
    return lax.broadcasted_iota(jnp.int32, (rows, LANES), 1)


def turned(x, shift):
    if isinstance(shift, int):
        shift %= LANES
        if shift == 0:
            return x
    return pltpu.roll(x, shift, 1)


def silu(v):
    half = 0.5 * v
    return half + half * jnp.tanh(half)


def as_columns(scratch, parts):
    scratch[...] = jnp.zeros_like(scratch)
    at = 0
    for part in parts:
        scratch[at : at + part.shape[0], : part.shape[1]] = part
        at += part.shape[0]
    return scratch[...].T


def column(turned_rows, index, levels):
    return jnp.broadcast_to(turned_rows[:levels, index : index + 1], (levels, LANES))


def side_packs(edges):
    lane = lane_ids(edges[0].shape[0])
    east = lane % 6 < 3
    last = [jnp.where(east, e, 0.0) for e in edges]
    first = [jnp.where(east, 0.0, e) for e in edges]
    east_pack = last[0] + turned(last[1], 3) + turned(last[2], 48)
    west_pack = turned(first[0], -3) + first[1] + turned(first[2], 45)
    return east_pack, west_pack


def prepare_kernel(tracers, levels, rows, moves, *refs):
    sources, refs = refs[:7], refs[7:]
    features, keep, give, active, small = refs[:5]
    edge_rows, refs = refs[5 : 5 + len(moves)], refs[5 + len(moves) :]
    (fields, in_scale, storm, balance, *loads), scratch, sems = refs[:7], refs[7], refs[8]
    part = levels * rows
    copies = [
        pltpu.make_async_copy(source, into, sems.at[n])
        for n, (source, into) in enumerate(zip(sources[1:], (in_scale, storm, balance, *loads)))
    ]
    chunks = [
        pltpu.make_async_copy(
            sources[0].at[pl.ds(t * part, part)], fields.at[pl.ds(t * part, part)], sems.at[len(copies) + t]
        )
        for t in range(tracers)
    ]
    for copy in copies + chunks:
        copy.start()
    for copy in copies:
        copy.wait()
    small[...] = jnp.zeros_like(small)
    at = 0
    for load in loads:
        small[at : at + load.shape[0], : load.shape[1]] = load[...].astype(F32)
        at += load.shape[0]
    lon, lat, lev = (lax.axis_index(name) for name in ("lon", "lat", "lev"))
    position = lax.broadcasted_iota(jnp.int32, balance.shape, 0)
    target = jnp.max(jnp.where(position == lon, balance[...], -1).astype(F32), axis=0, keepdims=True)
    scales = as_columns(scratch, [in_scale[...], target])
    mask = jnp.where(column(scales, tracers, rows) >= 0.0, storm[...].astype(F32), 0.0)
    active[...] = mask
    lane = lane_ids(levels)
    edges = []
    scale_lanes = jnp.zeros((levels, LANES), F32)
    for t in range(tracers):
        chunks[t].wait()
        scale = column(scales, t, levels)
        scale_lanes = jnp.where(lane == 96 + t, scale, scale_lanes)
        pack = jnp.zeros((levels, LANES), F32)
        for i in range(rows):
            x = fields[pl.ds(t * levels * rows + i, levels, stride=rows), :]
            features[i, t * levels : (t + 1) * levels, :] = (x * scale).astype(BF16)
            pack = jnp.where((lane >= 6 * i) & (lane < 6 * i + 6), turned(x, 6 * i + W), pack)
        edges.append(pack)
    lane = lane_ids(1)
    mask_pack = jnp.zeros((1, LANES), F32)
    for i in range(rows):
        mask_pack = jnp.where((lane >= 6 * i) & (lane < 6 * i + 6), turned(active[i : i + 1, :], 6 * i + W), mask_pack)
    mask_pack = jnp.broadcast_to(mask_pack, (EXTRA, LANES))
    none = jnp.zeros_like(mask_pack)
    last_pack, first_pack = side_packs(edges)
    last_mask, first_mask = side_packs([mask_pack, none, none])
    head = lev == 0
    keep[:levels] = jnp.where(head, last_pack, first_pack) + scale_lanes
    give[:levels] = jnp.where(head, first_pack, last_pack) + scale_lanes
    keep[levels:] = jnp.where(head, last_mask, first_mask)
    give[levels:] = jnp.where(head, first_mask, last_mask)
    for move, out in zip(moves, edge_rows):
        start = first_row_sent(move, lat, rows)
        for r in range(W):
            for t in range(tracers):
                x = fields[pl.ds(t * levels * rows + start + r, levels, stride=rows), :]
                out[(r * tracers + t) * levels : (r * tracers + t + 1) * levels, :] = x
        tail = W * tracers * levels
        for r in range(W):
            out[tail + r : tail + r + 1, :] = active[pl.ds(start + r, 1), :]
        out[tail + W :, :] = jnp.zeros((EXTRA - W, LANES), F32)


def first_row_sent(move, lat, rows):
    if move == 0:
        return jnp.where(lat == 0, rows - W, 0)
    return rows - W if move > 0 else 0


def first_row_received(move, lat, rows):
    if move == 0:
        return jnp.where(lat == 0, 0, rows - W)
    return rows - W if move > 0 else 0


def network(x, w_in, w_mid, w_last):
    hidden = silu(jnp.dot(w_in, x, preferred_element_type=F32)).astype(BF16)
    for layer in range(len(w_mid)):
        hidden = silu(jnp.dot(w_mid[layer], hidden, preferred_element_type=F32)).astype(BF16)
    return jnp.dot(w_last, hidden, preferred_element_type=F32).astype(BF16)


def taps(step, count):
    first = jnp.abs(step)
    second = jnp.where(count > 1.5, first, 0.0)
    third = jnp.where(count > 2.5, first, 0.0)
    rest = [1.0 - a for a in (first, second, third)]
    return (
        rest[0] * rest[1] * rest[2],
        first * rest[1] * rest[2] + rest[0] * second * rest[2] + rest[0] * rest[1] * third,
        first * second * rest[2] + first * rest[1] * third + rest[0] * second * third,
        first * second * third,
    )


OUT_SCALE, LON, LON_SIGN, LAT, LAT_SIGN, EDGE, PLANES = 0, 3, 7, 8, 12, 13, 18


def write_weights(weights, small, tracers, levels):
    columns = small[...].T
    for t in range(tracers):
        weights[OUT_SCALE + t] = column(columns, t, levels)
    count = column(columns, tracers + 2, levels)
    lane = lane_ids(levels)
    place = lane % 6
    step = column(columns, tracers, levels) / count
    up = step > 0.0
    w = taps(step, count)
    weights[LON_SIGN] = jnp.where(up, 1.0, 0.0)
    for k in range(4):
        weights[LON + k] = jnp.where(
            up, jnp.where(lane >= k, w[k], 0.0), jnp.where(lane < LANES - (W - k), w[W - k], 0.0)
        )
    east = [jnp.where(up | (place > 2) | (place < d), 0.0, w[W - d]) for d in range(3)]
    west = [jnp.where(up & (place > 2) & (place + d < 6), w[W - d], 0.0) for d in range(3)]
    weights[EDGE] = east[0] + west[0]
    weights[EDGE + 1] = east[1]
    weights[EDGE + 2] = west[1]
    weights[EDGE + 3] = east[2]
    weights[EDGE + 4] = west[2]
    step = column(columns, tracers + 1, levels) / count
    up = step > 0.0
    w = taps(step, count)
    weights[LAT_SIGN] = jnp.where(up, 1.0, 0.0)
    for k in range(4):
        weights[LAT + k] = jnp.where(up, w[W - k], w[k])


def sweep_lon(values, weights, span):
    up = weights[LON_SIGN, span, :] > 0.5
    values = [jnp.where(up, q, turned(q, -W)) for q in values]
    w = [weights[LON + k, span, :] for k in range(4)]
    return [w[0] * q + w[1] * turned(q, 1) + w[2] * turned(q, 2) + w[3] * turned(q, 3) for q in values]


def own_network_kernel(tracers, levels, rows, mine, other, w_in, w_mid, w_out, tendency, token, x):
    lev = lax.axis_index("lev")
    width = tracers * levels
    token[...] = jnp.zeros_like(token)
    near = pl.ds(pl.multiple_of(lev * width, width), width)
    far = pl.ds(pl.multiple_of((1 - lev) * width, width), width)
    w_last = w_out[near, :]
    for i in range(rows):
        x[near, i * LANES : (i + 1) * LANES] = mine[i]
        x[far, i * LANES : (i + 1) * LANES] = other[i]
    tendency[...] = network(x[...], w_in[...], w_mid, w_last)


def own_sweep_kernel(tracers, levels, rows, fields, tendency, small, active, swept, weights):
    write_weights(weights, small, tracers, levels)
    for g in range(0, levels, GROUP):
        span = slice(g, g + GROUP)
        for t in range(tracers):
            at = t * levels + g
            scale = weights[OUT_SCALE + t, span, :]
            values = []
            for i in range(rows):
                moist = tendency[at : at + GROUP, i * LANES : (i + 1) * LANES].astype(F32)
                q = fields[pl.ds(at * rows + i, GROUP, stride=rows), :]
                values.append(q + scale * moist * active[i : i + 1, :])
            for i, q in enumerate(sweep_lon(values, weights, span)):
                swept[i, at : at + GROUP, :] = q


def finish_kernel(tracers, levels, rows, moves, *refs):
    count = len(moves)
    swept, weights, w_in, w_mid, w_out, packs, ring, ring_other = refs[:8]
    corner, corner_other, edge, edge_other = (refs[8 + n * count : 8 + (n + 1) * count] for n in range(4))
    out, x, tendency, halo, mask_rows, fixes, beyond = refs[8 + 4 * count :]
    lat, lev = lax.axis_index("lat"), lax.axis_index("lev")
    width = tracers * levels
    block = levels + EXTRA
    head = lev == 0
    near = pl.ds(pl.multiple_of(lev * width, width), width)
    far = pl.ds(pl.multiple_of((1 - lev) * width, width), width)
    w_last = w_out[near, :]

    def sides(received, forwarded):
        own_r, other_r = received[:block], received[block:]
        other_f, own_f = forwarded[:block], forwarded[block:]
        return (
            (jnp.where(head, own_r, own_f), jnp.where(head, own_f, own_r)),
            (jnp.where(head, other_r, other_f), jnp.where(head, other_f, other_r)),
        )

    ring_sides = sides(ring, ring_other)
    corner_sides = [sides(c, f) for c, f in zip(corner, corner_other)]
    lane = lane_ids(levels)
    east = lane % 6 < 3

    def unpack(which, t, part):
        shift_east = (0, -3, -48)[t]
        shift_west = (3, 0, -45)[t]
        west_pack, east_pack = ring_sides[which]
        picked = east[: part.stop - part.start]
        value = jnp.where(picked, turned(east_pack[part], shift_east), turned(west_pack[part], shift_west))
        lane_part = lane[: part.stop - part.start]
        for n, move in enumerate(moves):
            west_pack, east_pack = corner_sides[n][which]
            base = 48 + 18 * n
            shift = base - 6 * first_row_received(move, lat, rows) + 2 * LANES
            far_value = jnp.where(
                picked, turned(east_pack[part], (shift + shift_east) % LANES), turned(west_pack[part], (shift + shift_west) % LANES)
            )
            value = jnp.where((lane_part >= base) & (lane_part < base + 18), far_value, value)
        return jnp.where(lane_part < 48 + 18 * count, value, 0.0)

    for which, place in ((0, near), (1, far)):
        start = lev * width if which == 0 else (1 - lev) * width
        source = edge if which == 0 else edge_other
        for t in range(tracers):
            scale = jnp.broadcast_to(packs[which * block : which * block + levels, 96 + t : 97 + t], (levels, LANES))
            to = pl.ds(pl.multiple_of(start + t * levels, levels), levels)
            value = unpack(which, t, slice(0, levels))
            if which == 0:
                halo[t] = value
            x[to, :LANES] = (value * scale).astype(BF16)
            for n in range(count):
                for r in range(W):
                    column_at = (1 + n * W + r) * LANES
                    value = source[n][(r * tracers + t) * levels : (r * tracers + t + 1) * levels, :]
                    x[to, column_at : column_at + LANES] = (value * scale).astype(BF16)
    mask_rows[...] = unpack(0, 0, slice(levels, block))
    tendency[...] = network(x[...], w_in[...], w_mid, w_last)

    tail = W * tracers * levels
    lane = lane_ids(levels)
    southward = jnp.where(lat == 0, 0.0, 1.0)
    everything = slice(0, levels)
    for t in range(tracers):
        at = t * levels
        scale = weights[OUT_SCALE + t]
        up = weights[LAT_SIGN] > 0.5

        def physics(value, column_at, mask):
            return value + scale * tendency[at : at + levels, column_at : column_at + LANES].astype(F32) * mask

        sides_q = physics(halo[t], 0, mask_rows[0:1, :])
        if count == 2:
            sides_q = jnp.where(up | (lane < 48), sides_q, turned(sides_q, -18))
        fix = weights[EDGE] * sides_q
        for k, shift in ((1, 1), (2, -1), (3, 2), (4, -2)):
            fix += weights[EDGE + k] * turned(sides_q, shift)
        values = []
        for r in range(W):
            rows_q = [
                physics(
                    edge[n][(r * tracers + t) * levels : (r * tracers + t + 1) * levels, :],
                    (1 + n * W + r) * LANES,
                    edge[n][tail + r : tail + r + 1, :],
                )
                for n in range(count)
            ]
            values.append(jnp.where(up, rows_q[0], rows_q[-1]))
        values = sweep_lon(values, weights, everything)
        at_edge = (lane < W) | (lane >= LANES - W)
        values = [q + jnp.where(at_edge, turned(fix, LANES - W - 48 - 6 * r), 0.0) for r, q in enumerate(values)]
        if count == 1:
            values = [jnp.where(weights[LAT_SIGN] == southward, q, 0.0) for q in values]
        fixes[t] = fix
        for r, q in enumerate(values):
            beyond[t * W + r] = q

    lane = lane_ids(HALF_GROUP)
    at_edge = (lane < W) | (lane >= LANES - W)
    for g in range(0, levels, HALF_GROUP):
        span = slice(g, g + HALF_GROUP)
        up = weights[LAT_SIGN, span, :] > 0.5
        w = [weights[LAT + k, span, :] for k in range(4)]
        for t in range(tracers):
            at = t * levels + g
            fix = fixes[t, span, :]
            inner = [
                swept[i, at : at + HALF_GROUP, :] + jnp.where(at_edge, turned(fix, LANES - W - 6 * i), 0.0)
                for i in range(rows)
            ]
            outer = [beyond[t * W + r, span, :] for r in range(W)]
            line = []
            for i in range(rows + W):
                above = outer[i] if i < W else inner[i - W]
                below = inner[i] if i < rows else outer[i - rows]
                line.append(jnp.where(up, above, below))
            results = [w[0] * line[i] + w[1] * line[i + 1] + w[2] * line[i + 2] + w[3] * line[i + 3] for i in range(rows)]
            for i, value in enumerate(results):
                out[pl.ds(at * rows + i, HALF_GROUP, stride=rows), :] = value


def call(kernel, out_shape, scratch, flops, moved, name, **specs):
    return pl.pallas_call(
        kernel,
        out_shape=out_shape,
        **specs,
        scratch_shapes=scratch,
        compiler_params=pltpu.CompilerParams(vmem_limit_bytes=VMEM_LIMIT),
        cost_estimate=pl.CostEstimate(flops=flops, bytes_accessed=moved, transcendentals=0),
        name=name,
    )


def swap_cores(x):
    return lax.ppermute(x, "lev", [(0, 1), (1, 0)])


def routes(lon_count, lat_count, move, along_lon):
    pairs = []
    for i in range(lon_count):
        for j in range(lat_count):
            to_lat = 1 - j if move == 0 else j + (move or 0)
            if not 0 <= to_lat < lat_count:
                continue
            for k in range(2):
                to_lon = (i + (1 - 2 * k)) % lon_count if along_lon else i
                pairs.append((((i * lat_count) + j) * 2 + k, ((to_lon * lat_count) + to_lat) * 2 + k))
    return pairs


def send(x, move, along_lon):
    axes = ("lon", "lat", "lev")
    lon_count, lat_count = lax.axis_size("lon"), lax.axis_size("lat")
    if move is None:
        pairs = []
        for i in range(lon_count):
            for j in range(lat_count):
                for k in range(2):
                    to_lon = (i + (1 - 2 * k)) % lon_count
                    pairs.append(((i * lat_count + j) * 2 + k, (to_lon * lat_count + j) * 2 + k))
    else:
        pairs = routes(lon_count, lat_count, move, along_lon)
    return lax.ppermute(x, axes, pairs)


def on_device(fields, in_scale, out_scale, w_in, w_mid, w_out, storm_mask, balance, substeps, courant):
    tracers, levels, rows, columns = fields.shape
    width = tracers * levels
    moves = (0,) if lax.axis_size("lat") == 2 else (1, -1)
    count = len(moves)
    flat = fields.reshape(width * rows, columns)
    block = levels + EXTRA
    edge_shape = jax.ShapeDtypeStruct((W * width + EXTRA, columns), F32)
    pack_shape = jax.ShapeDtypeStruct((block, LANES), F32)
    inputs = (flat, in_scale, storm_mask, balance.T, out_scale, courant, substeps.reshape(1, levels))
    inputs = [pltpu.with_memory_space_constraint(x, pltpu.HBM) for x in inputs]
    features, keep, give, active, small, *edge_rows = call(
        functools.partial(prepare_kernel, tracers, levels, rows, moves),
        [jax.ShapeDtypeStruct((rows, width, columns), BF16), pack_shape, pack_shape,
         jax.ShapeDtypeStruct((rows, columns), F32), jax.ShapeDtypeStruct((8, LANES), F32)] + [edge_shape] * count,
        [pltpu.VMEM(x.shape, x.dtype) for x in inputs]
        + [pltpu.VMEM((8, LANES), F32), pltpu.SemaphoreType.DMA((len(inputs) - 1 + tracers,))],
        10**6, 2 * 10**6, "prepare",
        in_specs=[pl.BlockSpec(memory_space=pltpu.HBM)] * len(inputs),
    )(*inputs)

    given = swap_cores(give)
    features_other = swap_cores(features)
    edge = [send(e, move, False) for e, move in zip(edge_rows, moves)]
    packs = jnp.concatenate([keep, given], axis=0)
    corner = [send(packs, move, True) for move in moves]
    ring = send(packs, None, True)

    tendency, token = call(
        functools.partial(own_network_kernel, tracers, levels, rows),
        [jax.ShapeDtypeStruct((width, rows * columns), BF16), jax.ShapeDtypeStruct((8, LANES), F32)],
        [pltpu.VMEM((2 * width, rows * columns), BF16)],
        2 * 10**9, 8 * 10**6, "own_network",
    )(features, features_other, w_in, w_mid, w_out)
    swept, weights = call(
        functools.partial(own_sweep_kernel, tracers, levels, rows),
        [jax.ShapeDtypeStruct((rows, width, columns), F32), jax.ShapeDtypeStruct((PLANES, levels, LANES), F32)],
        [],
        10**9, 4 * 10**6, "own_sweep",
    )(flat, tendency, small, active)

    forwarded = swap_cores(jnp.concatenate([ring, *corner], axis=0) + token[:1])
    ring_other, *corner_other = jnp.split(forwarded, count + 1, axis=0)
    edge_other = [swap_cores(e) for e in edge]
    total = (1 + W * count) * LANES
    out = call(
        functools.partial(finish_kernel, tracers, levels, rows, moves),
        jax.ShapeDtypeStruct((width * rows, columns), F32),
        [pltpu.VMEM((2 * width, total), BF16), pltpu.VMEM((width, total), BF16),
         pltpu.VMEM((tracers, levels, LANES), F32), pltpu.VMEM((EXTRA, LANES), F32),
         pltpu.VMEM((tracers, levels, LANES), F32), pltpu.VMEM((tracers * W, levels, LANES), F32)],
        10**9, 4 * 10**6, "finish",
    )(swept, weights, w_in, w_mid, w_out, packs, ring, ring_other, *corner, *corner_other, *edge, *edge_other)
    return out.reshape(fields.shape)


def solution(mesh):
    in_specs = (
        P("lev", None, ("group", "lat"), "lon"),
        P("lev", None),
        P("lev", None),
        P(),
        P(),
        P(),
        P(("group", "lat"), "lon"),
        P(("group", "lat"), None),
        P(),
        P(),
    )
    out_specs = P("lev", None, ("group", "lat"), "lon")
    return jax.shard_map(
        on_device, mesh=mesh, in_specs=in_specs, out_specs=out_specs, check_vma=False
    )
```

```python
import functools

import jax
import jax.numpy as jnp
from jax import lax
from jax.experimental import pallas as pl
from jax.experimental.pallas import tpu as pltpu
from jax.sharding import PartitionSpec as P

W = 3
LANES = 128
SCALE_LANE = 96
FIELD_BOUND = 8.0
FIXED_ONE = 32768.0 / FIELD_BOUND
FIXED_MOST = 32767.0
EXTRA = 8
F32 = jnp.float32
BF16 = jnp.bfloat16
GROUP = 32
HALF_GROUP = 16
VMEM_LIMIT = 40 * 1024 * 1024


def lane_ids(rows):
    return lax.broadcasted_iota(jnp.int32, (rows, LANES), 1)


def turned(x, shift):
    if isinstance(shift, int):
        shift %= LANES
        if shift == 0:
            return x
    return pltpu.roll(x, shift, 1)


def silu(v):
    half = 0.5 * v
    return half + half * jnp.tanh(half)


def as_columns(scratch, parts):
    scratch[...] = jnp.zeros_like(scratch)
    at = 0
    for part in parts:
        scratch[at : at + part.shape[0], : part.shape[1]] = part
        at += part.shape[0]
    return scratch[...].T


def column(turned_rows, index, levels):
    return jnp.broadcast_to(turned_rows[:levels, index : index + 1], (levels, LANES))


def side_packs(edges):
    lane = lane_ids(edges[0].shape[0])
    east = lane % 6 < 3
    last = [jnp.where(east, e, 0.0) for e in edges]
    first = [jnp.where(east, 0.0, e) for e in edges]
    east_pack = last[0] + turned(last[1], 3) + turned(last[2], 48)
    west_pack = turned(first[0], -3) + first[1] + turned(first[2], 45)
    return east_pack, west_pack


def edge_kernel(tracers, levels, rows, *refs):
    sources, (keep, give, active, small, features), refs = refs[:7], refs[7:12], refs[12:]
    (fields, in_scale, storm, balance, *loads), scratch, sems = refs[:7], refs[7], refs[8]
    part = levels * rows
    chunks = [
        pltpu.make_async_copy(sources[0].at[pl.ds(t * part, part)], fields.at[pl.ds(t * part, part)], sems.at[t])
        for t in range(tracers)
    ]
    copies = [
        pltpu.make_async_copy(source, into, sems.at[tracers + n])
        for n, (source, into) in enumerate(zip(sources[1:], (in_scale, storm, balance, *loads)))
    ]
    for copy in copies + chunks:
        copy.start()
    for copy in copies:
        copy.wait()
    small[...] = jnp.zeros_like(small)
    at = 0
    for load in loads:
        small[at : at + load.shape[0], : load.shape[1]] = load[...].astype(F32)
        at += load.shape[0]
    lon, lev = lax.axis_index("lon"), lax.axis_index("lev")
    position = lax.broadcasted_iota(jnp.int32, balance.shape, 0)
    target = jnp.max(jnp.where(position == lon, balance[...], -1).astype(F32), axis=0, keepdims=True)
    scales = as_columns(scratch, [in_scale[...], loads[0][...], target])
    mask = jnp.where(column(scales, 2 * tracers, rows) >= 0.0, storm[...].astype(F32), 0.0)
    active[...] = mask
    lane = lane_ids(levels)
    scale_lanes = jnp.zeros((levels, LANES), F32)
    for n in range(2 * tracers):
        scale_lanes = jnp.where(lane == SCALE_LANE + n, column(scales, n, levels), scale_lanes)
    lane = lane_ids(1)
    mask_pack = jnp.zeros((1, LANES), F32)
    for i in range(rows):
        mask_pack = jnp.where((lane >= 6 * i) & (lane < 6 * i + 6), turned(active[i : i + 1, :], 6 * i + W), mask_pack)
    mask_pack = jnp.broadcast_to(mask_pack, (EXTRA, LANES))
    none = jnp.zeros_like(mask_pack)
    last_mask, first_mask = side_packs([mask_pack, none, none])
    lane = lane_ids(levels)
    edges = []
    for t in range(tracers):
        chunks[t].wait()
        scale = column(scales, t, levels)
        pack = jnp.zeros((levels, LANES), F32)
        for i in range(rows):
            x = fields[pl.ds(t * part + i, levels, stride=rows), :]
            features[i, t * levels : (t + 1) * levels, :] = (x * scale).astype(BF16)
            pack = jnp.where((lane >= 6 * i) & (lane < 6 * i + 6), turned(x, 6 * i + W), pack)
        edges.append(pack)
    last_pack, first_pack = side_packs(edges)
    head = lev == 0
    keep[:levels] = jnp.where(head, last_pack, first_pack) + scale_lanes
    give[:levels] = jnp.where(head, first_pack, last_pack) + scale_lanes
    keep[levels:] = jnp.where(head, last_mask, first_mask)
    give[levels:] = jnp.where(head, first_mask, last_mask)


def binary_scale(largest):
    largest = largest * (1.0 / FIELD_BOUND)
    power, scale = jnp.zeros_like(largest), jnp.ones_like(largest)
    for bits in (64, 32, 16, 8, 4, 2, 1):
        small = largest < 2.0**-bits
        largest = jnp.where(small, largest * 2.0**bits, largest)
        scale = jnp.where(small, scale * 2.0**bits, scale)
        power = jnp.where(small, power + float(bits), power)
    return scale, power


def inverse_scale(power):
    scale = jnp.ones_like(power)
    for bits in (64, 32, 16, 8, 4, 2, 1):
        large = power > bits - 0.5
        scale = jnp.where(large, scale * 2.0**-bits, scale)
        power = jnp.where(large, power - float(bits), power)
    return scale


def to_fixed(x):
    return jnp.round(x).astype(jnp.int32).astype(jnp.int16)


def from_fixed(x):
    return x.astype(jnp.int32).astype(F32)


def row_message_kernel(tracers, levels, rows, moves, fields, active, *edge_rows):
    lat = lax.axis_index("lat")
    lane = lane_ids(levels)
    row = lax.broadcasted_iota(jnp.int32, (2 * EXTRA, LANES), 0)
    tail = W * tracers * levels
    for move, out in zip(moves, edge_rows):
        start = first_row_sent(move, lat, rows)
        values = [
            [fields[pl.ds((t * levels) * rows + start + r, levels, stride=rows), :] for r in range(W)]
            for t in range(tracers)
        ]
        largest = [jnp.max(jnp.maximum(jnp.maximum(jnp.abs(a), jnp.abs(b)), jnp.abs(c)), axis=1, keepdims=True) for a, b, c in values]
        bound = jnp.zeros((levels, LANES), F32)
        for t in range(tracers):
            bound = jnp.where(lane == t, largest[t], bound)
        scale, power = binary_scale(bound)
        for t in range(tracers):
            to_one = jnp.broadcast_to(scale[:, t : t + 1], (levels, LANES))
            for r, x in enumerate(values[t]):
                x = jnp.clip(x * to_one * FIXED_ONE, -FIXED_MOST, FIXED_MOST)
                out[(r * tracers + t) * levels : (r * tracers + t + 1) * levels, :] = to_fixed(x)
        out[tail : tail + levels, :] = to_fixed(power)
        mask = jnp.zeros(row.shape, F32)
        for r in range(W):
            mask = jnp.where(row == r, active[pl.ds(start + r, 1), :], mask)
        out[tail + levels :, :] = to_fixed(mask)


def first_row_sent(move, lat, rows):
    if move == 0:
        return jnp.where(lat == 0, rows - W, 0)
    return rows - W if move > 0 else 0


def first_row_received(move, lat, rows):
    if move == 0:
        return jnp.where(lat == 0, 0, rows - W)
    return rows - W if move > 0 else 0


def network(x, w_in, w_mid, w_last):
    hidden = silu(jnp.dot(w_in, x, preferred_element_type=F32)).astype(BF16)
    for layer in range(len(w_mid)):
        hidden = silu(jnp.dot(w_mid[layer], hidden, preferred_element_type=F32)).astype(BF16)
    return jnp.dot(w_last, hidden, preferred_element_type=F32).astype(BF16)


def taps(step, count):
    first = jnp.abs(step)
    second = jnp.where(count > 1.5, first, 0.0)
    third = jnp.where(count > 2.5, first, 0.0)
    rest = [1.0 - a for a in (first, second, third)]
    return (
        rest[0] * rest[1] * rest[2],
        first * rest[1] * rest[2] + rest[0] * second * rest[2] + rest[0] * rest[1] * third,
        first * second * rest[2] + first * rest[1] * third + rest[0] * second * third,
        first * second * third,
    )


def narrow_network(x, w_in, w_mid, w_last):
    def layer(hidden, w):
        return lax.dot_general(hidden, w, (((1,), (1,)), ((), ())), preferred_element_type=F32)

    hidden = silu(lax.dot_general(x, w_in, (((0,), (1,)), ((), ())), preferred_element_type=F32)).astype(BF16)
    for k in range(len(w_mid)):
        hidden = silu(layer(hidden, w_mid[k])).astype(BF16)
    return layer(w_last, hidden).astype(BF16)


OUT_SCALE, LON, LON_SIGN, LAT, LAT_SIGN, EDGE, PLANES = 0, 3, 7, 8, 12, 13, 18


def write_weights(weights, small, tracers, levels):
    columns = small[...].T
    for t in range(tracers):
        weights[OUT_SCALE + t] = column(columns, t, levels)
    count = column(columns, tracers + 2, levels)
    lane = lane_ids(levels)
    place = lane % 6
    step = column(columns, tracers, levels) / count
    up = step > 0.0
    w = taps(step, count)
    weights[LON_SIGN] = jnp.where(up, 1.0, 0.0)
    for k in range(4):
        weights[LON + k] = jnp.where(
            up, jnp.where(lane >= k, w[k], 0.0), jnp.where(lane < LANES - (W - k), w[W - k], 0.0)
        )
    east = [jnp.where(up | (place > 2) | (place < d), 0.0, w[W - d]) for d in range(3)]
    west = [jnp.where(up & (place > 2) & (place + d < 6), w[W - d], 0.0) for d in range(3)]
    weights[EDGE] = east[0] + west[0]
    weights[EDGE + 1] = east[1]
    weights[EDGE + 2] = west[1]
    weights[EDGE + 3] = east[2]
    weights[EDGE + 4] = west[2]
    step = column(columns, tracers + 1, levels) / count
    up = step > 0.0
    w = taps(step, count)
    weights[LAT_SIGN] = jnp.where(up, 1.0, 0.0)
    for k in range(4):
        weights[LAT + k] = jnp.where(up, w[W - k], w[k])


def sweep_lon(values, weights, span):
    up = weights[LON_SIGN, span, :] > 0.5
    values = [jnp.where(up, q, turned(q, -W)) for q in values]
    w = [weights[LON + k, span, :] for k in range(4)]
    return [w[0] * q + w[1] * turned(q, 1) + w[2] * turned(q, 2) + w[3] * turned(q, 3) for q in values]


def own_network_kernel(tracers, levels, rows, mine, other, w_in, w_mid, w_out, tendency, x):
    lev = lax.axis_index("lev")
    width = tracers * levels
    near = pl.ds(pl.multiple_of(lev * width, width), width)
    far = pl.ds(pl.multiple_of((1 - lev) * width, width), width)
    w_last = w_out[near, :]
    for i in range(rows):
        x[near, i * LANES : (i + 1) * LANES] = mine[i]
        x[far, i * LANES : (i + 1) * LANES] = other[i]
    tendency[...] = network(x[...], w_in[...], w_mid, w_last)


def own_sweep_kernel(tracers, levels, rows, fields, tendency, small, active, swept, weights, token):
    token[...] = jnp.zeros_like(token)
    write_weights(weights, small, tracers, levels)
    for g in range(0, levels, GROUP):
        span = slice(g, g + GROUP)
        for t in range(tracers):
            at = t * levels + g
            scale = weights[OUT_SCALE + t, span, :]
            values = []
            for i in range(rows):
                moist = tendency[at : at + GROUP, i * LANES : (i + 1) * LANES].astype(F32)
                q = fields[pl.ds(at * rows + i, GROUP, stride=rows), :]
                values.append(q + scale * moist * active[i : i + 1, :])
            for i, q in enumerate(sweep_lon(values, weights, span)):
                swept[i, at : at + GROUP, :] = q


def edge_network_kernel(tracers, levels, rows, moves, ring, *refs):
    count = len(moves)
    corner, (weights, w_in, w_mid, w_out, mine, other, x) = refs[:count], refs[count:]
    lat, lev = lax.axis_index("lat"), lax.axis_index("lev")
    width = tracers * levels
    block = levels + EXTRA
    head = lev == 0
    lane = lane_ids(levels)
    west = (lane % 6 >= 3) == head
    shifts = [jnp.where(head, a, b) for a, b in ((W, 0), (0, LANES - W), (LANES - 48 + W, LANES - 48))]

    def unpack(t, part):
        value = turned(ring[part, :], shifts[t])
        lane_part = lane[: value.shape[0]]
        used = lane_part < 48
        for n, move in enumerate(moves):
            base = 48 + 18 * n
            shift = shifts[t] + (base - 6 * first_row_received(move, lat, rows))
            shift = jnp.where(shift < 0, shift + LANES, jnp.where(shift >= LANES, shift - LANES, shift))
            here = (lane_part >= base) & (lane_part < base + 18)
            value = jnp.where(here, turned(corner[n][part, :], shift), value)
            used = used | here
        return jnp.where(used & west[: value.shape[0]], value, 0.0)

    mask = unpack(0, slice(levels, block))[:1]
    halos, scales = [], []
    for which in range(2):
        start = lev * width if which == 0 else (1 - lev) * width
        part = slice(which * block, which * block + levels)
        for t in range(tracers):
            in_scale, out_scale = (
                jnp.broadcast_to(ring[part, at : at + 1], (levels, LANES))
                for at in (SCALE_LANE + t, SCALE_LANE + tracers + t)
            )
            value = unpack(t, part)
            halos.append(value)
            scales.append(out_scale)
            x[pl.ds(pl.multiple_of(start + t * levels, levels), levels), :] = (value * in_scale).astype(BF16)
    tendency = narrow_network(x[...], w_in[...], w_mid, w_out[...]).astype(F32)
    x_tendency = [tendency[n * levels : (n + 1) * levels] for n in range(2 * tracers)]
    x_tendency = [
        jnp.where(head, x_tendency[n], x_tendency[(n + tracers) % (2 * tracers)]) for n in range(2 * tracers)
    ]
    values = [halo + scale * moist * mask for halo, scale, moist in zip(halos, scales, x_tendency)]
    if count == 2:
        up = weights[LAT_SIGN] > 0.5
        values = [jnp.where(up | (lane < 48), q, turned(q, -18)) for q in values]
    fix = [weights[EDGE] * q for q in values]
    for k, shift in ((1, 1), (2, -1), (3, 2), (4, -2)):
        fix = [f + weights[EDGE + k] * turned(q, shift) for f, q in zip(fix, values)]
    for t in range(tracers):
        mine[t] = fix[t]
        other[t] = fix[tracers + t]


def row_kernel(tracers, levels, moves, packs, *refs):
    count = len(moves)
    edge, edge_other, (weights, w_in, w_mid, w_out, beyond, x, tendency, fields) = refs[:count], refs[count : 2 * count], refs[2 * count :]
    lev = lax.axis_index("lev")
    width = tracers * levels
    block = levels + EXTRA
    near = pl.ds(pl.multiple_of(lev * width, width), width)
    tail = W * tracers * levels
    for which, source in ((0, edge), (1, edge_other)):
        start = lev * width if which == 0 else (1 - lev) * width
        unscale = [inverse_scale(from_fixed(source[n][tail : tail + levels, :])) * (1.0 / FIXED_ONE) for n in range(count)]
        for t in range(tracers):
            in_scale = jnp.broadcast_to(
                packs[which * block : which * block + levels, SCALE_LANE + t : SCALE_LANE + t + 1], (levels, LANES)
            )
            to = pl.ds(pl.multiple_of(start + t * levels, levels), levels)
            for n in range(count):
                scale = jnp.broadcast_to(unscale[n][:, t : t + 1], (levels, LANES))
                for r in range(W):
                    column_at = (n * W + r) * LANES
                    part = (r * tracers + t) * levels
                    value = from_fixed(source[n][part : part + levels, :]) * scale
                    x[to, column_at : column_at + LANES] = (value * in_scale).astype(BF16)
                    if which == 0:
                        fields[n, part : part + levels, :] = value
    masks = [from_fixed(e[tail + levels :, :]) for e in edge]
    tendency[...] = narrow_network(x[...], w_in[...], w_mid, w_out[near, :])
    up = weights[LAT_SIGN] > 0.5
    values = []
    for t in range(tracers):
        for r in range(W):
            rows_q = []
            for n in range(count):
                column_at = (n * W + r) * LANES
                moist = tendency[t * levels : (t + 1) * levels, column_at : column_at + LANES].astype(F32)
                value = fields[n, (r * tracers + t) * levels : (r * tracers + t + 1) * levels, :]
                rows_q.append(value + weights[OUT_SCALE + t] * moist * masks[n][r : r + 1, :])
            values.append(jnp.where(up, rows_q[0], rows_q[1]) if count > 1 else rows_q[0])
    for n, q in enumerate(sweep_lon(values, weights, slice(0, levels))):
        beyond[n] = q


def finish_kernel(tracers, levels, rows, moves, swept, weights, fix_mine, fix_other, beyond, out, result, sems):
    lat = lax.axis_index("lat")
    southward = jnp.where(lat == 0, 0.0, 1.0)
    copies = []
    lane = lane_ids(HALF_GROUP)
    at_edge = (lane < W) | (lane >= LANES - W)
    for g in range(0, levels, HALF_GROUP):
        span = slice(g, g + HALF_GROUP)
        sign = weights[LAT_SIGN, span, :]
        up = sign > 0.5
        w = [weights[LAT + k, span, :] for k in range(4)]
        for t in range(tracers):
            at = t * levels + g
            fix = fix_mine[t, span, :] + fix_other[t, span, :]

            def fixed(value, first):
                return value + jnp.where(at_edge, turned(fix, LANES - W - first), 0.0)

            inner = [fixed(swept[i, at : at + HALF_GROUP, :], 6 * i) for i in range(rows)]
            outer = [fixed(beyond[t * W + r, span, :], 48 + 6 * r) for r in range(W)]
            if len(moves) == 1:
                outer = [jnp.where(sign == southward, q, 0.0) for q in outer]
            line = []
            for i in range(rows + W):
                above = outer[i] if i < W else inner[i - W]
                below = inner[i] if i < rows else outer[i - rows]
                line.append(jnp.where(up, above, below))
            results = [w[0] * line[i] + w[1] * line[i + 1] + w[2] * line[i + 2] + w[3] * line[i + 3] for i in range(rows)]
            for i, value in enumerate(results):
                result[pl.ds(at * rows + i, HALF_GROUP, stride=rows), :] = value
            part = pl.ds(at * rows, HALF_GROUP * rows)
            copies.append(pltpu.make_async_copy(result.at[part], out.at[part], sems.at[len(copies)]))
            copies[-1].start()
    for copy in copies:
        copy.wait()


def call(kernel, out_shape, scratch, flops, moved, name, **specs):
    return pl.pallas_call(
        kernel,
        out_shape=out_shape,
        **specs,
        scratch_shapes=scratch,
        compiler_params=pltpu.CompilerParams(vmem_limit_bytes=VMEM_LIMIT),
        cost_estimate=pl.CostEstimate(flops=flops, bytes_accessed=moved, transcendentals=0),
        name=name,
    )


def swap_cores(x):
    return lax.ppermute(x, "lev", [(0, 1), (1, 0)])


def routes(lon_count, lat_count, move, along_lon):
    pairs = []
    for i in range(lon_count):
        for j in range(lat_count):
            to_lat = 1 - j if move == 0 else j + (move or 0)
            if not 0 <= to_lat < lat_count:
                continue
            for k in range(2):
                to_lon = (i + (1 - 2 * k)) % lon_count if along_lon else i
                pairs.append((((i * lat_count) + j) * 2 + k, ((to_lon * lat_count) + to_lat) * 2 + k))
    return pairs


def send(x, move, along_lon):
    axes = ("lon", "lat", "lev")
    lon_count, lat_count = lax.axis_size("lon"), lax.axis_size("lat")
    if move is None:
        pairs = []
        for i in range(lon_count):
            for j in range(lat_count):
                for k in range(2):
                    to_lon = (i + (1 - 2 * k)) % lon_count
                    pairs.append(((i * lat_count + j) * 2 + k, (to_lon * lat_count + j) * 2 + k))
    else:
        pairs = routes(lon_count, lat_count, move, along_lon)
    return lax.ppermute(x, axes, pairs)


def on_device(fields, in_scale, out_scale, w_in, w_mid, w_out, storm_mask, balance, substeps, courant):
    tracers, levels, rows, columns = fields.shape
    width = tracers * levels
    moves = (0,) if lax.axis_size("lat") == 2 else (1, -1)
    count = len(moves)
    flat = fields.reshape(width * rows, columns)
    block = levels + EXTRA
    edge_shape = jax.ShapeDtypeStruct((W * width + levels + 2 * EXTRA, columns), jnp.int16)
    pack_shape = jax.ShapeDtypeStruct((block, LANES), F32)
    inputs = (flat, in_scale, storm_mask, balance.T, out_scale, courant, substeps.reshape(1, levels))
    inputs = [pltpu.with_memory_space_constraint(x, pltpu.HBM) for x in inputs]
    small_shape = jax.ShapeDtypeStruct((EXTRA, LANES), F32)
    keep, give, active, small, features = call(
        functools.partial(edge_kernel, tracers, levels, rows),
        [pack_shape, pack_shape, jax.ShapeDtypeStruct((rows, columns), F32), small_shape,
         jax.ShapeDtypeStruct((rows, width, columns), BF16)],
        [pltpu.VMEM(x.shape, x.dtype) for x in inputs]
        + [pltpu.VMEM((EXTRA, LANES), F32), pltpu.SemaphoreType.DMA((len(inputs) - 1 + tracers,))],
        10**6, 2 * 10**6, "edges",
        in_specs=[pl.BlockSpec(memory_space=pltpu.HBM)] * len(inputs),
    )(*inputs)
    given = swap_cores(give)
    features_other = swap_cores(features)
    edge_rows = call(
        functools.partial(row_message_kernel, tracers, levels, rows, moves),
        [edge_shape] * count,
        [],
        10**6, 2 * 10**6, "row_messages",
    )(flat, active)
    packs = jnp.concatenate([keep, given], axis=0)
    corner = [send(packs, move, True) for move in moves]
    ring = send(packs, None, True)
    edge = [send(e, move, False) for e, move in zip(edge_rows, moves)]

    tendency = call(
        functools.partial(own_network_kernel, tracers, levels, rows),
        jax.ShapeDtypeStruct((width, rows * columns), BF16),
        [pltpu.VMEM((2 * width, rows * columns), BF16)],
        10**6, 10**6, "own_network",
    )(features, features_other, w_in, w_mid, w_out)
    swept, weights, token = call(
        functools.partial(own_sweep_kernel, tracers, levels, rows),
        [jax.ShapeDtypeStruct((rows, width, columns), F32), jax.ShapeDtypeStruct((PLANES, levels, LANES), F32),
         jax.ShapeDtypeStruct((2 * EXTRA, LANES), jnp.int16)],
        [],
        10**6, 10**6, "own_sweep",
    )(flat, tendency, small, active)

    fix_shape = jax.ShapeDtypeStruct((tracers, levels, LANES), F32)
    fix_mine, fix_given = call(
        functools.partial(edge_network_kernel, tracers, levels, rows, moves),
        [fix_shape, fix_shape],
        [pltpu.VMEM((2 * width, LANES), BF16)],
        10**9, 4 * 10**6, "edge_network",
    )(ring, *corner, weights, w_in, w_mid, w_out)
    fix_other = swap_cores(fix_given)
    edge_other = [swap_cores(e + token[:1]) for e in edge]
    total = W * count * LANES
    beyond = call(
        functools.partial(row_kernel, tracers, levels, moves),
        jax.ShapeDtypeStruct((tracers * W, levels, LANES), F32),
        [pltpu.VMEM((2 * width, total), BF16), pltpu.VMEM((width, total), BF16),
         pltpu.VMEM((count, W * width, LANES), F32)],
        10**9, 4 * 10**6, "row_network",
    )(packs, *edge, *edge_other, weights, w_in, w_mid, w_out)
    out = call(
        functools.partial(finish_kernel, tracers, levels, rows, moves),
        jax.ShapeDtypeStruct((width * rows, columns), F32),
        [pltpu.VMEM((width * rows, columns), F32), pltpu.SemaphoreType.DMA((width // HALF_GROUP,))],
        10**9, 4 * 10**6, "finish",
        out_specs=pl.BlockSpec(memory_space=pltpu.HBM),
    )(swept, weights, fix_mine, fix_other, beyond)
    return out.reshape(fields.shape)


def solution(mesh):
    in_specs = (
        P("lev", None, ("group", "lat"), "lon"),
        P("lev", None),
        P("lev", None),
        P(),
        P(),
        P(),
        P(("group", "lat"), "lon"),
        P(("group", "lat"), None),
        P(),
        P(),
    )
    out_specs = P("lev", None, ("group", "lat"), "lon")
    return jax.shard_map(
        on_device, mesh=mesh, in_specs=in_specs, out_specs=out_specs, check_vma=False
    )
```

```python
import functools

import jax
import jax.numpy as jnp
from jax import lax
from jax.experimental import pallas as pl
from jax.experimental.pallas import tpu as pltpu
from jax.sharding import PartitionSpec as P

W = 3
LANES = 128
HALF_LANES = 48
SCALE_LANE = 96
FIELD_BOUND = 8.0
FIXED_ONE = 32768.0 / FIELD_BOUND
FIXED_MOST = 32767.0
EXTRA = 8
F32 = jnp.float32
BF16 = jnp.bfloat16
GROUP = 32
HALF_GROUP = 16
VMEM_LIMIT = 40 * 1024 * 1024


def lane_ids(rows):
    return lax.broadcasted_iota(jnp.int32, (rows, LANES), 1)


def turned(x, shift):
    if isinstance(shift, int):
        shift %= LANES
        if shift == 0:
            return x
    return pltpu.roll(x, shift, 1)


def silu(v):
    half = 0.5 * v
    return half + half * jnp.tanh(half)


def as_columns(scratch, parts):
    scratch[...] = jnp.zeros_like(scratch)
    at = 0
    for part in parts:
        scratch[at : at + part.shape[0], : part.shape[1]] = part
        at += part.shape[0]
    return scratch[...].T


def column(turned_rows, index, levels):
    return jnp.broadcast_to(turned_rows[:levels, index : index + 1], (levels, LANES))


def side_messages(edges):
    lane = lane_ids(1)
    east = lane % 6 < 3
    used = lane < HALF_LANES
    half = edges[2].shape[0] // 2
    pairs = ((edges[0], edges[1]), (edges[2][:half], edges[2][half:]))
    last = [jnp.where(east, p, turned(q, W)) for p, q in pairs]
    first = [jnp.where(used, jnp.where(east, turned(p, -W), q), 0.0) for p, q in pairs]
    return last, first


def edge_kernel(tracers, levels, rows, *refs):
    sources, (keep, give, active, small, features), refs = refs[:7], refs[7:12], refs[12:]
    (fields, in_scale, storm, balance, *loads), scratch, sems = refs[:7], refs[7], refs[8]
    part = levels * rows
    chunks = [
        pltpu.make_async_copy(sources[0].at[pl.ds(t * part, part)], fields.at[pl.ds(t * part, part)], sems.at[t])
        for t in range(tracers)
    ]
    copies = [
        pltpu.make_async_copy(source, into, sems.at[tracers + n])
        for n, (source, into) in enumerate(zip(sources[1:], (in_scale, storm, balance, *loads)))
    ]
    for copy in copies + chunks:
        copy.start()
    for copy in copies:
        copy.wait()
    small[...] = jnp.zeros_like(small)
    at = 0
    for load in loads:
        small[at : at + load.shape[0], : load.shape[1]] = load[...].astype(F32)
        at += load.shape[0]
    lon, lev = lax.axis_index("lon"), lax.axis_index("lev")
    position = lax.broadcasted_iota(jnp.int32, balance.shape, 0)
    target = jnp.max(jnp.where(position == lon, balance[...], -1).astype(F32), axis=0, keepdims=True)
    scales = as_columns(scratch, [in_scale[...], loads[0][...], target])
    mask = jnp.where(column(scales, 2 * tracers, rows) >= 0.0, storm[...].astype(F32), 0.0)
    active[...] = mask
    lane = lane_ids(levels)
    own_scales, given_scales = jnp.zeros((levels, LANES), F32), jnp.zeros((levels, LANES), F32)
    for n in range(2 * tracers):
        scale = column(scales, n, levels)
        own_scales = jnp.where(lane == SCALE_LANE + n, scale, own_scales)
        given_scales = jnp.where(lane == SCALE_LANE + 2 * tracers + n, scale, given_scales)
    lane = lane_ids(1)
    mask_pack = jnp.zeros((1, LANES), F32)
    for i in range(rows):
        mask_pack = jnp.where((lane >= 6 * i) & (lane < 6 * i + 6), turned(mask[i : i + 1, :], 6 * i + W), mask_pack)
    mask_pack = jnp.broadcast_to(mask_pack, (EXTRA, LANES))
    east = lane % 6 < 3
    last_mask = jnp.where(east, mask_pack, 0.0)
    first_mask = turned(jnp.where(east, 0.0, mask_pack), -W)
    half = levels // 2
    head = lev == 0
    keep[levels + half :] = jnp.where(head, last_mask, first_mask)
    give[levels + half :] = turned(jnp.where(head, first_mask, last_mask), HALF_LANES)
    lane = lane_ids(levels)
    edges = []
    for t in range(tracers):
        chunks[t].wait()
        scale = column(scales, t, levels)
        pack = jnp.zeros((levels, LANES), F32)
        for i in range(rows):
            x = fields[pl.ds(t * part + i, levels, stride=rows), :]
            features[i, t * levels : (t + 1) * levels, :] = (x * scale).astype(BF16)
            pack = jnp.where((lane >= 6 * i) & (lane < 6 * i + 6), turned(x, 6 * i + W), pack)
        edges.append(pack)
    last, first = side_messages(edges)
    keep[:levels] = jnp.where(head, last[0], first[0]) + own_scales
    give[:levels] = turned(jnp.where(head, first[0], last[0]), HALF_LANES) + given_scales
    keep[levels : levels + half] = jnp.where(head, last[1], first[1])
    give[levels : levels + half] = turned(jnp.where(head, first[1], last[1]), HALF_LANES)


def binary_scale(largest):
    largest = largest * (1.0 / FIELD_BOUND)
    power, scale = jnp.zeros_like(largest), jnp.ones_like(largest)
    for bits in (64, 32, 16, 8, 4, 2, 1):
        small = largest < 2.0**-bits
        largest = jnp.where(small, largest * 2.0**bits, largest)
        scale = jnp.where(small, scale * 2.0**bits, scale)
        power = jnp.where(small, power + float(bits), power)
    return scale, power


def inverse_scale(power):
    scale = jnp.ones_like(power)
    for bits in (64, 32, 16, 8, 4, 2, 1):
        large = power > bits - 0.5
        scale = jnp.where(large, scale * 2.0**-bits, scale)
        power = jnp.where(large, power - float(bits), power)
    return scale


def to_fixed(x):
    return jnp.round(x).astype(jnp.int32).astype(jnp.int16)


def from_fixed(x):
    return x.astype(jnp.int32).astype(F32)


def row_message_kernel(tracers, levels, rows, moves, fields, active, *edge_rows):
    lat = lax.axis_index("lat")
    lane = lane_ids(levels)
    row = lax.broadcasted_iota(jnp.int32, (2 * EXTRA, LANES), 0)
    tail = W * tracers * levels
    for move, out in zip(moves, edge_rows):
        start = first_row_sent(move, lat, rows)
        values = [
            [fields[pl.ds((t * levels) * rows + start + r, levels, stride=rows), :] for r in range(W)]
            for t in range(tracers)
        ]
        largest = [jnp.max(jnp.maximum(jnp.maximum(jnp.abs(a), jnp.abs(b)), jnp.abs(c)), axis=1, keepdims=True) for a, b, c in values]
        bound = jnp.zeros((levels, LANES), F32)
        for t in range(tracers):
            bound = jnp.where(lane == t, largest[t], bound)
        scale, power = binary_scale(bound)
        for t in range(tracers):
            to_one = jnp.broadcast_to(scale[:, t : t + 1], (levels, LANES))
            for r, x in enumerate(values[t]):
                x = jnp.clip(x * to_one * FIXED_ONE, -FIXED_MOST, FIXED_MOST)
                out[(r * tracers + t) * levels : (r * tracers + t + 1) * levels, :] = to_fixed(x)
        out[tail : tail + levels, :] = to_fixed(power)
        mask = jnp.zeros(row.shape, F32)
        for r in range(W):
            mask = jnp.where(row == r, active[pl.ds(start + r, 1), :], mask)
        out[tail + levels :, :] = to_fixed(mask)


def first_row_sent(move, lat, rows):
    if move == 0:
        return jnp.where(lat == 0, rows - W, 0)
    return rows - W if move > 0 else 0


def first_row_received(move, lat, rows):
    if move == 0:
        return jnp.where(lat == 0, 0, rows - W)
    return rows - W if move > 0 else 0


def network(x, w_in, w_mid, w_last):
    hidden = silu(jnp.dot(w_in, x, preferred_element_type=F32)).astype(BF16)
    for layer in range(len(w_mid)):
        hidden = silu(jnp.dot(w_mid[layer], hidden, preferred_element_type=F32)).astype(BF16)
    return jnp.dot(w_last, hidden, preferred_element_type=F32).astype(BF16)


def taps(step, count):
    first = jnp.abs(step)
    second = jnp.where(count > 1.5, first, 0.0)
    third = jnp.where(count > 2.5, first, 0.0)
    rest = [1.0 - a for a in (first, second, third)]
    return (
        rest[0] * rest[1] * rest[2],
        first * rest[1] * rest[2] + rest[0] * second * rest[2] + rest[0] * rest[1] * third,
        first * second * rest[2] + first * rest[1] * third + rest[0] * second * third,
        first * second * third,
    )


def narrow_network(x, w_in, w_mid, w_last):
    def layer(hidden, w):
        return lax.dot_general(hidden, w, (((1,), (1,)), ((), ())), preferred_element_type=F32)

    hidden = silu(lax.dot_general(x, w_in, (((0,), (1,)), ((), ())), preferred_element_type=F32)).astype(BF16)
    for k in range(len(w_mid)):
        hidden = silu(layer(hidden, w_mid[k])).astype(BF16)
    return layer(w_last, hidden).astype(BF16)


OUT_SCALE, LON, LON_SIGN, LAT, LAT_SIGN, EDGE, PLANES = 0, 3, 7, 8, 12, 13, 18


def write_weights(weights, small, tracers, levels):
    columns = small[...].T
    for t in range(tracers):
        weights[OUT_SCALE + t] = column(columns, t, levels)
    count = column(columns, tracers + 2, levels)
    lane = lane_ids(levels)
    place = lane % 6
    step = column(columns, tracers, levels) / count
    up = step > 0.0
    w = taps(step, count)
    weights[LON_SIGN] = jnp.where(up, 1.0, 0.0)
    for k in range(4):
        weights[LON + k] = jnp.where(
            up, jnp.where(lane >= k, w[k], 0.0), jnp.where(lane < LANES - (W - k), w[W - k], 0.0)
        )
    east = [jnp.where(up | (place > 2) | (place < d), 0.0, w[W - d]) for d in range(3)]
    west = [jnp.where(up & (place > 2) & (place + d < 6), w[W - d], 0.0) for d in range(3)]
    weights[EDGE] = east[0] + west[0]
    weights[EDGE + 1] = east[1]
    weights[EDGE + 2] = west[1]
    weights[EDGE + 3] = east[2]
    weights[EDGE + 4] = west[2]
    step = column(columns, tracers + 1, levels) / count
    up = step > 0.0
    w = taps(step, count)
    weights[LAT_SIGN] = jnp.where(up, 1.0, 0.0)
    for k in range(4):
        weights[LAT + k] = jnp.where(up, w[W - k], w[k])


def sweep_lon(values, weights, span):
    up = weights[LON_SIGN, span, :] > 0.5
    values = [jnp.where(up, q, turned(q, -W)) for q in values]
    w = [weights[LON + k, span, :] for k in range(4)]
    return [w[0] * q + w[1] * turned(q, 1) + w[2] * turned(q, 2) + w[3] * turned(q, 3) for q in values]


def own_network_kernel(tracers, levels, rows, mine, other, w_in, w_mid, w_out, tendency, x):
    lev = lax.axis_index("lev")
    width = tracers * levels
    near = pl.ds(pl.multiple_of(lev * width, width), width)
    far = pl.ds(pl.multiple_of((1 - lev) * width, width), width)
    w_last = w_out[near, :]
    for i in range(rows):
        x[near, i * LANES : (i + 1) * LANES] = mine[i]
        x[far, i * LANES : (i + 1) * LANES] = other[i]
    tendency[...] = network(x[...], w_in[...], w_mid, w_last)


def own_sweep_kernel(tracers, levels, rows, fields, tendency, small, active, swept, weights, token):
    token[...] = jnp.zeros_like(token)
    write_weights(weights, small, tracers, levels)
    for g in range(0, levels, GROUP):
        span = slice(g, g + GROUP)
        for t in range(tracers):
            at = t * levels + g
            scale = weights[OUT_SCALE + t, span, :]
            values = []
            for i in range(rows):
                moist = tendency[at : at + GROUP, i * LANES : (i + 1) * LANES].astype(F32)
                q = fields[pl.ds(at * rows + i, GROUP, stride=rows), :]
                values.append(q + scale * moist * active[i : i + 1, :])
            for i, q in enumerate(sweep_lon(values, weights, span)):
                swept[i, at : at + GROUP, :] = q


def read_scale(message, which, n, tracers, levels):
    at = SCALE_LANE + 2 * tracers * which + n
    return jnp.broadcast_to(message[:levels, at : at + 1], (levels, LANES))


def edge_network_kernel(tracers, levels, rows, moves, ring, *refs):
    count = len(moves)
    corner, (weights, w_in, w_mid, w_out, mine, other, x) = refs[:count], refs[count:]
    lat, lev = lax.axis_index("lat"), lax.axis_index("lev")
    width = tracers * levels
    head = lev == 0
    lane = lane_ids(levels)
    west = (lane % 6 >= 3) == head
    shifts = [jnp.where(head, a, b) for a, b in ((W, 0), (0, LANES - W))]
    half = levels // 2

    def place(message, part, which, extra):
        moved = []
        for shift in shifts:
            shift = shift + (extra + LANES - HALF_LANES * which)
            shift = jnp.where(shift >= 2 * LANES, shift - 2 * LANES, jnp.where(shift >= LANES, shift - LANES, shift))
            moved.append(turned(message[part, :], shift))
        return moved

    def unpack(part, which):
        lane_part = lane[: part.stop - part.start]
        values = place(ring, part, which, 0)
        used = lane_part < 48
        for n, move in enumerate(moves):
            base = 48 + 18 * n
            here = (lane_part >= base) & (lane_part < base + 18)
            far = place(corner[n], part, which, base - 6 * first_row_received(move, lat, rows))
            values = [jnp.where(here, q, value) for q, value in zip(far, values)]
            used = used | here
        used = used & west[: lane_part.shape[0]]
        return [jnp.where(used, value, 0.0) for value in values]

    mask = unpack(slice(levels + half, levels + half + EXTRA), 0)[0][:1]
    halos, scales = [], []
    for which in range(2):
        start = lev * width if which == 0 else (1 - lev) * width
        values = unpack(slice(0, levels), which)
        values.append(jnp.concatenate(unpack(slice(levels, levels + half), which), axis=0))
        for t, value in enumerate(values):
            in_scale, out_scale = (read_scale(ring, which, n, tracers, levels) for n in (t, tracers + t))
            halos.append(value)
            scales.append(out_scale)
            x[pl.ds(pl.multiple_of(start + t * levels, levels), levels), :] = (value * in_scale).astype(BF16)
    tendency = narrow_network(x[...], w_in[...], w_mid, w_out[...]).astype(F32)
    x_tendency = [tendency[n * levels : (n + 1) * levels] for n in range(2 * tracers)]
    x_tendency = [
        jnp.where(head, x_tendency[n], x_tendency[(n + tracers) % (2 * tracers)]) for n in range(2 * tracers)
    ]
    values = [halo + scale * moist * mask for halo, scale, moist in zip(halos, scales, x_tendency)]
    if count == 2:
        up = weights[LAT_SIGN] > 0.5
        values = [jnp.where(up | (lane < 48), q, turned(q, -18)) for q in values]
    fix = [weights[EDGE] * q for q in values]
    for k, shift in ((1, 1), (2, -1), (3, 2), (4, -2)):
        fix = [f + weights[EDGE + k] * turned(q, shift) for f, q in zip(fix, values)]
    for t in range(tracers):
        mine[t] = fix[t]
        other[t] = fix[tracers + t]


def row_kernel(tracers, levels, moves, packs, *refs):
    count = len(moves)
    edge, edge_other, (weights, w_in, w_mid, w_out, beyond, x, tendency, fields) = refs[:count], refs[count : 2 * count], refs[2 * count :]
    lev = lax.axis_index("lev")
    width = tracers * levels
    near = pl.ds(pl.multiple_of(lev * width, width), width)
    tail = W * tracers * levels
    for which, source in ((0, edge), (1, edge_other)):
        start = lev * width if which == 0 else (1 - lev) * width
        unscale = [inverse_scale(from_fixed(source[n][tail : tail + levels, :])) * (1.0 / FIXED_ONE) for n in range(count)]
        for t in range(tracers):
            in_scale = read_scale(packs, which, t, tracers, levels)
            to = pl.ds(pl.multiple_of(start + t * levels, levels), levels)
            for n in range(count):
                scale = jnp.broadcast_to(unscale[n][:, t : t + 1], (levels, LANES))
                for r in range(W):
                    column_at = (n * W + r) * LANES
                    part = (r * tracers + t) * levels
                    value = from_fixed(source[n][part : part + levels, :]) * scale
                    x[to, column_at : column_at + LANES] = (value * in_scale).astype(BF16)
                    if which == 0:
                        fields[n, part : part + levels, :] = value
    masks = [from_fixed(e[tail + levels :, :]) for e in edge]
    tendency[...] = narrow_network(x[...], w_in[...], w_mid, w_out[near, :])
    up = weights[LAT_SIGN] > 0.5
    values = []
    for t in range(tracers):
        for r in range(W):
            rows_q = []
            for n in range(count):
                column_at = (n * W + r) * LANES
                moist = tendency[t * levels : (t + 1) * levels, column_at : column_at + LANES].astype(F32)
                value = fields[n, (r * tracers + t) * levels : (r * tracers + t + 1) * levels, :]
                rows_q.append(value + weights[OUT_SCALE + t] * moist * masks[n][r : r + 1, :])
            values.append(jnp.where(up, rows_q[0], rows_q[1]) if count > 1 else rows_q[0])
    for n, q in enumerate(sweep_lon(values, weights, slice(0, levels))):
        beyond[n] = q


def finish_kernel(tracers, levels, rows, moves, swept, weights, fix_mine, fix_other, beyond, out, result, sems):
    lat = lax.axis_index("lat")
    southward = jnp.where(lat == 0, 0.0, 1.0)
    copies = []
    lane = lane_ids(HALF_GROUP)
    at_edge = (lane < W) | (lane >= LANES - W)
    for g in range(0, levels, HALF_GROUP):
        span = slice(g, g + HALF_GROUP)
        sign = weights[LAT_SIGN, span, :]
        up = sign > 0.5
        w = [weights[LAT + k, span, :] for k in range(4)]
        for t in range(tracers):
            at = t * levels + g
            fix = fix_mine[t, span, :] + fix_other[t, span, :]

            def fixed(value, first):
                return value + jnp.where(at_edge, turned(fix, LANES - W - first), 0.0)

            inner = [fixed(swept[i, at : at + HALF_GROUP, :], 6 * i) for i in range(rows)]
            outer = [fixed(beyond[t * W + r, span, :], 48 + 6 * r) for r in range(W)]
            if len(moves) == 1:
                outer = [jnp.where(sign == southward, q, 0.0) for q in outer]
            line = []
            for i in range(rows + W):
                above = outer[i] if i < W else inner[i - W]
                below = inner[i] if i < rows else outer[i - rows]
                line.append(jnp.where(up, above, below))
            results = [w[0] * line[i] + w[1] * line[i + 1] + w[2] * line[i + 2] + w[3] * line[i + 3] for i in range(rows)]
            for i, value in enumerate(results):
                result[pl.ds(at * rows + i, HALF_GROUP, stride=rows), :] = value
            part = pl.ds(at * rows, HALF_GROUP * rows)
            copies.append(pltpu.make_async_copy(result.at[part], out.at[part], sems.at[len(copies)]))
            copies[-1].start()
    for copy in copies:
        copy.wait()


def call(kernel, out_shape, scratch, flops, moved, name, **specs):
    return pl.pallas_call(
        kernel,
        out_shape=out_shape,
        **specs,
        scratch_shapes=scratch,
        compiler_params=pltpu.CompilerParams(vmem_limit_bytes=VMEM_LIMIT),
        cost_estimate=pl.CostEstimate(flops=flops, bytes_accessed=moved, transcendentals=0),
        name=name,
    )


def swap_cores(x):
    return lax.ppermute(x, "lev", [(0, 1), (1, 0)])


def routes(lon_count, lat_count, move, along_lon):
    pairs = []
    for i in range(lon_count):
        for j in range(lat_count):
            to_lat = 1 - j if move == 0 else j + (move or 0)
            if not 0 <= to_lat < lat_count:
                continue
            for k in range(2):
                to_lon = (i + (1 - 2 * k)) % lon_count if along_lon else i
                pairs.append((((i * lat_count) + j) * 2 + k, ((to_lon * lat_count) + to_lat) * 2 + k))
    return pairs


def send(x, move, along_lon):
    axes = ("lon", "lat", "lev")
    lon_count, lat_count = lax.axis_size("lon"), lax.axis_size("lat")
    if move is None:
        pairs = []
        for i in range(lon_count):
            for j in range(lat_count):
                for k in range(2):
                    to_lon = (i + (1 - 2 * k)) % lon_count
                    pairs.append(((i * lat_count + j) * 2 + k, (to_lon * lat_count + j) * 2 + k))
    else:
        pairs = routes(lon_count, lat_count, move, along_lon)
    return lax.ppermute(x, axes, pairs)


def on_device(fields, in_scale, out_scale, w_in, w_mid, w_out, storm_mask, balance, substeps, courant):
    tracers, levels, rows, columns = fields.shape
    width = tracers * levels
    moves = (0,) if lax.axis_size("lat") == 2 else (1, -1)
    count = len(moves)
    flat = fields.reshape(width * rows, columns)
    edge_shape = jax.ShapeDtypeStruct((W * width + levels + 2 * EXTRA, columns), jnp.int16)
    pack_shape = jax.ShapeDtypeStruct((levels + levels // 2 + EXTRA, LANES), F32)
    inputs = (flat, in_scale, storm_mask, balance.T, out_scale, courant, substeps.reshape(1, levels))
    inputs = [pltpu.with_memory_space_constraint(x, pltpu.HBM) for x in inputs]
    small_shape = jax.ShapeDtypeStruct((EXTRA, LANES), F32)
    keep, give, active, small, features = call(
        functools.partial(edge_kernel, tracers, levels, rows),
        [pack_shape, pack_shape, jax.ShapeDtypeStruct((rows, columns), F32), small_shape,
         jax.ShapeDtypeStruct((rows, width, columns), BF16)],
        [pltpu.VMEM(x.shape, x.dtype) for x in inputs]
        + [pltpu.VMEM((EXTRA, LANES), F32), pltpu.SemaphoreType.DMA((len(inputs) - 1 + tracers,))],
        10000000000, 0, "edges",
        in_specs=[pl.BlockSpec(memory_space=pltpu.HBM)] * len(inputs),
    )(*inputs)
    given = swap_cores(give)
    features_other = swap_cores(features)
    edge_rows = call(
        functools.partial(row_message_kernel, tracers, levels, rows, moves),
        [edge_shape] * count,
        [],
        10000000000, 0, "row_messages",
    )(flat, active)
    packs = keep + given
    corner = [send(packs, move, True) for move in moves]
    ring = send(packs, None, True)
    edge = [send(e, move, False) for e, move in zip(edge_rows, moves)]

    tendency = call(
        functools.partial(own_network_kernel, tracers, levels, rows),
        jax.ShapeDtypeStruct((width, rows * columns), BF16),
        [pltpu.VMEM((2 * width, rows * columns), BF16)],
        10000000000, 0, "own_network",
    )(features, features_other, w_in, w_mid, w_out)
    swept, weights, token = call(
        functools.partial(own_sweep_kernel, tracers, levels, rows),
        [jax.ShapeDtypeStruct((rows, width, columns), F32), jax.ShapeDtypeStruct((PLANES, levels, LANES), F32),
         jax.ShapeDtypeStruct((2 * EXTRA, LANES), jnp.int16)],
        [],
        10000000000, 0, "own_sweep",
    )(flat, tendency, small, active)

    fix_shape = jax.ShapeDtypeStruct((tracers, levels, LANES), F32)
    fix_mine, fix_given = call(
        functools.partial(edge_network_kernel, tracers, levels, rows, moves),
        [fix_shape, fix_shape],
        [pltpu.VMEM((2 * width, LANES), BF16)],
        10000000000, 0, "edge_network",
    )(ring, *corner, weights, w_in, w_mid, w_out)
    fix_other = swap_cores(fix_given)
    edge_other = [swap_cores(e + token[:1]) for e in edge]
    total = W * count * LANES
    beyond = call(
        functools.partial(row_kernel, tracers, levels, moves),
        jax.ShapeDtypeStruct((tracers * W, levels, LANES), F32),
        [pltpu.VMEM((2 * width, total), BF16), pltpu.VMEM((width, total), BF16),
         pltpu.VMEM((count, W * width, LANES), F32)],
        10000000000, 0, "row_network",
    )(packs, *edge, *edge_other, weights, w_in, w_mid, w_out)
    out = call(
        functools.partial(finish_kernel, tracers, levels, rows, moves),
        jax.ShapeDtypeStruct((width * rows, columns), F32),
        [pltpu.VMEM((width * rows, columns), F32), pltpu.SemaphoreType.DMA((width // HALF_GROUP,))],
        10000000000, 0, "finish",
        out_specs=pl.BlockSpec(memory_space=pltpu.HBM),
    )(swept, weights, fix_mine, fix_other, beyond)
    return out.reshape(fields.shape)


def solution(mesh):
    in_specs = (
        P("lev", None, ("group", "lat"), "lon"),
        P("lev", None),
        P("lev", None),
        P(),
        P(),
        P(),
        P(("group", "lat"), "lon"),
        P(("group", "lat"), None),
        P(),
        P(),
    )
    out_specs = P("lev", None, ("group", "lat"), "lon")
    return jax.shard_map(
        on_device, mesh=mesh, in_specs=in_specs, out_specs=out_specs, check_vma=False
    )
```

```python
import functools

import jax
import jax.numpy as jnp
from jax import lax
from jax.experimental import pallas as pl
from jax.experimental.pallas import tpu as pltpu
from jax.sharding import PartitionSpec as P

W = 3
LANES = 128
HALF_LANES = 48
SCALE_LANE = 96
FIELD_BOUND = 8.0
FIXED_ONE = 32768.0 / FIELD_BOUND
FIXED_MOST = 32767.0
EXTRA = 8
F32 = jnp.float32
BF16 = jnp.bfloat16
GROUP = 32
HALF_GROUP = 16
VMEM_LIMIT = 40 * 1024 * 1024


def lane_ids(rows):
    return lax.broadcasted_iota(jnp.int32, (rows, LANES), 1)


def turned(x, shift):
    if isinstance(shift, int):
        shift %= LANES
        if shift == 0:
            return x
    return pltpu.roll(x, shift, 1)


def silu(v):
    half = 0.5 * v
    return half + half * jnp.tanh(half)


def as_columns(scratch, parts):
    scratch[...] = jnp.zeros_like(scratch)
    at = 0
    for part in parts:
        scratch[at : at + part.shape[0], : part.shape[1]] = part
        at += part.shape[0]
    return scratch[...].T


def column(turned_rows, index, levels):
    return jnp.broadcast_to(turned_rows[:levels, index : index + 1], (levels, LANES))


def side_messages(edges):
    lane = lane_ids(1)
    east = lane % 6 < 3
    used = lane < HALF_LANES
    half = edges[2].shape[0] // 2
    pairs = ((edges[0], edges[1]), (edges[2][:half], edges[2][half:]))
    last = [jnp.where(east, p, turned(q, W)) for p, q in pairs]
    first = [jnp.where(used, jnp.where(east, turned(p, -W), q), 0.0) for p, q in pairs]
    return last, first


def edge_kernel(tracers, levels, rows, *refs):
    sources, (keep, give, active, small, features), refs = refs[:7], refs[7:12], refs[12:]
    (fields, in_scale, storm, balance, *loads), scratch, sems = refs[:7], refs[7], refs[8]
    part = levels * rows
    chunks = [
        pltpu.make_async_copy(sources[0].at[pl.ds(t * part, part)], fields.at[pl.ds(t * part, part)], sems.at[t])
        for t in range(tracers)
    ]
    copies = [
        pltpu.make_async_copy(source, into, sems.at[tracers + n])
        for n, (source, into) in enumerate(zip(sources[1:], (in_scale, storm, balance, *loads)))
    ]
    for copy in copies + chunks:
        copy.start()
    for copy in copies:
        copy.wait()
    small[...] = jnp.zeros_like(small)
    at = 0
    for load in loads:
        small[at : at + load.shape[0], : load.shape[1]] = load[...].astype(F32)
        at += load.shape[0]
    lon, lev = lax.axis_index("lon"), lax.axis_index("lev")
    position = lax.broadcasted_iota(jnp.int32, balance.shape, 0)
    target = jnp.max(jnp.where(position == lon, balance[...], -1).astype(F32), axis=0, keepdims=True)
    scales = as_columns(scratch, [in_scale[...], loads[0][...], target])
    mask = jnp.where(column(scales, 2 * tracers, rows) >= 0.0, storm[...].astype(F32), 0.0)
    active[...] = mask
    lane = lane_ids(levels)
    own_scales, given_scales = jnp.zeros((levels, LANES), F32), jnp.zeros((levels, LANES), F32)
    for n in range(2 * tracers):
        scale = column(scales, n, levels)
        own_scales = jnp.where(lane == SCALE_LANE + n, scale, own_scales)
        given_scales = jnp.where(lane == SCALE_LANE + 2 * tracers + n, scale, given_scales)
    lane = lane_ids(1)
    mask_pack = jnp.zeros((1, LANES), F32)
    for i in range(rows):
        mask_pack = jnp.where((lane >= 6 * i) & (lane < 6 * i + 6), turned(mask[i : i + 1, :], 6 * i + W), mask_pack)
    mask_pack = jnp.broadcast_to(mask_pack, (EXTRA, LANES))
    east = lane % 6 < 3
    last_mask = jnp.where(east, mask_pack, 0.0)
    first_mask = turned(jnp.where(east, 0.0, mask_pack), -W)
    half = levels // 2
    head = lev == 0
    keep[levels + half :] = jnp.where(head, last_mask, first_mask)
    give[levels + half :] = turned(jnp.where(head, first_mask, last_mask), HALF_LANES)
    lane = lane_ids(levels)
    edges = []
    for t in range(tracers):
        chunks[t].wait()
        scale = column(scales, t, levels)
        pack = jnp.zeros((levels, LANES), F32)
        for i in range(rows):
            x = fields[pl.ds(t * part + i, levels, stride=rows), :]
            features[i, t * levels : (t + 1) * levels, :] = (x * scale).astype(BF16)
            pack = jnp.where((lane >= 6 * i) & (lane < 6 * i + 6), turned(x, 6 * i + W), pack)
        edges.append(pack)
    last, first = side_messages(edges)
    keep[:levels] = jnp.where(head, last[0], first[0]) + own_scales
    give[:levels] = turned(jnp.where(head, first[0], last[0]), HALF_LANES) + given_scales
    keep[levels : levels + half] = jnp.where(head, last[1], first[1])
    give[levels : levels + half] = turned(jnp.where(head, first[1], last[1]), HALF_LANES)


def binary_scale(largest):
    largest = largest * (1.0 / FIELD_BOUND)
    power, scale = jnp.zeros_like(largest), jnp.ones_like(largest)
    for bits in (64, 32, 16, 8, 4, 2, 1):
        small = largest < 2.0**-bits
        largest = jnp.where(small, largest * 2.0**bits, largest)
        scale = jnp.where(small, scale * 2.0**bits, scale)
        power = jnp.where(small, power + float(bits), power)
    return scale, power


def inverse_scale(power):
    scale = jnp.ones_like(power)
    for bits in (64, 32, 16, 8, 4, 2, 1):
        large = power > bits - 0.5
        scale = jnp.where(large, scale * 2.0**-bits, scale)
        power = jnp.where(large, power - float(bits), power)
    return scale


def to_fixed(x):
    return jnp.round(x).astype(jnp.int32).astype(jnp.int16)


def from_fixed(x):
    return x.astype(jnp.int32).astype(F32)


def row_message_kernel(tracers, levels, rows, moves, fields, active, *edge_rows):
    lat = lax.axis_index("lat")
    lane = lane_ids(levels)
    row = lax.broadcasted_iota(jnp.int32, (2 * EXTRA, LANES), 0)
    tail = W * tracers * levels
    for move, out in zip(moves, edge_rows):
        start = first_row_sent(move, lat, rows)
        values = [
            [fields[pl.ds((t * levels) * rows + start + r, levels, stride=rows), :] for r in range(W)]
            for t in range(tracers)
        ]
        largest = [jnp.max(jnp.maximum(jnp.maximum(jnp.abs(a), jnp.abs(b)), jnp.abs(c)), axis=1, keepdims=True) for a, b, c in values]
        bound = jnp.zeros((levels, LANES), F32)
        for t in range(tracers):
            bound = jnp.where(lane == t, largest[t], bound)
        scale, power = binary_scale(bound)
        for t in range(tracers):
            to_one = jnp.broadcast_to(scale[:, t : t + 1], (levels, LANES))
            for r, x in enumerate(values[t]):
                x = jnp.clip(x * to_one * FIXED_ONE, -FIXED_MOST, FIXED_MOST)
                out[(r * tracers + t) * levels : (r * tracers + t + 1) * levels, :] = to_fixed(x)
        out[tail : tail + levels, :] = to_fixed(power)
        mask = jnp.zeros(row.shape, F32)
        for r in range(W):
            mask = jnp.where(row == r, active[pl.ds(start + r, 1), :], mask)
        out[tail + levels :, :] = to_fixed(mask)


def first_row_sent(move, lat, rows):
    if move == 0:
        return jnp.where(lat == 0, rows - W, 0)
    return rows - W if move > 0 else 0


def first_row_received(move, lat, rows):
    if move == 0:
        return jnp.where(lat == 0, 0, rows - W)
    return rows - W if move > 0 else 0


def network(x, w_in, w_mid, w_last):
    hidden = silu(jnp.dot(w_in, x, preferred_element_type=F32)).astype(BF16)
    for layer in range(len(w_mid)):
        hidden = silu(jnp.dot(w_mid[layer], hidden, preferred_element_type=F32)).astype(BF16)
    return jnp.dot(w_last, hidden, preferred_element_type=F32).astype(BF16)


def taps(step, count):
    first = jnp.abs(step)
    second = jnp.where(count > 1.5, first, 0.0)
    third = jnp.where(count > 2.5, first, 0.0)
    rest = [1.0 - a for a in (first, second, third)]
    return (
        rest[0] * rest[1] * rest[2],
        first * rest[1] * rest[2] + rest[0] * second * rest[2] + rest[0] * rest[1] * third,
        first * second * rest[2] + first * rest[1] * third + rest[0] * second * third,
        first * second * third,
    )


def first_layer(x, w_in):
    return silu(lax.dot_general(x, w_in, (((0,), (1,)), ((), ())), preferred_element_type=F32)).astype(BF16)


def further_layers(hidden, w_mid, w_last):
    def layer(hidden, w):
        return lax.dot_general(hidden, w, (((1,), (1,)), ((), ())), preferred_element_type=F32)

    for k in range(len(w_mid)):
        hidden = silu(layer(hidden, w_mid[k])).astype(BF16)
    return layer(w_last, hidden).astype(BF16)


OUT_SCALE, LON, LON_SIGN, LAT, LAT_SIGN, EDGE, PLANES = 0, 3, 7, 8, 12, 13, 18


def write_weights(weights, small, tracers, levels):
    columns = small[...].T
    for t in range(tracers):
        weights[OUT_SCALE + t] = column(columns, t, levels)
    count = column(columns, tracers + 2, levels)
    lane = lane_ids(levels)
    place = lane % 6
    step = column(columns, tracers, levels) / count
    up = step > 0.0
    w = taps(step, count)
    weights[LON_SIGN] = jnp.where(up, 1.0, 0.0)
    for k in range(4):
        weights[LON + k] = jnp.where(
            up, jnp.where(lane >= k, w[k], 0.0), jnp.where(lane < LANES - (W - k), w[W - k], 0.0)
        )
    east = [jnp.where(up | (place > 2) | (place < d), 0.0, w[W - d]) for d in range(3)]
    west = [jnp.where(up & (place > 2) & (place + d < 6), w[W - d], 0.0) for d in range(3)]
    weights[EDGE] = east[0] + west[0]
    weights[EDGE + 1] = east[1]
    weights[EDGE + 2] = west[1]
    weights[EDGE + 3] = east[2]
    weights[EDGE + 4] = west[2]
    step = column(columns, tracers + 1, levels) / count
    up = step > 0.0
    w = taps(step, count)
    weights[LAT_SIGN] = jnp.where(up, 1.0, 0.0)
    for k in range(4):
        weights[LAT + k] = jnp.where(up, w[W - k], w[k])


def sweep_lon(values, weights, span):
    up = weights[LON_SIGN, span, :] > 0.5
    values = [jnp.where(up, q, turned(q, -W)) for q in values]
    w = [weights[LON + k, span, :] for k in range(4)]
    return [w[0] * q + w[1] * turned(q, 1) + w[2] * turned(q, 2) + w[3] * turned(q, 3) for q in values]


def own_network_kernel(tracers, levels, rows, mine, other, w_in, w_mid, w_out, tendency, token, x):
    token[...] = jnp.zeros_like(token)
    lev = lax.axis_index("lev")
    width = tracers * levels
    near = pl.ds(pl.multiple_of(lev * width, width), width)
    far = pl.ds(pl.multiple_of((1 - lev) * width, width), width)
    w_last = w_out[near, :]
    for i in range(rows):
        x[near, i * LANES : (i + 1) * LANES] = mine[i]
        x[far, i * LANES : (i + 1) * LANES] = other[i]
    tendency[...] = network(x[...], w_in[...], w_mid, w_last)


def own_sweep_kernel(tracers, levels, rows, fields, tendency, small, active, swept, weights):
    write_weights(weights, small, tracers, levels)
    for g in range(0, levels, GROUP):
        span = slice(g, g + GROUP)
        for t in range(tracers):
            at = t * levels + g
            scale = weights[OUT_SCALE + t, span, :]
            values = []
            for i in range(rows):
                moist = tendency[at : at + GROUP, i * LANES : (i + 1) * LANES].astype(F32)
                q = fields[pl.ds(at * rows + i, GROUP, stride=rows), :]
                values.append(q + scale * moist * active[i : i + 1, :])
            for i, q in enumerate(sweep_lon(values, weights, span)):
                swept[i, at : at + GROUP, :] = q


def read_scale(message, which, n, tracers, levels):
    at = SCALE_LANE + 2 * tracers * which + n
    return jnp.broadcast_to(message[:levels, at : at + 1], (levels, LANES))


def row_input_kernel(tracers, levels, moves, packs, *refs):
    count = len(moves)
    edge, edge_other, (w_in, hidden, fields, masks, x) = refs[:count], refs[count : 2 * count], refs[2 * count :]
    lev = lax.axis_index("lev")
    width = tracers * levels
    tail = W * width
    for which, source in ((0, edge), (1, edge_other)):
        start = lev * width if which == 0 else (1 - lev) * width
        for n in range(count):
            unit = inverse_scale(from_fixed(source[n][tail : tail + levels, :])) * (1.0 / FIXED_ONE)
            for t in range(tracers):
                in_scale = read_scale(packs, which, t, tracers, levels)
                scale = jnp.broadcast_to(unit[:, t : t + 1], (levels, LANES))
                to = pl.ds(pl.multiple_of(start + t * levels, levels), levels)
                parts = [(r * tracers + t) * levels for r in range(W)]
                values = [from_fixed(source[n][part : part + levels, :]) * scale for part in parts]
                for r, value in enumerate(values):
                    column_at = (n * W + r) * LANES
                    x[to, column_at : column_at + LANES] = (value * in_scale).astype(BF16)
                    if which == 0:
                        fields[n, t * W + r] = value
    for n in range(count):
        masks[n] = from_fixed(edge[n][tail + levels :, :])
    hidden[...] = first_layer(x[...], w_in[...])


def halo_network_kernel(tracers, levels, rows, moves, _, ring, *refs):
    count = len(moves)
    corner = refs[:count]
    weights, w_in, w_mid, w_out, mine, other, x = refs[count:]
    lat, lev = lax.axis_index("lat"), lax.axis_index("lev")
    width = tracers * levels
    head = lev == 0
    lane = lane_ids(levels)
    west = (lane % 6 >= 3) == head
    shifts = [jnp.where(head, a, b) for a, b in ((W, 0), (0, LANES - W))]
    half = levels // 2

    def place(message, part, which, extra):
        moved = []
        for shift in shifts:
            shift = shift + (extra + LANES - HALF_LANES * which)
            shift = jnp.where(shift >= 2 * LANES, shift - 2 * LANES, jnp.where(shift >= LANES, shift - LANES, shift))
            moved.append(turned(message[part, :], shift))
        return moved

    def unpack(part, which):
        lane_part = lane[: part.stop - part.start]
        values = place(ring, part, which, 0)
        used = lane_part < 48
        for n, move in enumerate(moves):
            base = 48 + 18 * n
            here = (lane_part >= base) & (lane_part < base + 18)
            far = place(corner[n], part, which, base - 6 * first_row_received(move, lat, rows))
            values = [jnp.where(here, q, value) for q, value in zip(far, values)]
            used = used | here
        used = used & west[: lane_part.shape[0]]
        return [jnp.where(used, value, 0.0) for value in values]

    mask = unpack(slice(levels + half, levels + half + EXTRA), 0)[0][:1]
    halos, scales = [], []
    for which in range(2):
        start = lev * width if which == 0 else (1 - lev) * width
        values = unpack(slice(0, levels), which)
        values.append(jnp.concatenate(unpack(slice(levels, levels + half), which), axis=0))
        for t, value in enumerate(values):
            in_scale, out_scale = (read_scale(ring, which, n, tracers, levels) for n in (t, tracers + t))
            halos.append(value)
            scales.append(out_scale)
            x[pl.ds(pl.multiple_of(start + t * levels, levels), levels), :] = (value * in_scale).astype(BF16)
    tendency = further_layers(first_layer(x[...], w_in[...]), w_mid, w_out[...]).astype(F32)
    x_tendency = [tendency[n * levels : (n + 1) * levels] for n in range(2 * tracers)]
    x_tendency = [
        jnp.where(head, x_tendency[n], x_tendency[(n + tracers) % (2 * tracers)]) for n in range(2 * tracers)
    ]
    values = [halo + scale * moist * mask for halo, scale, moist in zip(halos, scales, x_tendency)]
    if count == 2:
        up = weights[LAT_SIGN] > 0.5
        values = [jnp.where(up | (lane < 48), q, turned(q, -18)) for q in values]
    fix = [weights[EDGE] * q for q in values]
    for k, shift in ((1, 1), (2, -1), (3, 2), (4, -2)):
        fix = [f + weights[EDGE + k] * turned(q, shift) for f, q in zip(fix, values)]
    for t in range(tracers):
        mine[t] = fix[t]
        other[t] = fix[tracers + t]


def row_kernel(tracers, levels, moves, hidden, fields, masks, weights, w_mid, w_out, beyond, tendency):
    lev = lax.axis_index("lev")
    width = tracers * levels
    near = pl.ds(pl.multiple_of(lev * width, width), width)
    tendency[...] = further_layers(hidden[...], w_mid, w_out[near, :])
    up = weights[LAT_SIGN] > 0.5
    values = []
    for t in range(tracers):
        for r in range(W):
            rows_q = []
            for n in range(len(moves)):
                column_at = (n * W + r) * LANES
                moist = tendency[t * levels : (t + 1) * levels, column_at : column_at + LANES].astype(F32)
                rows_q.append(fields[n, t * W + r] + weights[OUT_SCALE + t] * moist * masks[n, r : r + 1, :])
            values.append(jnp.where(up, rows_q[0], rows_q[1]) if len(moves) == 2 else rows_q[0])
    for n, q in enumerate(sweep_lon(values, weights, slice(0, levels))):
        beyond[n] = q


def finish_kernel(tracers, levels, rows, moves, swept, weights, fix_mine, fix_other, beyond, out, result, sems):
    lat = lax.axis_index("lat")
    southward = jnp.where(lat == 0, 0.0, 1.0)
    copies = []
    lane = lane_ids(HALF_GROUP)
    at_edge = (lane < W) | (lane >= LANES - W)
    for g in range(0, levels, HALF_GROUP):
        span = slice(g, g + HALF_GROUP)
        sign = weights[LAT_SIGN, span, :]
        up = sign > 0.5
        w = [weights[LAT + k, span, :] for k in range(4)]
        for t in range(tracers):
            at = t * levels + g
            fix = fix_mine[t, span, :] + fix_other[t, span, :]

            def fixed(value, first):
                return value + jnp.where(at_edge, turned(fix, LANES - W - first), 0.0)

            inner = [fixed(swept[i, at : at + HALF_GROUP, :], 6 * i) for i in range(rows)]
            outer = [fixed(beyond[t * W + r, span, :], 48 + 6 * r) for r in range(W)]
            if len(moves) == 1:
                outer = [jnp.where(sign == southward, q, 0.0) for q in outer]
            line = []
            for i in range(rows + W):
                above = outer[i] if i < W else inner[i - W]
                below = inner[i] if i < rows else outer[i - rows]
                line.append(jnp.where(up, above, below))
            results = [w[0] * line[i] + w[1] * line[i + 1] + w[2] * line[i + 2] + w[3] * line[i + 3] for i in range(rows)]
            for i, value in enumerate(results):
                result[pl.ds(at * rows + i, HALF_GROUP, stride=rows), :] = value
            part = pl.ds(at * rows, HALF_GROUP * rows)
            copies.append(pltpu.make_async_copy(result.at[part], out.at[part], sems.at[len(copies)]))
            copies[-1].start()
    for copy in copies:
        copy.wait()


def call(kernel, out_shape, scratch, flops, moved, name, **specs):
    return pl.pallas_call(
        kernel,
        out_shape=out_shape,
        **specs,
        scratch_shapes=scratch,
        compiler_params=pltpu.CompilerParams(vmem_limit_bytes=VMEM_LIMIT),
        cost_estimate=pl.CostEstimate(flops=flops, bytes_accessed=moved, transcendentals=0),
        name=name,
    )


def swap_cores(x):
    return lax.ppermute(x, "lev", [(0, 1), (1, 0)])


def routes(lon_count, lat_count, move, along_lon):
    pairs = []
    for i in range(lon_count):
        for j in range(lat_count):
            to_lat = 1 - j if move == 0 else j + (move or 0)
            if not 0 <= to_lat < lat_count:
                continue
            for k in range(2):
                to_lon = (i + (1 - 2 * k)) % lon_count if along_lon else i
                pairs.append((((i * lat_count) + j) * 2 + k, ((to_lon * lat_count) + to_lat) * 2 + k))
    return pairs


def send(x, move, along_lon):
    axes = ("lon", "lat", "lev")
    lon_count, lat_count = lax.axis_size("lon"), lax.axis_size("lat")
    if move is None:
        pairs = []
        for i in range(lon_count):
            for j in range(lat_count):
                for k in range(2):
                    to_lon = (i + (1 - 2 * k)) % lon_count
                    pairs.append(((i * lat_count + j) * 2 + k, (to_lon * lat_count + j) * 2 + k))
    else:
        pairs = routes(lon_count, lat_count, move, along_lon)
    return lax.ppermute(x, axes, pairs)


def on_device(fields, in_scale, out_scale, w_in, w_mid, w_out, storm_mask, balance, substeps, courant):
    tracers, levels, rows, columns = fields.shape
    width = tracers * levels
    moves = (0,) if lax.axis_size("lat") == 2 else (1, -1)
    count = len(moves)
    flat = fields.reshape(width * rows, columns)
    edge_shape = jax.ShapeDtypeStruct((W * width + levels + 2 * EXTRA, columns), jnp.int16)
    pack_shape = jax.ShapeDtypeStruct((levels + levels // 2 + EXTRA, LANES), F32)
    inputs = (flat, in_scale, storm_mask, balance.T, out_scale, courant, substeps.reshape(1, levels))
    inputs = [pltpu.with_memory_space_constraint(x, pltpu.HBM) for x in inputs]
    small_shape = jax.ShapeDtypeStruct((EXTRA, LANES), F32)
    keep, give, active, small, features = call(
        functools.partial(edge_kernel, tracers, levels, rows),
        [pack_shape, pack_shape, jax.ShapeDtypeStruct((rows, columns), F32), small_shape,
         jax.ShapeDtypeStruct((rows, width, columns), BF16)],
        [pltpu.VMEM(x.shape, x.dtype) for x in inputs]
        + [pltpu.VMEM((EXTRA, LANES), F32), pltpu.SemaphoreType.DMA((len(inputs) - 1 + tracers,))],
        10000000000, 0, "edges",
        in_specs=[pl.BlockSpec(memory_space=pltpu.HBM)] * len(inputs),
    )(*inputs)
    given = swap_cores(give)
    features_other = swap_cores(features)
    edge_rows = call(
        functools.partial(row_message_kernel, tracers, levels, rows, moves),
        [edge_shape] * count,
        [],
        10000000000, 0, "row_messages",
    )(flat, active)
    packs = keep + given
    corner = [send(packs, move, True) for move in moves]
    ring = send(packs, None, True)
    edge = [send(e, move, False) for e, move in zip(edge_rows, moves)]

    tendency, token = call(
        functools.partial(own_network_kernel, tracers, levels, rows),
        [jax.ShapeDtypeStruct((width, rows * columns), BF16), jax.ShapeDtypeStruct((2 * EXTRA, LANES), jnp.int16)],
        [pltpu.VMEM((2 * width, rows * columns), BF16)],
        10000000000, 0, "own_network",
    )(features, features_other, w_in, w_mid, w_out)
    swept, weights = call(
        functools.partial(own_sweep_kernel, tracers, levels, rows),
        [jax.ShapeDtypeStruct((rows, width, columns), F32), jax.ShapeDtypeStruct((PLANES, levels, LANES), F32)],
        [],
        10000000000, 0, "own_sweep",
    )(flat, tendency, small, active)

    fix_shape = jax.ShapeDtypeStruct((tracers, levels, LANES), F32)
    edge_other = [swap_cores(e + token[:1]) for e in edge]
    total = W * count * LANES
    physics_shape = jax.ShapeDtypeStruct((count, tracers * W, levels, LANES), F32)
    hidden, row_fields, row_masks = call(
        functools.partial(row_input_kernel, tracers, levels, moves),
        [jax.ShapeDtypeStruct((total, w_in.shape[0]), BF16), physics_shape,
         jax.ShapeDtypeStruct((count, 2 * EXTRA, LANES), F32)],
        [pltpu.VMEM((2 * width, total), BF16)],
        10**10, 0, "row_input",
    )(packs, *edge, *edge_other, w_in)
    fix_mine, fix_given = call(
        functools.partial(halo_network_kernel, tracers, levels, rows, moves),
        [fix_shape, fix_shape],
        [pltpu.VMEM((2 * width, LANES), BF16)],
        10**10, 0, "halo_network",
    )(row_masks, ring, *corner, weights, w_in, w_mid, w_out)
    fix_other = swap_cores(fix_given)
    beyond = call(
        functools.partial(row_kernel, tracers, levels, moves),
        jax.ShapeDtypeStruct((tracers * W, levels, LANES), F32),
        [pltpu.VMEM((width, total), BF16)],
        10**10, 0, "row_network",
    )(hidden, row_fields, row_masks, weights, w_mid, w_out)
    out = call(
        functools.partial(finish_kernel, tracers, levels, rows, moves),
        jax.ShapeDtypeStruct((width * rows, columns), F32),
        [pltpu.VMEM((width * rows, columns), F32), pltpu.SemaphoreType.DMA((width // HALF_GROUP,))],
        10000000000, 0, "finish",
        out_specs=pl.BlockSpec(memory_space=pltpu.HBM),
    )(swept, weights, fix_mine, fix_other, beyond)
    return out.reshape(fields.shape)


def solution(mesh):
    in_specs = (
        P("lev", None, ("group", "lat"), "lon"),
        P("lev", None),
        P("lev", None),
        P(),
        P(),
        P(),
        P(("group", "lat"), "lon"),
        P(("group", "lat"), None),
        P(),
        P(),
    )
    out_specs = P("lev", None, ("group", "lat"), "lon")
    return jax.shard_map(
        on_device, mesh=mesh, in_specs=in_specs, out_specs=out_specs, check_vma=False
    )
```

```python
import functools

import jax
import jax.numpy as jnp
from jax import lax
from jax.experimental import pallas as pl
from jax.experimental.pallas import tpu as pltpu
from jax.sharding import PartitionSpec as P

W = 3
LANES = 128
HALF_LANES = 48
SCALE_LANE = 96
FIELD_BOUND = 8.0
FIXED_ONE = 32768.0 / FIELD_BOUND
FIXED_MOST = 32767.0
EXTRA = 8
F32 = jnp.float32
BF16 = jnp.bfloat16
GROUP = 32
HALF_GROUP = 16
VMEM_LIMIT = 40 * 1024 * 1024


def lane_ids(rows):
    return lax.broadcasted_iota(jnp.int32, (rows, LANES), 1)


def turned(x, shift):
    if isinstance(shift, int):
        shift %= LANES
        if shift == 0:
            return x
    return pltpu.roll(x, shift, 1)


def silu(v):
    half = 0.5 * v
    return half + half * jnp.tanh(half)


def as_columns(scratch, parts):
    scratch[...] = jnp.zeros_like(scratch)
    at = 0
    for part in parts:
        scratch[at : at + part.shape[0], : part.shape[1]] = part
        at += part.shape[0]
    return scratch[...].T


def column(turned_rows, index, levels):
    return jnp.broadcast_to(turned_rows[:levels, index : index + 1], (levels, LANES))


def side_messages(edges):
    lane = lane_ids(1)
    east = lane % 6 < 3
    used = lane < HALF_LANES
    half = edges[2].shape[0] // 2
    pairs = ((edges[0], edges[1]), (edges[2][:half], edges[2][half:]))
    last = [jnp.where(east, p, turned(q, W)) for p, q in pairs]
    first = [jnp.where(used, jnp.where(east, turned(p, -W), q), 0.0) for p, q in pairs]
    return last, first


def scalar_kernel(tracers, levels, rows, *refs):
    sources, (small, active, scale_lanes, mask_rows, in_scales), refs = refs[:6], refs[6:11], refs[11:]
    (in_scale, storm, balance, *loads), scratch, sems = refs[:6], refs[6], refs[7]
    copies = [
        pltpu.make_async_copy(source, into, sems.at[n]) for n, (source, into) in enumerate(zip(sources, refs[:6]))
    ]
    for copy in copies:
        copy.start()
    for copy in copies:
        copy.wait()
    small[...] = jnp.zeros_like(small)
    at = 0
    for load in loads:
        small[at : at + load.shape[0], : load.shape[1]] = load[...].astype(F32)
        at += load.shape[0]
    lon, lev = lax.axis_index("lon"), lax.axis_index("lev")
    position = lax.broadcasted_iota(jnp.int32, balance.shape, 0)
    target = jnp.max(jnp.where(position == lon, balance[...], -1).astype(F32), axis=0, keepdims=True)
    scales = as_columns(scratch, [in_scale[...], loads[0][...], target])
    mask = jnp.where(column(scales, 2 * tracers, rows) >= 0.0, storm[...].astype(F32), 0.0)
    active[...] = mask
    lane = lane_ids(levels)
    own_scales, given_scales = jnp.zeros((levels, LANES), F32), jnp.zeros((levels, LANES), F32)
    for n in range(2 * tracers):
        scale = column(scales, n, levels)
        own_scales = jnp.where(lane == SCALE_LANE + n, scale, own_scales)
        given_scales = jnp.where(lane == SCALE_LANE + 2 * tracers + n, scale, given_scales)
        if n < tracers:
            in_scales[n] = scale
    scale_lanes[0], scale_lanes[1] = own_scales, given_scales
    lane = lane_ids(1)
    mask_pack = jnp.zeros((1, LANES), F32)
    for i in range(rows):
        mask_pack = jnp.where((lane >= 6 * i) & (lane < 6 * i + 6), turned(mask[i : i + 1, :], 6 * i + W), mask_pack)
    mask_pack = jnp.broadcast_to(mask_pack, (EXTRA, LANES))
    east = lane % 6 < 3
    last_mask = jnp.where(east, mask_pack, 0.0)
    first_mask = turned(jnp.where(east, 0.0, mask_pack), -W)
    head = lev == 0
    mask_rows[0] = jnp.where(head, last_mask, first_mask)
    mask_rows[1] = turned(jnp.where(head, first_mask, last_mask), HALF_LANES)


def edge_kernel(tracers, levels, rows, fields, scale_lanes, mask_rows, in_scales, keep, give, features):
    lane = lane_ids(levels)
    half = levels // 2
    head = lax.axis_index("lev") == 0
    edges, values = [], []
    for t in range(tracers):
        pack = jnp.zeros((levels, LANES), F32)
        for i in range(rows):
            x = fields[pl.ds((t * levels) * rows + i, levels, stride=rows), :]
            values.append((x * in_scales[t]).astype(BF16))
            pack = jnp.where((lane >= 6 * i) & (lane < 6 * i + 6), turned(x, 6 * i + W), pack)
        edges.append(pack)
    last, first = side_messages(edges)
    keep[:levels] = jnp.where(head, last[0], first[0]) + scale_lanes[0]
    give[:levels] = turned(jnp.where(head, first[0], last[0]), HALF_LANES) + scale_lanes[1]
    keep[levels : levels + half] = jnp.where(head, last[1], first[1])
    give[levels : levels + half] = turned(jnp.where(head, first[1], last[1]), HALF_LANES)
    keep[levels + half :] = mask_rows[0]
    give[levels + half :] = mask_rows[1]
    for n, x in enumerate(values):
        t, i = n // rows, n % rows
        features[i, t * levels : (t + 1) * levels, :] = x


def binary_scale(largest):
    largest = largest * (1.0 / FIELD_BOUND)
    power, scale = jnp.zeros_like(largest), jnp.ones_like(largest)
    for bits in (64, 32, 16, 8, 4, 2, 1):
        small = largest < 2.0**-bits
        largest = jnp.where(small, largest * 2.0**bits, largest)
        scale = jnp.where(small, scale * 2.0**bits, scale)
        power = jnp.where(small, power + float(bits), power)
    return scale, power


def inverse_scale(power):
    scale = jnp.ones_like(power)
    for bits in (64, 32, 16, 8, 4, 2, 1):
        large = power > bits - 0.5
        scale = jnp.where(large, scale * 2.0**-bits, scale)
        power = jnp.where(large, power - float(bits), power)
    return scale


def to_fixed(x):
    return jnp.round(x).astype(jnp.int32).astype(jnp.int16)


def from_fixed(x):
    return x.astype(jnp.int32).astype(F32)


def row_message_kernel(tracers, levels, rows, moves, fields, active, *edge_rows):
    lat = lax.axis_index("lat")
    lane = lane_ids(levels)
    row = lax.broadcasted_iota(jnp.int32, (2 * EXTRA, LANES), 0)
    tail = W * tracers * levels
    for move, out in zip(moves, edge_rows):
        start = first_row_sent(move, lat, rows)
        values = [
            [fields[pl.ds((t * levels) * rows + start + r, levels, stride=rows), :] for r in range(W)]
            for t in range(tracers)
        ]
        largest = [jnp.max(jnp.maximum(jnp.maximum(jnp.abs(a), jnp.abs(b)), jnp.abs(c)), axis=1, keepdims=True) for a, b, c in values]
        bound = jnp.zeros((levels, LANES), F32)
        for t in range(tracers):
            bound = jnp.where(lane == t, largest[t], bound)
        scale, power = binary_scale(bound)
        for t in range(tracers):
            to_one = jnp.broadcast_to(scale[:, t : t + 1], (levels, LANES))
            for r, x in enumerate(values[t]):
                x = jnp.clip(x * to_one * FIXED_ONE, -FIXED_MOST, FIXED_MOST)
                out[(r * tracers + t) * levels : (r * tracers + t + 1) * levels, :] = to_fixed(x)
        out[tail : tail + levels, :] = to_fixed(power)
        mask = jnp.zeros(row.shape, F32)
        for r in range(W):
            mask = jnp.where(row == r, active[pl.ds(start + r, 1), :], mask)
        out[tail + levels :, :] = to_fixed(mask)


def first_row_sent(move, lat, rows):
    if move == 0:
        return jnp.where(lat == 0, rows - W, 0)
    return rows - W if move > 0 else 0


def first_row_received(move, lat, rows):
    if move == 0:
        return jnp.where(lat == 0, 0, rows - W)
    return rows - W if move > 0 else 0


def network(x, w_in, w_mid, w_last):
    hidden = silu(jnp.dot(w_in, x, preferred_element_type=F32)).astype(BF16)
    for layer in range(len(w_mid)):
        hidden = silu(jnp.dot(w_mid[layer], hidden, preferred_element_type=F32)).astype(BF16)
    return jnp.dot(w_last, hidden, preferred_element_type=F32).astype(BF16)


def taps(step, count):
    first = jnp.abs(step)
    second = jnp.where(count > 1.5, first, 0.0)
    third = jnp.where(count > 2.5, first, 0.0)
    rest = [1.0 - a for a in (first, second, third)]
    return (
        rest[0] * rest[1] * rest[2],
        first * rest[1] * rest[2] + rest[0] * second * rest[2] + rest[0] * rest[1] * third,
        first * second * rest[2] + first * rest[1] * third + rest[0] * second * third,
        first * second * third,
    )


def first_layer(x, w_in):
    return silu(lax.dot_general(x, w_in, (((0,), (1,)), ((), ())), preferred_element_type=F32)).astype(BF16)


def further_layers(hidden, w_mid, w_last):
    def layer(hidden, w):
        return lax.dot_general(hidden, w, (((1,), (1,)), ((), ())), preferred_element_type=F32)

    for k in range(len(w_mid)):
        hidden = silu(layer(hidden, w_mid[k])).astype(BF16)
    return layer(w_last, hidden).astype(BF16)


OUT_SCALE, LON, LON_SIGN, LAT, LAT_SIGN, EDGE, PLANES = 0, 3, 7, 8, 12, 13, 18


def write_weights(weights, small, tracers, levels):
    columns = small[...].T
    for t in range(tracers):
        weights[OUT_SCALE + t] = column(columns, t, levels)
    count = column(columns, tracers + 2, levels)
    lane = lane_ids(levels)
    place = lane % 6
    step = column(columns, tracers, levels) / count
    up = step > 0.0
    w = taps(step, count)
    weights[LON_SIGN] = jnp.where(up, 1.0, 0.0)
    for k in range(4):
        weights[LON + k] = jnp.where(
            up, jnp.where(lane >= k, w[k], 0.0), jnp.where(lane < LANES - (W - k), w[W - k], 0.0)
        )
    east = [jnp.where(up | (place > 2) | (place < d), 0.0, w[W - d]) for d in range(3)]
    west = [jnp.where(up & (place > 2) & (place + d < 6), w[W - d], 0.0) for d in range(3)]
    weights[EDGE] = east[0] + west[0]
    weights[EDGE + 1] = east[1]
    weights[EDGE + 2] = west[1]
    weights[EDGE + 3] = east[2]
    weights[EDGE + 4] = west[2]
    step = column(columns, tracers + 1, levels) / count
    up = step > 0.0
    w = taps(step, count)
    weights[LAT_SIGN] = jnp.where(up, 1.0, 0.0)
    for k in range(4):
        weights[LAT + k] = jnp.where(up, w[W - k], w[k])


def sweep_lon(values, weights, span):
    up = weights[LON_SIGN, span, :] > 0.5
    values = [jnp.where(up, q, turned(q, -W)) for q in values]
    w = [weights[LON + k, span, :] for k in range(4)]
    return [w[0] * q + w[1] * turned(q, 1) + w[2] * turned(q, 2) + w[3] * turned(q, 3) for q in values]


def own_network_kernel(tracers, levels, rows, mine, other, w_in, w_mid, w_out, tendency, token, x):
    token[...] = jnp.zeros_like(token)
    lev = lax.axis_index("lev")
    width = tracers * levels
    near = pl.ds(pl.multiple_of(lev * width, width), width)
    far = pl.ds(pl.multiple_of((1 - lev) * width, width), width)
    w_last = w_out[near, :]
    for i in range(rows):
        x[near, i * LANES : (i + 1) * LANES] = mine[i]
        x[far, i * LANES : (i + 1) * LANES] = other[i]
    tendency[...] = network(x[...], w_in[...], w_mid, w_last)


def own_sweep_kernel(tracers, levels, rows, fields, tendency, small, active, swept, weights):
    write_weights(weights, small, tracers, levels)
    for g in range(0, levels, GROUP):
        span = slice(g, g + GROUP)
        for t in range(tracers):
            at = t * levels + g
            scale = weights[OUT_SCALE + t, span, :]
            values = []
            for i in range(rows):
                moist = tendency[at : at + GROUP, i * LANES : (i + 1) * LANES].astype(F32)
                q = fields[pl.ds(at * rows + i, GROUP, stride=rows), :]
                values.append(q + scale * moist * active[i : i + 1, :])
            for i, q in enumerate(sweep_lon(values, weights, span)):
                swept[i, at : at + GROUP, :] = q


def read_scale(message, which, n, tracers, levels):
    at = SCALE_LANE + 2 * tracers * which + n
    return jnp.broadcast_to(message[:levels, at : at + 1], (levels, LANES))


def row_input_kernel(tracers, levels, moves, packs, *refs):
    count = len(moves)
    edge, edge_other, (w_in, hidden, fields, masks, x) = refs[:count], refs[count : 2 * count], refs[2 * count :]
    lev = lax.axis_index("lev")
    width = tracers * levels
    tail = W * width
    for which, source in ((0, edge), (1, edge_other)):
        start = lev * width if which == 0 else (1 - lev) * width
        for n in range(count):
            unit = inverse_scale(from_fixed(source[n][tail : tail + levels, :])) * (1.0 / FIXED_ONE)
            for t in range(tracers):
                in_scale = read_scale(packs, which, t, tracers, levels)
                scale = jnp.broadcast_to(unit[:, t : t + 1], (levels, LANES))
                to = pl.ds(pl.multiple_of(start + t * levels, levels), levels)
                parts = [(r * tracers + t) * levels for r in range(W)]
                values = [from_fixed(source[n][part : part + levels, :]) * scale for part in parts]
                for r, value in enumerate(values):
                    column_at = (n * W + r) * LANES
                    x[to, column_at : column_at + LANES] = (value * in_scale).astype(BF16)
                    if which == 0:
                        fields[n, t * W + r] = value
    for n in range(count):
        masks[n] = from_fixed(edge[n][tail + levels :, :])
    hidden[...] = first_layer(x[...], w_in[...])


def edge_corrections(values, weights, head):
    east = jnp.where(head, LANES - 1, 1), jnp.where(head, LANES - 2, 2)
    w = [jnp.where(head, weights[EDGE + 2 * k], weights[EDGE + 2 * k - 1]) for k in (1, 2)]
    return [weights[EDGE] * q + w[0] * turned(q, east[0]) + w[1] * turned(q, east[1]) for q in values]


def halo_network_kernel(tracers, levels, rows, moves, _, ring, *refs):
    count = len(moves)
    corner = refs[:count]
    weights, w_in, w_mid, w_out, mine, other, x = refs[count:]
    lat, lev = lax.axis_index("lat"), lax.axis_index("lev")
    width = tracers * levels
    head = lev == 0
    lane = lane_ids(levels)
    west = (lane % 6 >= 3) == head
    shifts = [jnp.where(head, a, b) for a, b in ((W, 0), (0, LANES - W))]
    half = levels // 2

    def place(message, part, which, extra):
        moved = []
        for shift in shifts:
            shift = shift + (extra + LANES - HALF_LANES * which)
            shift = jnp.where(shift >= 2 * LANES, shift - 2 * LANES, jnp.where(shift >= LANES, shift - LANES, shift))
            moved.append(turned(message[part, :], shift))
        return moved

    def unpack(part, which):
        lane_part = lane[: part.stop - part.start]
        values = place(ring, part, which, 0)
        used = lane_part < 48
        for n, move in enumerate(moves):
            base = 48 + 18 * n
            here = (lane_part >= base) & (lane_part < base + 18)
            far = place(corner[n], part, which, base - 6 * first_row_received(move, lat, rows))
            values = [jnp.where(here, q, value) for q, value in zip(far, values)]
            used = used | here
        used = used & west[: lane_part.shape[0]]
        return [jnp.where(used, value, 0.0) for value in values]

    mask = unpack(slice(levels + half, levels + half + EXTRA), 0)[0][:1]
    halos, scales = [], []
    for which in range(2):
        start = lev * width if which == 0 else (1 - lev) * width
        values = unpack(slice(0, levels), which)
        values.append(jnp.concatenate(unpack(slice(levels, levels + half), which), axis=0))
        for t, value in enumerate(values):
            in_scale, out_scale = (read_scale(ring, which, n, tracers, levels) for n in (t, tracers + t))
            halos.append(value)
            scales.append(out_scale)
            x[pl.ds(pl.multiple_of(start + t * levels, levels), levels), :] = (value * in_scale).astype(BF16)
    tendency = further_layers(first_layer(x[...], w_in[...]), w_mid, w_out[...]).astype(F32)
    x_tendency = [tendency[n * levels : (n + 1) * levels] for n in range(2 * tracers)]
    x_tendency = [
        jnp.where(head, x_tendency[n], x_tendency[(n + tracers) % (2 * tracers)]) for n in range(2 * tracers)
    ]
    values = [halo + scale * moist * mask for halo, scale, moist in zip(halos, scales, x_tendency)]
    if count == 2:
        up = weights[LAT_SIGN] > 0.5
        values = [jnp.where(up | (lane < 48), q, turned(q, -18)) for q in values]
    for t, q in enumerate(edge_corrections(values[tracers:], weights, head)):
        other[t] = q
    for t in range(tracers):
        mine[t] = values[t]


def row_kernel(tracers, levels, moves, hidden, fields, masks, halo, weights, w_mid, w_out, beyond, fix, tendency):
    lev = lax.axis_index("lev")
    for t, q in enumerate(edge_corrections([halo[t] for t in range(tracers)], weights, lev == 0)):
        fix[t] = q
    width = tracers * levels
    near = pl.ds(pl.multiple_of(lev * width, width), width)
    tendency[...] = further_layers(hidden[...], w_mid, w_out[near, :])
    up = weights[LAT_SIGN] > 0.5
    values = []
    for t in range(tracers):
        for r in range(W):
            rows_q = []
            for n in range(len(moves)):
                column_at = (n * W + r) * LANES
                moist = tendency[t * levels : (t + 1) * levels, column_at : column_at + LANES].astype(F32)
                rows_q.append(fields[n, t * W + r] + weights[OUT_SCALE + t] * moist * masks[n, r : r + 1, :])
            values.append(jnp.where(up, rows_q[0], rows_q[1]) if len(moves) == 2 else rows_q[0])
    for n, q in enumerate(sweep_lon(values, weights, slice(0, levels))):
        beyond[n] = q


def finish_kernel(tracers, levels, rows, moves, swept, weights, fix_mine, fix_other, beyond, out, result, sems):
    lat = lax.axis_index("lat")
    southward = jnp.where(lat == 0, 0.0, 1.0)
    copies = []
    lane = lane_ids(HALF_GROUP)
    at_edge = (lane < W) | (lane >= LANES - W)
    for g in range(0, levels, HALF_GROUP):
        span = slice(g, g + HALF_GROUP)
        sign = weights[LAT_SIGN, span, :]
        up = sign > 0.5
        w = [weights[LAT + k, span, :] for k in range(4)]
        for t in range(tracers):
            at = t * levels + g
            fix = fix_mine[t, span, :] + fix_other[t, span, :]

            def fixed(value, first):
                return value + jnp.where(at_edge, turned(fix, LANES - W - first), 0.0)

            inner = [fixed(swept[i, at : at + HALF_GROUP, :], 6 * i) for i in range(rows)]
            outer = [fixed(beyond[t * W + r, span, :], 48 + 6 * r) for r in range(W)]
            if len(moves) == 1:
                outer = [jnp.where(sign == southward, q, 0.0) for q in outer]
            line = []
            for i in range(rows + W):
                above = outer[i] if i < W else inner[i - W]
                below = inner[i] if i < rows else outer[i - rows]
                line.append(jnp.where(up, above, below))
            results = [w[0] * line[i] + w[1] * line[i + 1] + w[2] * line[i + 2] + w[3] * line[i + 3] for i in range(rows)]
            for i, value in enumerate(results):
                result[pl.ds(at * rows + i, HALF_GROUP, stride=rows), :] = value
            part = pl.ds(at * rows, HALF_GROUP * rows)
            copies.append(pltpu.make_async_copy(result.at[part], out.at[part], sems.at[len(copies)]))
            copies[-1].start()
    for copy in copies:
        copy.wait()


def call(kernel, out_shape, scratch, flops, moved, name, **specs):
    return pl.pallas_call(
        kernel,
        out_shape=out_shape,
        **specs,
        scratch_shapes=scratch,
        compiler_params=pltpu.CompilerParams(vmem_limit_bytes=VMEM_LIMIT),
        cost_estimate=pl.CostEstimate(flops=flops, bytes_accessed=moved, transcendentals=0),
        name=name,
    )


def swap_cores(x):
    return lax.ppermute(x, "lev", [(0, 1), (1, 0)])


def routes(lon_count, lat_count, move, along_lon):
    pairs = []
    for i in range(lon_count):
        for j in range(lat_count):
            to_lat = 1 - j if move == 0 else j + (move or 0)
            if not 0 <= to_lat < lat_count:
                continue
            for k in range(2):
                to_lon = (i + (1 - 2 * k)) % lon_count if along_lon else i
                pairs.append((((i * lat_count) + j) * 2 + k, ((to_lon * lat_count) + to_lat) * 2 + k))
    return pairs


def send(x, move, along_lon):
    axes = ("lon", "lat", "lev")
    lon_count, lat_count = lax.axis_size("lon"), lax.axis_size("lat")
    if move is None:
        pairs = []
        for i in range(lon_count):
            for j in range(lat_count):
                for k in range(2):
                    to_lon = (i + (1 - 2 * k)) % lon_count
                    pairs.append(((i * lat_count + j) * 2 + k, (to_lon * lat_count + j) * 2 + k))
    else:
        pairs = routes(lon_count, lat_count, move, along_lon)
    return lax.ppermute(x, axes, pairs)


def on_device(fields, in_scale, out_scale, w_in, w_mid, w_out, storm_mask, balance, substeps, courant):
    tracers, levels, rows, columns = fields.shape
    width = tracers * levels
    moves = (0,) if lax.axis_size("lat") == 2 else (1, -1)
    count = len(moves)
    flat = fields.reshape(width * rows, columns)
    edge_shape = jax.ShapeDtypeStruct((W * width + levels + 2 * EXTRA, columns), jnp.int16)
    pack_shape = jax.ShapeDtypeStruct((levels + levels // 2 + EXTRA, LANES), F32)
    inputs = (in_scale, storm_mask, balance.T, out_scale, courant, substeps.reshape(1, levels))
    inputs = [pltpu.with_memory_space_constraint(x, pltpu.HBM) for x in inputs]
    small, active, scale_lanes, mask_rows, in_scales = call(
        functools.partial(scalar_kernel, tracers, levels, rows),
        [jax.ShapeDtypeStruct((EXTRA, LANES), F32), jax.ShapeDtypeStruct((rows, columns), F32),
         jax.ShapeDtypeStruct((2, levels, LANES), F32), jax.ShapeDtypeStruct((2, EXTRA, LANES), F32),
         jax.ShapeDtypeStruct((tracers, levels, LANES), F32)],
        [pltpu.VMEM(x.shape, x.dtype) for x in inputs]
        + [pltpu.VMEM((EXTRA, LANES), F32), pltpu.SemaphoreType.DMA((len(inputs),))],
        10**10, 0, "scalars",
        in_specs=[pl.BlockSpec(memory_space=pltpu.HBM)] * len(inputs),
    )(*inputs)
    keep, give, features = call(
        functools.partial(edge_kernel, tracers, levels, rows),
        [pack_shape, pack_shape, jax.ShapeDtypeStruct((rows, width, columns), BF16)],
        [],
        10**10, 0, "edges",
    )(flat, scale_lanes, mask_rows, in_scales)
    given = swap_cores(give)
    features_other = swap_cores(features)
    edge_rows = call(
        functools.partial(row_message_kernel, tracers, levels, rows, moves),
        [edge_shape] * count,
        [],
        10000000000, 0, "row_messages",
    )(flat, active)
    packs = keep + given
    corner = [send(packs, move, True) for move in moves]
    ring = send(packs, None, True)
    edge = [send(e, move, False) for e, move in zip(edge_rows, moves)]

    tendency, token = call(
        functools.partial(own_network_kernel, tracers, levels, rows),
        [jax.ShapeDtypeStruct((width, rows * columns), BF16), jax.ShapeDtypeStruct((2 * EXTRA, LANES), jnp.int16)],
        [pltpu.VMEM((2 * width, rows * columns), BF16)],
        10000000000, 0, "own_network",
    )(features, features_other, w_in, w_mid, w_out)
    swept, weights = call(
        functools.partial(own_sweep_kernel, tracers, levels, rows),
        [jax.ShapeDtypeStruct((rows, width, columns), F32), jax.ShapeDtypeStruct((PLANES, levels, LANES), F32)],
        [],
        10000000000, 0, "own_sweep",
    )(flat, tendency, small, active)

    fix_shape = jax.ShapeDtypeStruct((tracers, levels, LANES), F32)
    edge_other = [swap_cores(e + token[:1]) for e in edge]
    total = W * count * LANES
    physics_shape = jax.ShapeDtypeStruct((count, tracers * W, levels, LANES), F32)
    hidden, row_fields, row_masks = call(
        functools.partial(row_input_kernel, tracers, levels, moves),
        [jax.ShapeDtypeStruct((total, w_in.shape[0]), BF16), physics_shape,
         jax.ShapeDtypeStruct((count, 2 * EXTRA, LANES), F32)],
        [pltpu.VMEM((2 * width, total), BF16)],
        10**10, 0, "row_input",
    )(packs, *edge, *edge_other, w_in)
    halo, fix_given = call(
        functools.partial(halo_network_kernel, tracers, levels, rows, moves),
        [fix_shape, fix_shape],
        [pltpu.VMEM((2 * width, LANES), BF16)],
        10**10, 0, "halo_network",
    )(row_masks, ring, *corner, weights, w_in, w_mid, w_out)
    fix_other = swap_cores(fix_given)
    beyond, fix_mine = call(
        functools.partial(row_kernel, tracers, levels, moves),
        [jax.ShapeDtypeStruct((tracers * W, levels, LANES), F32), fix_shape],
        [pltpu.VMEM((width, total), BF16)],
        10**10, 0, "row_network",
    )(hidden, row_fields, row_masks, halo, weights, w_mid, w_out)
    out = call(
        functools.partial(finish_kernel, tracers, levels, rows, moves),
        jax.ShapeDtypeStruct((width * rows, columns), F32),
        [pltpu.VMEM((width * rows, columns), F32), pltpu.SemaphoreType.DMA((width // HALF_GROUP,))],
        10000000000, 0, "finish",
        out_specs=pl.BlockSpec(memory_space=pltpu.HBM),
    )(swept, weights, fix_mine, fix_other, beyond)
    return out.reshape(fields.shape)


def solution(mesh):
    in_specs = (
        P("lev", None, ("group", "lat"), "lon"),
        P("lev", None),
        P("lev", None),
        P(),
        P(),
        P(),
        P(("group", "lat"), "lon"),
        P(("group", "lat"), None),
        P(),
        P(),
    )
    out_specs = P("lev", None, ("group", "lat"), "lon")
    return jax.shard_map(
        on_device, mesh=mesh, in_specs=in_specs, out_specs=out_specs, check_vma=False
    )
```

```python
import functools

import jax
import jax.numpy as jnp
from jax import lax
from jax.experimental import pallas as pl
from jax.experimental.pallas import tpu as pltpu
from jax.sharding import PartitionSpec as P

W = 3
LANES = 128
HALF_LANES = 48
TARGET_ROW = 6
SCALE_LANE = 96
FIELD_BOUND = 8.0
FIXED_ONE = 32768.0 / FIELD_BOUND
FIXED_MOST = 32767.0
EXTRA = 8
F32 = jnp.float32
BF16 = jnp.bfloat16
GROUP = 32
HALF_GROUP = 16
VMEM_LIMIT = 40 * 1024 * 1024


def lane_ids(rows):
    return lax.broadcasted_iota(jnp.int32, (rows, LANES), 1)


def turned(x, shift):
    if isinstance(shift, int):
        shift %= LANES
        if shift == 0:
            return x
    return pltpu.roll(x, shift, 1)


def silu(v):
    half = 0.5 * v
    return half + half * jnp.tanh(half)


def as_columns(scratch, parts):
    scratch[...] = jnp.zeros_like(scratch)
    at = 0
    for part in parts:
        scratch[at : at + part.shape[0], : part.shape[1]] = part
        at += part.shape[0]
    return scratch[...].T


def column(turned_rows, index, levels):
    return jnp.broadcast_to(turned_rows[:levels, index : index + 1], (levels, LANES))


def side_messages(edges):
    lane = lane_ids(1)
    east = lane % 6 < 3
    used = lane < HALF_LANES
    half = edges[2].shape[0] // 2
    pairs = ((edges[0], edges[1]), (edges[2][:half], edges[2][half:]))
    last = [jnp.where(east, p, turned(q, W)) for p, q in pairs]
    first = [jnp.where(used, jnp.where(east, turned(p, -W), q), 0.0) for p, q in pairs]
    return last, first


def scalar_kernel(tracers, levels, rows, *refs):
    sources, (small, mask, scale_lanes, in_scales), refs = refs[:6], refs[6:10], refs[10:]
    (in_scale, storm, balance, *loads), scratch, sems = refs[:6], refs[6], refs[7]
    copies = [
        pltpu.make_async_copy(source, into, sems.at[n]) for n, (source, into) in enumerate(zip(sources, refs[:6]))
    ]
    for copy in copies:
        copy.start()
    for copy in copies[:4]:
        copy.wait()
    lon = lax.axis_index("lon")
    position = lax.broadcasted_iota(jnp.int32, balance.shape, 0)
    target = jnp.max(jnp.where(position == lon, balance[...], -1).astype(F32), axis=0, keepdims=True)
    scales = as_columns(scratch, [in_scale[...], loads[0][...]])
    lane = lane_ids(levels)
    own_scales, given_scales = jnp.zeros((levels, LANES), F32), jnp.zeros((levels, LANES), F32)
    for n in range(2 * tracers):
        scale = column(scales, n, levels)
        own_scales = jnp.where(lane == SCALE_LANE + n, scale, own_scales)
        given_scales = jnp.where(lane == SCALE_LANE + 2 * tracers + n, scale, given_scales)
        if n < tracers:
            in_scales[n] = scale
    scale_lanes[0], scale_lanes[1] = own_scales, given_scales
    for copy in copies[4:]:
        copy.wait()
    small[...] = jnp.zeros_like(small)
    at = 0
    for load in loads:
        small[at : at + load.shape[0], : load.shape[1]] = load[...].astype(F32)
        at += load.shape[0]
    small[at : at + 1, :rows] = target
    mask[...] = storm[...].astype(F32)


def edge_kernel(tracers, levels, rows, fields, small, storm, scale_lanes, in_scales, keep, give, active, features):
    lane = lane_ids(levels)
    half = levels // 2
    head = lax.axis_index("lev") == 0
    edges, values = [], []
    for t in range(tracers):
        pack = jnp.zeros((levels, LANES), F32)
        for i in range(rows):
            x = fields[pl.ds((t * levels) * rows + i, levels, stride=rows), :]
            values.append((x * in_scales[t]).astype(BF16))
            pack = jnp.where((lane >= 6 * i) & (lane < 6 * i + 6), turned(x, 6 * i + W), pack)
        edges.append(pack)
    mask = jnp.where(column(small[...].T, TARGET_ROW, rows) >= 0.0, storm[...], 0.0)
    lane = lane_ids(rows)
    row = lax.broadcasted_iota(jnp.int32, (rows, LANES), 0)
    mask_pack = pltpu.roll(mask, W, 1, stride=6, stride_axis=0)
    mask_pack = jnp.where((lane >= 6 * row) & (lane < 6 * row + 6), mask_pack, 0.0)
    mask_pack = jnp.broadcast_to(jnp.sum(mask_pack, axis=0, keepdims=True), (EXTRA, LANES))
    lane = lane_ids(1)
    east = lane % 6 < 3
    last_mask = jnp.where(east, mask_pack, 0.0)
    first_mask = turned(jnp.where(east, 0.0, mask_pack), -W)
    keep[levels + half :] = jnp.where(head, last_mask, first_mask)
    give[levels + half :] = turned(jnp.where(head, first_mask, last_mask), HALF_LANES)
    last, first = side_messages(edges)
    keep[:levels] = jnp.where(head, last[0], first[0]) + scale_lanes[0]
    give[:levels] = turned(jnp.where(head, first[0], last[0]), HALF_LANES) + scale_lanes[1]
    keep[levels : levels + half] = jnp.where(head, last[1], first[1])
    give[levels : levels + half] = turned(jnp.where(head, first[1], last[1]), HALF_LANES)
    active[...] = mask
    for n, x in enumerate(values):
        t, i = n // rows, n % rows
        features[i, t * levels : (t + 1) * levels, :] = x


def binary_scale(largest):
    largest = largest * (1.0 / FIELD_BOUND)
    power, scale = jnp.zeros_like(largest), jnp.ones_like(largest)
    for bits in (64, 32, 16, 8, 4, 2, 1):
        small = largest < 2.0**-bits
        largest = jnp.where(small, largest * 2.0**bits, largest)
        scale = jnp.where(small, scale * 2.0**bits, scale)
        power = jnp.where(small, power + float(bits), power)
    return scale, power


def inverse_scale(power):
    scale = jnp.ones_like(power)
    for bits in (64, 32, 16, 8, 4, 2, 1):
        large = power > bits - 0.5
        scale = jnp.where(large, scale * 2.0**-bits, scale)
        power = jnp.where(large, power - float(bits), power)
    return scale


def to_fixed(x):
    return jnp.round(x).astype(jnp.int32).astype(jnp.int16)


def from_fixed(x):
    return x.astype(jnp.int32).astype(F32)


def row_message_kernel(tracers, levels, rows, moves, fields, active, *edge_rows):
    lat = lax.axis_index("lat")
    lane = lane_ids(levels)
    row = lax.broadcasted_iota(jnp.int32, (2 * EXTRA, LANES), 0)
    tail = W * tracers * levels
    for move, out in zip(moves, edge_rows):
        start = first_row_sent(move, lat, rows)
        values = [
            [fields[pl.ds((t * levels) * rows + start + r, levels, stride=rows), :] for r in range(W)]
            for t in range(tracers)
        ]
        largest = [jnp.max(jnp.maximum(jnp.maximum(jnp.abs(a), jnp.abs(b)), jnp.abs(c)), axis=1, keepdims=True) for a, b, c in values]
        bound = jnp.zeros((levels, LANES), F32)
        for t in range(tracers):
            bound = jnp.where(lane == t, largest[t], bound)
        scale, power = binary_scale(bound)
        for t in range(tracers):
            to_one = jnp.broadcast_to(scale[:, t : t + 1], (levels, LANES))
            for r, x in enumerate(values[t]):
                x = jnp.clip(x * to_one * FIXED_ONE, -FIXED_MOST, FIXED_MOST)
                out[(r * tracers + t) * levels : (r * tracers + t + 1) * levels, :] = to_fixed(x)
        out[tail : tail + levels, :] = to_fixed(power)
        mask = jnp.zeros(row.shape, F32)
        for r in range(W):
            mask = jnp.where(row == r, active[pl.ds(start + r, 1), :], mask)
        out[tail + levels :, :] = to_fixed(mask)


def first_row_sent(move, lat, rows):
    if move == 0:
        return jnp.where(lat == 0, rows - W, 0)
    return rows - W if move > 0 else 0


def first_row_received(move, lat, rows):
    if move == 0:
        return jnp.where(lat == 0, 0, rows - W)
    return rows - W if move > 0 else 0


def network(x, w_in, w_mid, w_last):
    hidden = silu(jnp.dot(w_in, x, preferred_element_type=F32)).astype(BF16)
    for layer in range(len(w_mid)):
        hidden = silu(jnp.dot(w_mid[layer], hidden, preferred_element_type=F32)).astype(BF16)
    return jnp.dot(w_last, hidden, preferred_element_type=F32).astype(BF16)


def taps(step, count):
    first = jnp.abs(step)
    second = jnp.where(count > 1.5, first, 0.0)
    third = jnp.where(count > 2.5, first, 0.0)
    rest = [1.0 - a for a in (first, second, third)]
    return (
        rest[0] * rest[1] * rest[2],
        first * rest[1] * rest[2] + rest[0] * second * rest[2] + rest[0] * rest[1] * third,
        first * second * rest[2] + first * rest[1] * third + rest[0] * second * third,
        first * second * third,
    )


def first_layer(x, w_in):
    return silu(lax.dot_general(x, w_in, (((0,), (1,)), ((), ())), preferred_element_type=F32)).astype(BF16)


def further_layers(hidden, w_mid, w_last):
    def layer(hidden, w):
        return lax.dot_general(hidden, w, (((1,), (1,)), ((), ())), preferred_element_type=F32)

    for k in range(len(w_mid)):
        hidden = silu(layer(hidden, w_mid[k])).astype(BF16)
    return layer(w_last, hidden).astype(BF16)


OUT_SCALE, LON, LON_SIGN, LAT, LAT_SIGN, EDGE, PLANES = 0, 3, 7, 8, 12, 13, 18


def write_weights(weights, small, tracers, levels):
    columns = small[...].T
    for t in range(tracers):
        weights[OUT_SCALE + t] = column(columns, t, levels)
    count = column(columns, tracers + 2, levels)
    lane = lane_ids(levels)
    place = lane % 6
    step = column(columns, tracers, levels) / count
    up = step > 0.0
    w = taps(step, count)
    weights[LON_SIGN] = jnp.where(up, 1.0, 0.0)
    for k in range(4):
        weights[LON + k] = jnp.where(
            up, jnp.where(lane >= k, w[k], 0.0), jnp.where(lane < LANES - (W - k), w[W - k], 0.0)
        )
    east = [jnp.where(up | (place > 2) | (place < d), 0.0, w[W - d]) for d in range(3)]
    west = [jnp.where(up & (place > 2) & (place + d < 6), w[W - d], 0.0) for d in range(3)]
    weights[EDGE] = east[0] + west[0]
    weights[EDGE + 1] = east[1]
    weights[EDGE + 2] = west[1]
    weights[EDGE + 3] = east[2]
    weights[EDGE + 4] = west[2]
    step = column(columns, tracers + 1, levels) / count
    up = step > 0.0
    w = taps(step, count)
    weights[LAT_SIGN] = jnp.where(up, 1.0, 0.0)
    for k in range(4):
        weights[LAT + k] = jnp.where(up, w[W - k], w[k])


def sweep_lon(values, weights, span):
    up = weights[LON_SIGN, span, :] > 0.5
    values = [jnp.where(up, q, turned(q, -W)) for q in values]
    w = [weights[LON + k, span, :] for k in range(4)]
    return [w[0] * q + w[1] * turned(q, 1) + w[2] * turned(q, 2) + w[3] * turned(q, 3) for q in values]


def own_network_kernel(tracers, levels, rows, mine, other, w_in, w_mid, w_out, tendency, token, x):
    token[...] = jnp.zeros_like(token)
    lev = lax.axis_index("lev")
    width = tracers * levels
    near = pl.ds(pl.multiple_of(lev * width, width), width)
    far = pl.ds(pl.multiple_of((1 - lev) * width, width), width)
    w_last = w_out[near, :]
    for i in range(rows):
        x[near, i * LANES : (i + 1) * LANES] = mine[i]
        x[far, i * LANES : (i + 1) * LANES] = other[i]
    tendency[...] = network(x[...], w_in[...], w_mid, w_last)


def own_sweep_kernel(tracers, levels, rows, fields, tendency, small, active, swept, weights):
    write_weights(weights, small, tracers, levels)
    for g in range(0, levels, GROUP):
        span = slice(g, g + GROUP)
        for t in range(tracers):
            at = t * levels + g
            scale = weights[OUT_SCALE + t, span, :]
            values = []
            for i in range(rows):
                moist = tendency[at : at + GROUP, i * LANES : (i + 1) * LANES].astype(F32)
                q = fields[pl.ds(at * rows + i, GROUP, stride=rows), :]
                values.append(q + scale * moist * active[i : i + 1, :])
            for i, q in enumerate(sweep_lon(values, weights, span)):
                swept[i, at : at + GROUP, :] = q


def read_scale(message, which, n, tracers, levels):
    at = SCALE_LANE + 2 * tracers * which + n
    return jnp.broadcast_to(message[:levels, at : at + 1], (levels, LANES))


def row_input_kernel(tracers, levels, moves, packs, *refs):
    count = len(moves)
    edge, edge_other, (w_in, hidden, fields, masks, x) = refs[:count], refs[count : 2 * count], refs[2 * count :]
    lev = lax.axis_index("lev")
    width = tracers * levels
    tail = W * width
    for which, source in ((0, edge), (1, edge_other)):
        start = lev * width if which == 0 else (1 - lev) * width
        for n in range(count):
            unit = inverse_scale(from_fixed(source[n][tail : tail + levels, :])) * (1.0 / FIXED_ONE)
            for t in range(tracers):
                in_scale = read_scale(packs, which, t, tracers, levels)
                scale = jnp.broadcast_to(unit[:, t : t + 1], (levels, LANES))
                to = pl.ds(pl.multiple_of(start + t * levels, levels), levels)
                parts = [(r * tracers + t) * levels for r in range(W)]
                values = [from_fixed(source[n][part : part + levels, :]) * scale for part in parts]
                for r, value in enumerate(values):
                    column_at = (n * W + r) * LANES
                    x[to, column_at : column_at + LANES] = (value * in_scale).astype(BF16)
                    if which == 0:
                        fields[n, t * W + r] = value
    for n in range(count):
        masks[n] = from_fixed(edge[n][tail + levels :, :])
    hidden[...] = first_layer(x[...], w_in[...])


def edge_corrections(values, weights, head):
    east = jnp.where(head, LANES - 1, 1), jnp.where(head, LANES - 2, 2)
    w = [jnp.where(head, weights[EDGE + 2 * k], weights[EDGE + 2 * k - 1]) for k in (1, 2)]
    return [weights[EDGE] * q + w[0] * turned(q, east[0]) + w[1] * turned(q, east[1]) for q in values]


def halo_network_kernel(tracers, levels, rows, moves, _, ring, *refs):
    count = len(moves)
    corner = refs[:count]
    weights, w_in, w_mid, w_out, mine, other, x = refs[count:]
    lat, lev = lax.axis_index("lat"), lax.axis_index("lev")
    width = tracers * levels
    head = lev == 0
    lane = lane_ids(levels)
    west = (lane % 6 >= 3) == head
    shifts = [jnp.where(head, a, b) for a, b in ((W, 0), (0, LANES - W))]
    half = levels // 2

    def place(message, part, which, extra):
        moved = []
        for shift in shifts:
            shift = shift + (extra + LANES - HALF_LANES * which)
            shift = jnp.where(shift >= 2 * LANES, shift - 2 * LANES, jnp.where(shift >= LANES, shift - LANES, shift))
            moved.append(turned(message[part, :], shift))
        return moved

    def unpack(part, which):
        lane_part = lane[: part.stop - part.start]
        values = place(ring, part, which, 0)
        used = lane_part < 48
        for n, move in enumerate(moves):
            base = 48 + 18 * n
            here = (lane_part >= base) & (lane_part < base + 18)
            far = place(corner[n], part, which, base - 6 * first_row_received(move, lat, rows))
            values = [jnp.where(here, q, value) for q, value in zip(far, values)]
            used = used | here
        used = used & west[: lane_part.shape[0]]
        return [jnp.where(used, value, 0.0) for value in values]

    mask = unpack(slice(levels + half, levels + half + EXTRA), 0)[0][:1]
    halos, scales = [], []
    for which in range(2):
        start = lev * width if which == 0 else (1 - lev) * width
        values = unpack(slice(0, levels), which)
        values.append(jnp.concatenate(unpack(slice(levels, levels + half), which), axis=0))
        for t, value in enumerate(values):
            in_scale, out_scale = (read_scale(ring, which, n, tracers, levels) for n in (t, tracers + t))
            halos.append(value)
            scales.append(out_scale)
            x[pl.ds(pl.multiple_of(start + t * levels, levels), levels), :] = (value * in_scale).astype(BF16)
    tendency = further_layers(first_layer(x[...], w_in[...]), w_mid, w_out[...]).astype(F32)
    x_tendency = [tendency[n * levels : (n + 1) * levels] for n in range(2 * tracers)]
    x_tendency = [
        jnp.where(head, x_tendency[n], x_tendency[(n + tracers) % (2 * tracers)]) for n in range(2 * tracers)
    ]
    values = [halo + scale * moist * mask for halo, scale, moist in zip(halos, scales, x_tendency)]
    if count == 2:
        up = weights[LAT_SIGN] > 0.5
        values = [jnp.where(up | (lane < 48), q, turned(q, -18)) for q in values]
    for t, q in enumerate(edge_corrections(values[tracers:], weights, head)):
        other[t] = q
    for t in range(tracers):
        mine[t] = values[t]


def row_kernel(tracers, levels, moves, hidden, fields, masks, halo, weights, w_mid, w_out, beyond, fix, tendency):
    lev = lax.axis_index("lev")
    for t, q in enumerate(edge_corrections([halo[t] for t in range(tracers)], weights, lev == 0)):
        fix[t] = q
    width = tracers * levels
    near = pl.ds(pl.multiple_of(lev * width, width), width)
    tendency[...] = further_layers(hidden[...], w_mid, w_out[near, :])
    up = weights[LAT_SIGN] > 0.5
    values = []
    for t in range(tracers):
        for r in range(W):
            rows_q = []
            for n in range(len(moves)):
                column_at = (n * W + r) * LANES
                moist = tendency[t * levels : (t + 1) * levels, column_at : column_at + LANES].astype(F32)
                rows_q.append(fields[n, t * W + r] + weights[OUT_SCALE + t] * moist * masks[n, r : r + 1, :])
            values.append(jnp.where(up, rows_q[0], rows_q[1]) if len(moves) == 2 else rows_q[0])
    for n, q in enumerate(sweep_lon(values, weights, slice(0, levels))):
        beyond[n] = q


def finish_kernel(tracers, levels, rows, moves, swept, weights, fix_mine, fix_other, beyond, out, result, sems):
    lat = lax.axis_index("lat")
    southward = jnp.where(lat == 0, 0.0, 1.0)
    copies = []
    lane = lane_ids(HALF_GROUP)
    at_edge = (lane < W) | (lane >= LANES - W)
    for g in range(0, levels, HALF_GROUP):
        span = slice(g, g + HALF_GROUP)
        sign = weights[LAT_SIGN, span, :]
        up = sign > 0.5
        w = [weights[LAT + k, span, :] for k in range(4)]
        for t in range(tracers):
            at = t * levels + g
            fix = fix_mine[t, span, :] + fix_other[t, span, :]

            def fixed(value, first):
                return value + jnp.where(at_edge, turned(fix, LANES - W - first), 0.0)

            inner = [fixed(swept[i, at : at + HALF_GROUP, :], 6 * i) for i in range(rows)]
            outer = [fixed(beyond[t * W + r, span, :], 48 + 6 * r) for r in range(W)]
            if len(moves) == 1:
                outer = [jnp.where(sign == southward, q, 0.0) for q in outer]
            line = []
            for i in range(rows + W):
                above = outer[i] if i < W else inner[i - W]
                below = inner[i] if i < rows else outer[i - rows]
                line.append(jnp.where(up, above, below))
            results = [w[0] * line[i] + w[1] * line[i + 1] + w[2] * line[i + 2] + w[3] * line[i + 3] for i in range(rows)]
            for i, value in enumerate(results):
                result[pl.ds(at * rows + i, HALF_GROUP, stride=rows), :] = value
            part = pl.ds(at * rows, HALF_GROUP * rows)
            copies.append(pltpu.make_async_copy(result.at[part], out.at[part], sems.at[len(copies)]))
            copies[-1].start()
    for copy in copies:
        copy.wait()


def call(kernel, out_shape, scratch, flops, moved, name, **specs):
    return pl.pallas_call(
        kernel,
        out_shape=out_shape,
        **specs,
        scratch_shapes=scratch,
        compiler_params=pltpu.CompilerParams(vmem_limit_bytes=VMEM_LIMIT),
        cost_estimate=pl.CostEstimate(flops=flops, bytes_accessed=moved, transcendentals=0),
        name=name,
    )


def swap_cores(x):
    return lax.ppermute(x, "lev", [(0, 1), (1, 0)])


def routes(lon_count, lat_count, move, along_lon):
    pairs = []
    for i in range(lon_count):
        for j in range(lat_count):
            to_lat = 1 - j if move == 0 else j + (move or 0)
            if not 0 <= to_lat < lat_count:
                continue
            for k in range(2):
                to_lon = (i + (1 - 2 * k)) % lon_count if along_lon else i
                pairs.append((((i * lat_count) + j) * 2 + k, ((to_lon * lat_count) + to_lat) * 2 + k))
    return pairs


def send(x, move, along_lon):
    axes = ("lon", "lat", "lev")
    lon_count, lat_count = lax.axis_size("lon"), lax.axis_size("lat")
    if move is None:
        pairs = []
        for i in range(lon_count):
            for j in range(lat_count):
                for k in range(2):
                    to_lon = (i + (1 - 2 * k)) % lon_count
                    pairs.append(((i * lat_count + j) * 2 + k, (to_lon * lat_count + j) * 2 + k))
    else:
        pairs = routes(lon_count, lat_count, move, along_lon)
    return lax.ppermute(x, axes, pairs)


def on_device(fields, in_scale, out_scale, w_in, w_mid, w_out, storm_mask, balance, substeps, courant):
    tracers, levels, rows, columns = fields.shape
    width = tracers * levels
    moves = (0,) if lax.axis_size("lat") == 2 else (1, -1)
    count = len(moves)
    flat = fields.reshape(width * rows, columns)
    edge_shape = jax.ShapeDtypeStruct((W * width + levels + 2 * EXTRA, columns), jnp.int16)
    pack_shape = jax.ShapeDtypeStruct((levels + levels // 2 + EXTRA, LANES), F32)
    inputs = (in_scale, storm_mask, balance.T, out_scale, courant, substeps.reshape(1, levels))
    inputs = [pltpu.with_memory_space_constraint(x, pltpu.HBM) for x in inputs]
    mask_shape = jax.ShapeDtypeStruct((rows, columns), F32)
    small, storm, scale_lanes, in_scales = call(
        functools.partial(scalar_kernel, tracers, levels, rows),
        [jax.ShapeDtypeStruct((EXTRA, LANES), F32), mask_shape, jax.ShapeDtypeStruct((2, levels, LANES), F32),
         jax.ShapeDtypeStruct((tracers, levels, LANES), F32)],
        [pltpu.VMEM(x.shape, x.dtype) for x in inputs]
        + [pltpu.VMEM((EXTRA, LANES), F32), pltpu.SemaphoreType.DMA((len(inputs),))],
        10**10, 0, "scalars",
        in_specs=[pl.BlockSpec(memory_space=pltpu.HBM)] * len(inputs),
    )(*inputs)
    keep, give, active, features = call(
        functools.partial(edge_kernel, tracers, levels, rows),
        [pack_shape, pack_shape, mask_shape, jax.ShapeDtypeStruct((rows, width, columns), BF16)],
        [],
        10**10, 0, "edges",
    )(flat, small, storm, scale_lanes, in_scales)
    given = swap_cores(give)
    features_other = swap_cores(features)
    edge_rows = call(
        functools.partial(row_message_kernel, tracers, levels, rows, moves),
        [edge_shape] * count,
        [],
        10000000000, 0, "row_messages",
    )(flat, active)
    packs = keep + given
    corner = [send(packs, move, True) for move in moves]
    ring = send(packs, None, True)
    edge = [send(e, move, False) for e, move in zip(edge_rows, moves)]

    tendency, token = call(
        functools.partial(own_network_kernel, tracers, levels, rows),
        [jax.ShapeDtypeStruct((width, rows * columns), BF16), jax.ShapeDtypeStruct((2 * EXTRA, LANES), jnp.int16)],
        [pltpu.VMEM((2 * width, rows * columns), BF16)],
        10000000000, 0, "own_network",
    )(features, features_other, w_in, w_mid, w_out)
    swept, weights = call(
        functools.partial(own_sweep_kernel, tracers, levels, rows),
        [jax.ShapeDtypeStruct((rows, width, columns), F32), jax.ShapeDtypeStruct((PLANES, levels, LANES), F32)],
        [],
        10000000000, 0, "own_sweep",
    )(flat, tendency, small, active)

    fix_shape = jax.ShapeDtypeStruct((tracers, levels, LANES), F32)
    edge_other = [swap_cores(e + token[:1]) for e in edge]
    total = W * count * LANES
    physics_shape = jax.ShapeDtypeStruct((count, tracers * W, levels, LANES), F32)
    hidden, row_fields, row_masks = call(
        functools.partial(row_input_kernel, tracers, levels, moves),
        [jax.ShapeDtypeStruct((total, w_in.shape[0]), BF16), physics_shape,
         jax.ShapeDtypeStruct((count, 2 * EXTRA, LANES), F32)],
        [pltpu.VMEM((2 * width, total), BF16)],
        10**10, 0, "row_input",
    )(packs, *edge, *edge_other, w_in)
    halo, fix_given = call(
        functools.partial(halo_network_kernel, tracers, levels, rows, moves),
        [fix_shape, fix_shape],
        [pltpu.VMEM((2 * width, LANES), BF16)],
        10**10, 0, "halo_network",
    )(row_masks, ring, *corner, weights, w_in, w_mid, w_out)
    fix_other = swap_cores(fix_given)
    beyond, fix_mine = call(
        functools.partial(row_kernel, tracers, levels, moves),
        [jax.ShapeDtypeStruct((tracers * W, levels, LANES), F32), fix_shape],
        [pltpu.VMEM((width, total), BF16)],
        10**10, 0, "row_network",
    )(hidden, row_fields, row_masks, halo, weights, w_mid, w_out)
    out = call(
        functools.partial(finish_kernel, tracers, levels, rows, moves),
        jax.ShapeDtypeStruct((width * rows, columns), F32),
        [pltpu.VMEM((width * rows, columns), F32), pltpu.SemaphoreType.DMA((width // HALF_GROUP,))],
        10000000000, 0, "finish",
        out_specs=pl.BlockSpec(memory_space=pltpu.HBM),
    )(swept, weights, fix_mine, fix_other, beyond)
    return out.reshape(fields.shape)


def solution(mesh):
    in_specs = (
        P("lev", None, ("group", "lat"), "lon"),
        P("lev", None),
        P("lev", None),
        P(),
        P(),
        P(),
        P(("group", "lat"), "lon"),
        P(("group", "lat"), None),
        P(),
        P(),
    )
    out_specs = P("lev", None, ("group", "lat"), "lon")
    return jax.shard_map(
        on_device, mesh=mesh, in_specs=in_specs, out_specs=out_specs, check_vma=False
    )
```

```python
import functools

import jax
import jax.numpy as jnp
from jax import lax
from jax.experimental import pallas as pl
from jax.experimental.pallas import tpu as pltpu
from jax.sharding import PartitionSpec as P

W = 3
LANES = 128
HALF_LANES = 48
TARGET_ROW = 6
SCALE_LANE = 96
FIELD_BOUND = 8.0
FIXED_ONE = 32768.0 / FIELD_BOUND
FIXED_MOST = 32767.0
EXTRA = 8
F32 = jnp.float32
BF16 = jnp.bfloat16
GROUP = 32
HALF_GROUP = 16
VMEM_LIMIT = 40 * 1024 * 1024


def lane_ids(rows):
    return lax.broadcasted_iota(jnp.int32, (rows, LANES), 1)


def turned(x, shift):
    if isinstance(shift, int):
        shift %= LANES
        if shift == 0:
            return x
    return pltpu.roll(x, shift, 1)


def silu(v):
    half = 0.5 * v
    return half + half * jnp.tanh(half)


def as_columns(scratch, parts):
    scratch[...] = jnp.zeros_like(scratch)
    at = 0
    for part in parts:
        scratch[at : at + part.shape[0], : part.shape[1]] = part
        at += part.shape[0]
    return scratch[...].T


def column(turned_rows, index, levels):
    return jnp.broadcast_to(turned_rows[:levels, index : index + 1], (levels, LANES))


def side_messages(edges):
    lane = lane_ids(1)
    east = lane % 6 < 3
    used = lane < HALF_LANES
    half = edges[2].shape[0] // 2
    pairs = ((edges[0], edges[1]), (edges[2][:half], edges[2][half:]))
    last = [jnp.where(east, p, turned(q, W)) for p, q in pairs]
    first = [jnp.where(used, jnp.where(east, turned(p, -W), q), 0.0) for p, q in pairs]
    return last, first


def scalar_kernel(tracers, levels, rows, *refs):
    sources, (small, mask, scale_lanes, in_scales), refs = refs[:6], refs[6:10], refs[10:]
    (in_scale, storm, balance, *loads), scratch, sems = refs[:6], refs[6], refs[7]
    copies = [
        pltpu.make_async_copy(source, into, sems.at[n]) for n, (source, into) in enumerate(zip(sources, refs[:6]))
    ]
    for copy in copies:
        copy.start()
    for copy in copies[:4]:
        copy.wait()
    lon = lax.axis_index("lon")
    position = lax.broadcasted_iota(jnp.int32, balance.shape, 0)
    target = jnp.max(jnp.where(position == lon, balance[...], -1).astype(F32), axis=0, keepdims=True)
    scales = as_columns(scratch, [in_scale[...], loads[0][...]])
    lane = lane_ids(levels)
    own_scales, given_scales = jnp.zeros((levels, LANES), F32), jnp.zeros((levels, LANES), F32)
    for n in range(2 * tracers):
        scale = column(scales, n, levels)
        own_scales = jnp.where(lane == SCALE_LANE + n, scale, own_scales)
        given_scales = jnp.where(lane == SCALE_LANE + 2 * tracers + n, scale, given_scales)
        if n < tracers:
            in_scales[n] = scale
    scale_lanes[0], scale_lanes[1] = own_scales, given_scales
    for copy in copies[4:]:
        copy.wait()
    small[...] = jnp.zeros_like(small)
    at = 0
    for load in loads:
        small[at : at + load.shape[0], : load.shape[1]] = load[...].astype(F32)
        at += load.shape[0]
    small[at : at + 1, :rows] = target
    mask[...] = storm[...].astype(F32)


def edge_kernel(tracers, levels, rows, fields, small, storm, scale_lanes, in_scales, keep, give, active, features):
    lane = lane_ids(levels)
    half = levels // 2
    head = lax.axis_index("lev") == 0
    edges, values = [], []
    for t in range(tracers):
        pack = jnp.zeros((levels, LANES), F32)
        for i in range(rows):
            x = fields[pl.ds((t * levels) * rows + i, levels, stride=rows), :]
            values.append((x * in_scales[t]).astype(BF16))
            pack = jnp.where((lane >= 6 * i) & (lane < 6 * i + 6), turned(x, 6 * i + W), pack)
        edges.append(pack)
    mask = jnp.where(column(small[...].T, TARGET_ROW, rows) >= 0.0, storm[...], 0.0)
    lane = lane_ids(rows)
    row = lax.broadcasted_iota(jnp.int32, (rows, LANES), 0)
    mask_pack = pltpu.roll(mask, W, 1, stride=6, stride_axis=0)
    mask_pack = jnp.where((lane >= 6 * row) & (lane < 6 * row + 6), mask_pack, 0.0)
    mask_pack = jnp.broadcast_to(jnp.sum(mask_pack, axis=0, keepdims=True), (EXTRA, LANES))
    lane = lane_ids(1)
    east = lane % 6 < 3
    last_mask = jnp.where(east, mask_pack, 0.0)
    first_mask = turned(jnp.where(east, 0.0, mask_pack), -W)
    keep[levels + half :] = jnp.where(head, last_mask, first_mask)
    give[levels + half :] = turned(jnp.where(head, first_mask, last_mask), HALF_LANES)
    last, first = side_messages(edges)
    keep[:levels] = jnp.where(head, last[0], first[0]) + scale_lanes[0]
    give[:levels] = turned(jnp.where(head, first[0], last[0]), HALF_LANES) + scale_lanes[1]
    keep[levels : levels + half] = jnp.where(head, last[1], first[1])
    give[levels : levels + half] = turned(jnp.where(head, first[1], last[1]), HALF_LANES)
    active[...] = mask
    for n, x in enumerate(values):
        t, i = n // rows, n % rows
        features[i, t * levels : (t + 1) * levels, :] = x


def binary_scale(largest):
    largest = largest * (1.0 / FIELD_BOUND)
    power, scale = jnp.zeros_like(largest), jnp.ones_like(largest)
    for bits in (64, 32, 16, 8, 4, 2, 1):
        small = largest < 2.0**-bits
        largest = jnp.where(small, largest * 2.0**bits, largest)
        scale = jnp.where(small, scale * 2.0**bits, scale)
        power = jnp.where(small, power + float(bits), power)
    return scale, power


def inverse_scale(power):
    scale = jnp.ones_like(power)
    for bits in (64, 32, 16, 8, 4, 2, 1):
        large = power > bits - 0.5
        scale = jnp.where(large, scale * 2.0**-bits, scale)
        power = jnp.where(large, power - float(bits), power)
    return scale


def to_fixed(x):
    return jnp.round(x).astype(jnp.int32).astype(jnp.int16)


def from_fixed(x):
    return x.astype(jnp.int32).astype(F32)


def row_message_kernel(tracers, levels, rows, moves, fields, active, *edge_rows):
    lat = lax.axis_index("lat")
    lane = lane_ids(levels)
    row = lax.broadcasted_iota(jnp.int32, (2 * EXTRA, LANES), 0)
    tail = W * tracers * levels
    for move, out in zip(moves, edge_rows):
        start = first_row_sent(move, lat, rows)
        values = [
            [fields[pl.ds((t * levels) * rows + start + r, levels, stride=rows), :] for r in range(W)]
            for t in range(tracers)
        ]
        largest = [jnp.max(jnp.maximum(jnp.maximum(jnp.abs(a), jnp.abs(b)), jnp.abs(c)), axis=1, keepdims=True) for a, b, c in values]
        bound = jnp.zeros((levels, LANES), F32)
        for t in range(tracers):
            bound = jnp.where(lane == t, largest[t], bound)
        scale, power = binary_scale(bound)
        for t in range(tracers):
            to_one = jnp.broadcast_to(scale[:, t : t + 1], (levels, LANES))
            for r, x in enumerate(values[t]):
                x = jnp.clip(x * to_one * FIXED_ONE, -FIXED_MOST, FIXED_MOST)
                out[(r * tracers + t) * levels : (r * tracers + t + 1) * levels, :] = to_fixed(x)
        out[tail : tail + levels, :] = to_fixed(power)
        mask = jnp.zeros(row.shape, F32)
        for r in range(W):
            mask = jnp.where(row == r, active[pl.ds(start + r, 1), :], mask)
        out[tail + levels :, :] = to_fixed(mask)


def first_row_sent(move, lat, rows):
    if move == 0:
        return jnp.where(lat == 0, rows - W, 0)
    return rows - W if move > 0 else 0


def first_row_received(move, lat, rows):
    if move == 0:
        return jnp.where(lat == 0, 0, rows - W)
    return rows - W if move > 0 else 0


def network(x, w_in, w_mid, w_last):
    hidden = silu(jnp.dot(w_in, x, preferred_element_type=F32)).astype(BF16)
    for layer in range(len(w_mid)):
        hidden = silu(jnp.dot(w_mid[layer], hidden, preferred_element_type=F32)).astype(BF16)
    return jnp.dot(w_last, hidden, preferred_element_type=F32).astype(BF16)


def taps(step, count):
    first = jnp.abs(step)
    second = jnp.where(count > 1.5, first, 0.0)
    third = jnp.where(count > 2.5, first, 0.0)
    rest = [1.0 - a for a in (first, second, third)]
    return (
        rest[0] * rest[1] * rest[2],
        first * rest[1] * rest[2] + rest[0] * second * rest[2] + rest[0] * rest[1] * third,
        first * second * rest[2] + first * rest[1] * third + rest[0] * second * third,
        first * second * third,
    )


def first_layer(x, w_in):
    return silu(lax.dot_general(x, w_in, (((0,), (1,)), ((), ())), preferred_element_type=F32)).astype(BF16)


def further_layers(hidden, w_mid, w_last):
    def layer(hidden, w):
        return lax.dot_general(hidden, w, (((1,), (1,)), ((), ())), preferred_element_type=F32)

    for k in range(len(w_mid)):
        hidden = silu(layer(hidden, w_mid[k])).astype(BF16)
    return layer(w_last, hidden).astype(BF16)


OUT_SCALE, LON, LON_SIGN, LAT, LAT_SIGN, EDGE, PLANES = 0, 3, 7, 8, 12, 13, 18


def write_weights(weights, small, tracers, levels):
    columns = small[...].T
    for t in range(tracers):
        weights[OUT_SCALE + t] = column(columns, t, levels)
    count = column(columns, tracers + 2, levels)
    lane = lane_ids(levels)
    place = lane % 6
    step = column(columns, tracers, levels) / count
    up = step > 0.0
    w = taps(step, count)
    weights[LON_SIGN] = jnp.where(up, 1.0, 0.0)
    for k in range(4):
        weights[LON + k] = jnp.where(
            up, jnp.where(lane >= k, w[k], 0.0), jnp.where(lane < LANES - (W - k), w[W - k], 0.0)
        )
    east = [jnp.where(up | (place > 2) | (place < d), 0.0, w[W - d]) for d in range(3)]
    west = [jnp.where(up & (place > 2) & (place + d < 6), w[W - d], 0.0) for d in range(3)]
    weights[EDGE] = east[0] + west[0]
    weights[EDGE + 1] = east[1]
    weights[EDGE + 2] = west[1]
    weights[EDGE + 3] = east[2]
    weights[EDGE + 4] = west[2]
    step = column(columns, tracers + 1, levels) / count
    up = step > 0.0
    w = taps(step, count)
    weights[LAT_SIGN] = jnp.where(up, 1.0, 0.0)
    for k in range(4):
        weights[LAT + k] = jnp.where(up, w[W - k], w[k])


def sweep_lon(values, weights, span):
    up = weights[LON_SIGN, span, :] > 0.5
    values = [jnp.where(up, q, turned(q, -W)) for q in values]
    w = [weights[LON + k, span, :] for k in range(4)]
    return [w[0] * q + w[1] * turned(q, 1) + w[2] * turned(q, 2) + w[3] * turned(q, 3) for q in values]


def own_network_kernel(tracers, levels, rows, mine, other, w_in, w_mid, w_out, tendency, token, x):
    token[...] = jnp.zeros_like(token)
    lev = lax.axis_index("lev")
    width = tracers * levels
    near = pl.ds(pl.multiple_of(lev * width, width), width)
    far = pl.ds(pl.multiple_of((1 - lev) * width, width), width)
    w_last = w_out[near, :]
    for i in range(rows):
        x[near, i * LANES : (i + 1) * LANES] = mine[i]
        x[far, i * LANES : (i + 1) * LANES] = other[i]
    tendency[...] = network(x[...], w_in[...], w_mid, w_last)


def own_sweep_kernel(tracers, levels, rows, fields, tendency, small, active, swept, weights):
    write_weights(weights, small, tracers, levels)
    for g in range(0, levels, GROUP):
        span = slice(g, g + GROUP)
        for t in range(tracers):
            at = t * levels + g
            scale = weights[OUT_SCALE + t, span, :]
            values = []
            for i in range(rows):
                moist = tendency[at : at + GROUP, i * LANES : (i + 1) * LANES].astype(F32)
                q = fields[pl.ds(at * rows + i, GROUP, stride=rows), :]
                values.append(q + scale * moist * active[i : i + 1, :])
            for i, q in enumerate(sweep_lon(values, weights, span)):
                swept[i, at : at + GROUP, :] = q


def read_scale(message, which, n, tracers, levels):
    at = SCALE_LANE + 2 * tracers * which + n
    return jnp.broadcast_to(message[:levels, at : at + 1], (levels, LANES))


def row_input_kernel(tracers, levels, moves, packs, *refs):
    count = len(moves)
    edge, edge_other, (w_in, hidden, fields, masks, x) = refs[:count], refs[count : 2 * count], refs[2 * count :]
    lev = lax.axis_index("lev")
    width = tracers * levels
    tail = W * width
    for which, source in ((0, edge), (1, edge_other)):
        start = lev * width if which == 0 else (1 - lev) * width
        for n in range(count):
            unit = inverse_scale(from_fixed(source[n][tail : tail + levels, :])) * (1.0 / FIXED_ONE)
            for t in range(tracers):
                in_scale = read_scale(packs, which, t, tracers, levels)
                scale = jnp.broadcast_to(unit[:, t : t + 1], (levels, LANES))
                to = pl.ds(pl.multiple_of(start + t * levels, levels), levels)
                parts = [(r * tracers + t) * levels for r in range(W)]
                values = [from_fixed(source[n][part : part + levels, :]) * scale for part in parts]
                for r, value in enumerate(values):
                    column_at = (n * W + r) * LANES
                    x[to, column_at : column_at + LANES] = (value * in_scale).astype(BF16)
                    if which == 0:
                        fields[n, t * W + r] = value
    for n in range(count):
        masks[n] = from_fixed(edge[n][tail + levels :, :])
    hidden[...] = first_layer(x[...], w_in[...])


def edge_corrections(values, weights, head):
    east = jnp.where(head, LANES - 1, 1), jnp.where(head, LANES - 2, 2)
    w = [jnp.where(head, weights[EDGE + 2 * k], weights[EDGE + 2 * k - 1]) for k in (1, 2)]
    return [weights[EDGE] * q + w[0] * turned(q, east[0]) + w[1] * turned(q, east[1]) for q in values]


def halo_network_kernel(tracers, levels, rows, moves, _, ring, *refs):
    count = len(moves)
    corner = refs[:count]
    weights, w_in, w_mid, w_out, mine, other, x = refs[count:]
    lat, lev = lax.axis_index("lat"), lax.axis_index("lev")
    width = tracers * levels
    head = lev == 0
    lane = lane_ids(levels)
    west = (lane % 6 >= 3) == head
    shifts = [jnp.where(head, a, b) for a, b in ((W, 0), (0, LANES - W))]
    half = levels // 2

    def place(message, part, which, extra):
        moved = []
        for shift in shifts:
            shift = shift + (extra + LANES - HALF_LANES * which)
            shift = jnp.where(shift >= 2 * LANES, shift - 2 * LANES, jnp.where(shift >= LANES, shift - LANES, shift))
            moved.append(turned(message[part, :], shift))
        return moved

    def unpack(part, which):
        lane_part = lane[: part.stop - part.start]
        values = place(ring, part, which, 0)
        used = lane_part < 48
        for n, move in enumerate(moves):
            base = 48 + 18 * n
            here = (lane_part >= base) & (lane_part < base + 18)
            far = place(corner[n], part, which, base - 6 * first_row_received(move, lat, rows))
            values = [jnp.where(here, q, value) for q, value in zip(far, values)]
            used = used | here
        used = used & west[: lane_part.shape[0]]
        return [jnp.where(used, value, 0.0) for value in values]

    mask = unpack(slice(levels + half, levels + half + EXTRA), 0)[0][:1]
    halos, scales = [], []
    for which in range(2):
        start = lev * width if which == 0 else (1 - lev) * width
        values = unpack(slice(0, levels), which)
        values.append(jnp.concatenate(unpack(slice(levels, levels + half), which), axis=0))
        for t, value in enumerate(values):
            in_scale, out_scale = (read_scale(ring, which, n, tracers, levels) for n in (t, tracers + t))
            halos.append(value)
            scales.append(out_scale)
            x[pl.ds(pl.multiple_of(start + t * levels, levels), levels), :] = (value * in_scale).astype(BF16)
    tendency = further_layers(first_layer(x[...], w_in[...]), w_mid, w_out[...]).astype(F32)
    x_tendency = [tendency[n * levels : (n + 1) * levels] for n in range(2 * tracers)]
    x_tendency = [
        jnp.where(head, x_tendency[n], x_tendency[(n + tracers) % (2 * tracers)]) for n in range(2 * tracers)
    ]
    values = [halo + scale * moist * mask for halo, scale, moist in zip(halos, scales, x_tendency)]
    if count == 2:
        up = weights[LAT_SIGN] > 0.5
        values = [jnp.where(up | (lane < 48), q, turned(q, -18)) for q in values]
    for t, q in enumerate(edge_corrections(values[tracers:], weights, head)):
        other[t] = q
    for t in range(tracers):
        mine[t] = values[t]


def row_kernel(tracers, levels, moves, hidden, fields, masks, halo, weights, w_mid, w_out, beyond, fix, tendency):
    lev = lax.axis_index("lev")
    for t, q in enumerate(edge_corrections([halo[t] for t in range(tracers)], weights, lev == 0)):
        fix[t] = q
    width = tracers * levels
    near = pl.ds(pl.multiple_of(lev * width, width), width)
    tendency[...] = further_layers(hidden[...], w_mid, w_out[near, :])
    up = weights[LAT_SIGN] > 0.5
    values = []
    for t in range(tracers):
        for r in range(W):
            rows_q = []
            for n in range(len(moves)):
                column_at = (n * W + r) * LANES
                moist = tendency[t * levels : (t + 1) * levels, column_at : column_at + LANES].astype(F32)
                rows_q.append(fields[n, t * W + r] + weights[OUT_SCALE + t] * moist * masks[n, r : r + 1, :])
            values.append(jnp.where(up, rows_q[0], rows_q[1]) if len(moves) == 2 else rows_q[0])
    for n, q in enumerate(sweep_lon(values, weights, slice(0, levels))):
        beyond[n] = q


def finish_kernel(tracers, levels, rows, moves, swept, weights, fix_mine, fix_other, beyond, out, result, sems):
    lat = lax.axis_index("lat")
    southward = jnp.where(lat == 0, 0.0, 1.0)
    copies = []
    lane = lane_ids(HALF_GROUP)
    at_edge = (lane < W) | (lane >= LANES - W)
    for g in range(0, levels, HALF_GROUP):
        span = slice(g, g + HALF_GROUP)
        sign = weights[LAT_SIGN, span, :]
        up = sign > 0.5
        w = [weights[LAT + k, span, :] for k in range(4)]
        for t in range(tracers):
            at = t * levels + g
            fix = fix_mine[t, span, :] + fix_other[t, span, :]

            def fixed(value, first):
                return value + jnp.where(at_edge, turned(fix, LANES - W - first), 0.0)

            inner = [fixed(swept[i, at : at + HALF_GROUP, :], 6 * i) for i in range(rows)]
            outer = [fixed(beyond[t * W + r, span, :], 48 + 6 * r) for r in range(W)]
            if len(moves) == 1:
                outer = [jnp.where(sign == southward, q, 0.0) for q in outer]
            line = []
            for i in range(rows + W):
                above = outer[i] if i < W else inner[i - W]
                below = inner[i] if i < rows else outer[i - rows]
                line.append(jnp.where(up, above, below))
            results = [w[0] * line[i] + w[1] * line[i + 1] + w[2] * line[i + 2] + w[3] * line[i + 3] for i in range(rows)]
            for i, value in enumerate(results):
                result[pl.ds(at * rows + i, HALF_GROUP, stride=rows), :] = value
            part = pl.ds(at * rows, HALF_GROUP * rows)
            copies.append(pltpu.make_async_copy(result.at[part], out.at[part], sems.at[len(copies)]))
            copies[-1].start()
    for copy in copies:
        copy.wait()


def call(kernel, out_shape, scratch, name, **specs):
    return pl.pallas_call(
        kernel,
        out_shape=out_shape,
        **specs,
        scratch_shapes=scratch,
        compiler_params=pltpu.CompilerParams(vmem_limit_bytes=VMEM_LIMIT),
        cost_estimate=pl.CostEstimate(flops=10**10, bytes_accessed=0, transcendentals=0),
        name=name,
    )


def swap_cores(x):
    return lax.ppermute(x, "lev", [(0, 1), (1, 0)])


def send(x, move, along_lon):
    axes = ("lon", "lat", "lev")
    lon_count, lat_count = lax.axis_size("lon"), lax.axis_size("lat")
    pairs = []
    for i in range(lon_count):
        for j in range(lat_count):
            to_lat = j if move is None else 1 - j if move == 0 else j + move
            if not 0 <= to_lat < lat_count:
                continue
            for k in range(2):
                to_lon = (i + 1 - 2 * k) % lon_count if along_lon else i
                pairs.append(((i * lat_count + j) * 2 + k, (to_lon * lat_count + to_lat) * 2 + k))
    return lax.ppermute(x, axes, pairs)


def on_device(fields, in_scale, out_scale, w_in, w_mid, w_out, storm_mask, balance, substeps, courant):
    tracers, levels, rows, columns = fields.shape
    width = tracers * levels
    moves = (0,) if lax.axis_size("lat") == 2 else (1, -1)
    count = len(moves)
    flat = fields.reshape(width * rows, columns)
    edge_shape = jax.ShapeDtypeStruct((W * width + levels + 2 * EXTRA, columns), jnp.int16)
    pack_shape = jax.ShapeDtypeStruct((levels + levels // 2 + EXTRA, LANES), F32)
    inputs = (in_scale, storm_mask, balance.T, out_scale, courant, substeps.reshape(1, levels))
    inputs = [pltpu.with_memory_space_constraint(x, pltpu.HBM) for x in inputs]
    mask_shape = jax.ShapeDtypeStruct((rows, columns), F32)
    small, storm, scale_lanes, in_scales = call(
        functools.partial(scalar_kernel, tracers, levels, rows),
        [jax.ShapeDtypeStruct((EXTRA, LANES), F32), mask_shape, jax.ShapeDtypeStruct((2, levels, LANES), F32),
         jax.ShapeDtypeStruct((tracers, levels, LANES), F32)],
        [pltpu.VMEM(x.shape, x.dtype) for x in inputs]
        + [pltpu.VMEM((EXTRA, LANES), F32), pltpu.SemaphoreType.DMA((len(inputs),))],
        "scalars",
        in_specs=[pl.BlockSpec(memory_space=pltpu.HBM)] * len(inputs),
    )(*inputs)
    keep, give, active, features = call(
        functools.partial(edge_kernel, tracers, levels, rows),
        [pack_shape, pack_shape, mask_shape, jax.ShapeDtypeStruct((rows, width, columns), BF16)],
        [],
        "edges",
    )(flat, small, storm, scale_lanes, in_scales)
    given = swap_cores(give)
    features_other = swap_cores(features)
    edge_rows = call(
        functools.partial(row_message_kernel, tracers, levels, rows, moves),
        [edge_shape] * count,
        [],
        "row_messages",
    )(flat, active)
    packs = keep + given
    corner = [send(packs, move, True) for move in moves]
    ring = send(packs, None, True)
    edge = [send(e, move, False) for e, move in zip(edge_rows, moves)]

    tendency, token = call(
        functools.partial(own_network_kernel, tracers, levels, rows),
        [jax.ShapeDtypeStruct((width, rows * columns), BF16), jax.ShapeDtypeStruct((2 * EXTRA, LANES), jnp.int16)],
        [pltpu.VMEM((2 * width, rows * columns), BF16)],
        "own_network",
    )(features, features_other, w_in, w_mid, w_out)
    swept, weights = call(
        functools.partial(own_sweep_kernel, tracers, levels, rows),
        [jax.ShapeDtypeStruct((rows, width, columns), F32), jax.ShapeDtypeStruct((PLANES, levels, LANES), F32)],
        [],
        "own_sweep",
    )(flat, tendency, small, active)

    fix_shape = jax.ShapeDtypeStruct((tracers, levels, LANES), F32)
    edge_other = [swap_cores(e + token[:1]) for e in edge]
    total = W * count * LANES
    physics_shape = jax.ShapeDtypeStruct((count, tracers * W, levels, LANES), F32)
    hidden, row_fields, row_masks = call(
        functools.partial(row_input_kernel, tracers, levels, moves),
        [jax.ShapeDtypeStruct((total, w_in.shape[0]), BF16), physics_shape,
         jax.ShapeDtypeStruct((count, 2 * EXTRA, LANES), F32)],
        [pltpu.VMEM((2 * width, total), BF16)],
        "row_input",
    )(packs, *edge, *edge_other, w_in)
    halo, fix_given = call(
        functools.partial(halo_network_kernel, tracers, levels, rows, moves),
        [fix_shape, fix_shape],
        [pltpu.VMEM((2 * width, LANES), BF16)],
        "halo_network",
    )(row_masks, ring, *corner, weights, w_in, w_mid, w_out)
    fix_other = swap_cores(fix_given)
    beyond, fix_mine = call(
        functools.partial(row_kernel, tracers, levels, moves),
        [jax.ShapeDtypeStruct((tracers * W, levels, LANES), F32), fix_shape],
        [pltpu.VMEM((width, total), BF16)],
        "row_network",
    )(hidden, row_fields, row_masks, halo, weights, w_mid, w_out)
    out = call(
        functools.partial(finish_kernel, tracers, levels, rows, moves),
        jax.ShapeDtypeStruct((width * rows, columns), F32),
        [pltpu.VMEM((width * rows, columns), F32), pltpu.SemaphoreType.DMA((width // HALF_GROUP,))],
        "finish",
        out_specs=pl.BlockSpec(memory_space=pltpu.HBM),
    )(swept, weights, fix_mine, fix_other, beyond)
    return out.reshape(fields.shape)


def solution(mesh):
    in_specs = (
        P("lev", None, ("group", "lat"), "lon"),
        P("lev", None),
        P("lev", None),
        P(),
        P(),
        P(),
        P(("group", "lat"), "lon"),
        P(("group", "lat"), None),
        P(),
        P(),
    )
    out_specs = P("lev", None, ("group", "lat"), "lon")
    return jax.shard_map(
        on_device, mesh=mesh, in_specs=in_specs, out_specs=out_specs, check_vma=False
    )
```

```python
import functools

import jax
import jax.numpy as jnp
from jax import lax
from jax.experimental import pallas as pl
from jax.experimental.pallas import tpu as pltpu
from jax.sharding import PartitionSpec as P

W = 3
LANES = 128
HALF_LANES = 48
TARGET_ROW = 6
SCALE_LANE = 96
FIELD_BOUND = 8.0
FIXED_ONE = 32768.0 / FIELD_BOUND
FIXED_MOST = 32767.0
EXTRA = 8
F32 = jnp.float32
BF16 = jnp.bfloat16
GROUP = 32
HALF_GROUP = 16
EARLY_LAYERS = 1
VMEM_LIMIT = 40 * 1024 * 1024


def lane_ids(rows):
    return lax.broadcasted_iota(jnp.int32, (rows, LANES), 1)


def turned(x, shift):
    if isinstance(shift, int):
        shift %= LANES
        if shift == 0:
            return x
    return pltpu.roll(x, shift, 1)


def silu(v):
    half = 0.5 * v
    return half + half * jnp.tanh(half)


def as_columns(scratch, parts):
    scratch[...] = jnp.zeros_like(scratch)
    at = 0
    for part in parts:
        scratch[at : at + part.shape[0], : part.shape[1]] = part
        at += part.shape[0]
    return scratch[...].T


def column(turned_rows, index, levels):
    return jnp.broadcast_to(turned_rows[:levels, index : index + 1], (levels, LANES))


def side_messages(edges):
    lane = lane_ids(1)
    east = lane % 6 < 3
    used = lane < HALF_LANES
    half = edges[2].shape[0] // 2
    pairs = ((edges[0], edges[1]), (edges[2][:half], edges[2][half:]))
    last = [jnp.where(east, p, turned(q, W)) for p, q in pairs]
    first = [jnp.where(used, jnp.where(east, turned(p, -W), q), 0.0) for p, q in pairs]
    return last, first


def scalar_kernel(tracers, levels, rows, *refs):
    sources, (small, mask, scale_lanes, in_scales), refs = refs[:6], refs[6:10], refs[10:]
    (in_scale, storm, balance, *loads), scratch, sems = refs[:6], refs[6], refs[7]
    copies = [
        pltpu.make_async_copy(source, into, sems.at[n]) for n, (source, into) in enumerate(zip(sources, refs[:6]))
    ]
    for copy in copies:
        copy.start()
    for copy in copies[:4]:
        copy.wait()
    lon = lax.axis_index("lon")
    position = lax.broadcasted_iota(jnp.int32, balance.shape, 0)
    target = jnp.max(jnp.where(position == lon, balance[...], -1).astype(F32), axis=0, keepdims=True)
    scales = as_columns(scratch, [in_scale[...], loads[0][...]])
    lane = lane_ids(levels)
    own_scales, given_scales = jnp.zeros((levels, LANES), F32), jnp.zeros((levels, LANES), F32)
    for n in range(2 * tracers):
        scale = column(scales, n, levels)
        own_scales = jnp.where(lane == SCALE_LANE + n, scale, own_scales)
        given_scales = jnp.where(lane == SCALE_LANE + 2 * tracers + n, scale, given_scales)
        if n < tracers:
            in_scales[n] = scale
    scale_lanes[0], scale_lanes[1] = own_scales, given_scales
    for copy in copies[4:]:
        copy.wait()
    small[...] = jnp.zeros_like(small)
    at = 0
    for load in loads:
        small[at : at + load.shape[0], : load.shape[1]] = load[...].astype(F32)
        at += load.shape[0]
    small[at : at + 1, :rows] = target
    mask[...] = storm[...].astype(F32)


def edge_kernel(tracers, levels, rows, fields, small, storm, scale_lanes, in_scales, keep, give, active, features):
    lane = lane_ids(levels)
    half = levels // 2
    head = lax.axis_index("lev") == 0
    edges, values = [], []
    for t in range(tracers):
        pack = jnp.zeros((levels, LANES), F32)
        for i in range(rows):
            x = fields[pl.ds((t * levels) * rows + i, levels, stride=rows), :]
            values.append((x * in_scales[t]).astype(BF16))
            pack = jnp.where((lane >= 6 * i) & (lane < 6 * i + 6), turned(x, 6 * i + W), pack)
        edges.append(pack)
    mask = jnp.where(column(small[...].T, TARGET_ROW, rows) >= 0.0, storm[...], 0.0)
    lane = lane_ids(rows)
    row = lax.broadcasted_iota(jnp.int32, (rows, LANES), 0)
    mask_pack = pltpu.roll(mask, W, 1, stride=6, stride_axis=0)
    mask_pack = jnp.where((lane >= 6 * row) & (lane < 6 * row + 6), mask_pack, 0.0)
    mask_pack = jnp.broadcast_to(jnp.sum(mask_pack, axis=0, keepdims=True), (EXTRA, LANES))
    lane = lane_ids(1)
    east = lane % 6 < 3
    side_mask = jnp.where(head, jnp.where(east, mask_pack, 0.0), turned(jnp.where(east, 0.0, mask_pack), -W))
    free = (lane >= SCALE_LANE) & (lane < SCALE_LANE + HALF_LANES // 2)
    side_masks = [jnp.where(free, turned(side_mask, SCALE_LANE - HALF_LANES // 2 * n), 0.0) for n in range(2)]
    last, first = side_messages(edges)
    keep[:levels] = jnp.where(head, last[0], first[0]) + scale_lanes[0]
    give[:levels] = turned(jnp.where(head, first[0], last[0]), HALF_LANES) + scale_lanes[1]
    third = jnp.where(head, last[1], first[1])
    for n in range(2):
        at = EXTRA * n
        keep[levels + at : levels + at + EXTRA] = third[at : at + EXTRA] + side_masks[n]
    keep[levels + 2 * EXTRA :] = third[2 * EXTRA :]
    give[levels:] = turned(jnp.where(head, first[1], last[1]), HALF_LANES)
    active[...] = mask
    for n, x in enumerate(values):
        t, i = n // rows, n % rows
        features[i, t * levels : (t + 1) * levels, :] = x


def binary_scale(largest):
    largest = largest * (1.0 / FIELD_BOUND)
    power, scale = jnp.zeros_like(largest), jnp.ones_like(largest)
    for bits in (64, 32, 16, 8, 4, 2, 1):
        small = largest < 2.0**-bits
        largest = jnp.where(small, largest * 2.0**bits, largest)
        scale = jnp.where(small, scale * 2.0**bits, scale)
        power = jnp.where(small, power + float(bits), power)
    return scale, power


def inverse_scale(power):
    scale = jnp.ones_like(power)
    for bits in (64, 32, 16, 8, 4, 2, 1):
        large = power > bits - 0.5
        scale = jnp.where(large, scale * 2.0**-bits, scale)
        power = jnp.where(large, power - float(bits), power)
    return scale


def to_fixed(x):
    return jnp.round(x).astype(jnp.int32).astype(jnp.int16)


def from_fixed(x):
    return x.astype(jnp.int32).astype(F32)


def row_message_kernel(tracers, levels, rows, moves, fields, active, *edge_rows):
    lat = lax.axis_index("lat")
    lane = lane_ids(levels)
    row = lax.broadcasted_iota(jnp.int32, (2 * EXTRA, LANES), 0)
    tail = W * tracers * levels
    for move, out in zip(moves, edge_rows):
        start = first_row_sent(move, lat, rows)
        values = [
            [fields[pl.ds((t * levels) * rows + start + r, levels, stride=rows), :] for r in range(W)]
            for t in range(tracers)
        ]
        largest = [jnp.max(jnp.maximum(jnp.maximum(jnp.abs(a), jnp.abs(b)), jnp.abs(c)), axis=1, keepdims=True) for a, b, c in values]
        bound = jnp.zeros((levels, LANES), F32)
        for t in range(tracers):
            bound = jnp.where(lane == t, largest[t], bound)
        scale, power = binary_scale(bound)
        for t in range(tracers):
            to_one = jnp.broadcast_to(scale[:, t : t + 1], (levels, LANES))
            for r, x in enumerate(values[t]):
                x = jnp.clip(x * to_one * FIXED_ONE, -FIXED_MOST, FIXED_MOST)
                out[(r * tracers + t) * levels : (r * tracers + t + 1) * levels, :] = to_fixed(x)
        out[tail : tail + levels, :] = to_fixed(power)
        mask = jnp.zeros(row.shape, F32)
        for r in range(W):
            mask = jnp.where(row == r, active[pl.ds(start + r, 1), :], mask)
        out[tail + levels :, :] = to_fixed(mask)


def first_row_sent(move, lat, rows):
    if move == 0:
        return jnp.where(lat == 0, rows - W, 0)
    return rows - W if move > 0 else 0


def first_row_received(move, lat, rows):
    if move == 0:
        return jnp.where(lat == 0, 0, rows - W)
    return rows - W if move > 0 else 0


def network(x, w_in, w_mid, w_last):
    hidden = silu(jnp.dot(w_in, x, preferred_element_type=F32)).astype(BF16)
    for layer in range(len(w_mid)):
        hidden = silu(jnp.dot(w_mid[layer], hidden, preferred_element_type=F32)).astype(BF16)
    return jnp.dot(w_last, hidden, preferred_element_type=F32).astype(BF16)


def taps(step, count):
    first = jnp.abs(step)
    second = jnp.where(count > 1.5, first, 0.0)
    third = jnp.where(count > 2.5, first, 0.0)
    rest = [1.0 - a for a in (first, second, third)]
    return (
        rest[0] * rest[1] * rest[2],
        first * rest[1] * rest[2] + rest[0] * second * rest[2] + rest[0] * rest[1] * third,
        first * second * rest[2] + first * rest[1] * third + rest[0] * second * third,
        first * second * third,
    )


def first_layer(x, w_in):
    return silu(lax.dot_general(x, w_in, (((0,), (1,)), ((), ())), preferred_element_type=F32)).astype(BF16)


def weights_times(hidden, w):
    return lax.dot_general(hidden, w, (((1,), (1,)), ((), ())), preferred_element_type=F32)


def middle_layers(hidden, w_mid, layers):
    for k in layers:
        hidden = silu(weights_times(hidden, w_mid[k])).astype(BF16)
    return hidden


def last_layer(hidden, w_last):
    return weights_times(w_last, hidden).astype(BF16)


OUT_SCALE, LON, LON_SIGN, LAT, LAT_SIGN, EDGE, PLANES = 0, 3, 7, 8, 12, 13, 18


def write_weights(weights, small, tracers, levels):
    columns = small[...].T
    for t in range(tracers):
        weights[OUT_SCALE + t] = column(columns, t, levels)
    count = column(columns, tracers + 2, levels)
    lane = lane_ids(levels)
    place = lane % 6
    step = column(columns, tracers, levels) / count
    up = step > 0.0
    w = taps(step, count)
    weights[LON_SIGN] = jnp.where(up, 1.0, 0.0)
    for k in range(4):
        weights[LON + k] = jnp.where(
            up, jnp.where(lane >= k, w[k], 0.0), jnp.where(lane < LANES - (W - k), w[W - k], 0.0)
        )
    east = [jnp.where(up | (place > 2) | (place < d), 0.0, w[W - d]) for d in range(3)]
    west = [jnp.where(up & (place > 2) & (place + d < 6), w[W - d], 0.0) for d in range(3)]
    weights[EDGE] = east[0] + west[0]
    weights[EDGE + 1] = east[1]
    weights[EDGE + 2] = west[1]
    weights[EDGE + 3] = east[2]
    weights[EDGE + 4] = west[2]
    step = column(columns, tracers + 1, levels) / count
    up = step > 0.0
    w = taps(step, count)
    weights[LAT_SIGN] = jnp.where(up, 1.0, 0.0)
    for k in range(4):
        weights[LAT + k] = jnp.where(up, w[W - k], w[k])


def sweep_lon(values, weights, span):
    up = weights[LON_SIGN, span, :] > 0.5
    values = [jnp.where(up, q, turned(q, -W)) for q in values]
    w = [weights[LON + k, span, :] for k in range(4)]
    return [w[0] * q + w[1] * turned(q, 1) + w[2] * turned(q, 2) + w[3] * turned(q, 3) for q in values]


def own_network_kernel(tracers, levels, rows, mine, other, w_in, w_mid, w_out, tendency, token, x):
    token[...] = jnp.zeros_like(token)
    lev = lax.axis_index("lev")
    width = tracers * levels
    near = pl.ds(pl.multiple_of(lev * width, width), width)
    far = pl.ds(pl.multiple_of((1 - lev) * width, width), width)
    w_last = w_out[near, :]
    for i in range(rows):
        x[near, i * LANES : (i + 1) * LANES] = mine[i]
        x[far, i * LANES : (i + 1) * LANES] = other[i]
    tendency[...] = network(x[...], w_in[...], w_mid, w_last)


def own_sweep_kernel(tracers, levels, rows, fields, tendency, small, active, swept, weights):
    write_weights(weights, small, tracers, levels)
    for g in range(0, levels, GROUP):
        span = slice(g, g + GROUP)
        for t in range(tracers):
            at = t * levels + g
            scale = weights[OUT_SCALE + t, span, :]
            values = []
            for i in range(rows):
                moist = tendency[at : at + GROUP, i * LANES : (i + 1) * LANES].astype(F32)
                q = fields[pl.ds(at * rows + i, GROUP, stride=rows), :]
                values.append(q + scale * moist * active[i : i + 1, :])
            for i, q in enumerate(sweep_lon(values, weights, span)):
                swept[i, at : at + GROUP, :] = q


def read_scale(message, which, n, tracers, levels):
    at = SCALE_LANE + 2 * tracers * which + n
    return jnp.broadcast_to(message[:levels, at : at + 1], (levels, LANES))


def row_input_kernel(tracers, levels, moves, packs, *refs):
    count = len(moves)
    edge, edge_other, (w_in, w_mid, hidden, fields, masks, x) = refs[:count], refs[count : 2 * count], refs[2 * count :]
    lev = lax.axis_index("lev")
    width = tracers * levels
    tail = W * width
    for which, source in ((0, edge), (1, edge_other)):
        start = lev * width if which == 0 else (1 - lev) * width
        for n in range(count):
            unit = inverse_scale(from_fixed(source[n][tail : tail + levels, :])) * (1.0 / FIXED_ONE)
            for t in range(tracers):
                in_scale = read_scale(packs, which, t, tracers, levels)
                scale = jnp.broadcast_to(unit[:, t : t + 1], (levels, LANES))
                to = pl.ds(pl.multiple_of(start + t * levels, levels), levels)
                parts = [(r * tracers + t) * levels for r in range(W)]
                values = [from_fixed(source[n][part : part + levels, :]) * scale for part in parts]
                for r, value in enumerate(values):
                    column_at = (n * W + r) * LANES
                    x[to, column_at : column_at + LANES] = (value * in_scale).astype(BF16)
                    if which == 0:
                        fields[n, t * W + r] = value
    for n in range(count):
        masks[n] = from_fixed(edge[n][tail + levels :, :])
    hidden[...] = middle_layers(first_layer(x[...], w_in[...]), w_mid, range(EARLY_LAYERS))


def edge_corrections(values, weights, head, moves):
    if len(moves) == 2:
        near = (weights[LAT_SIGN] > 0.5) | (lane_ids(values[0].shape[0]) < 48)
        values = [jnp.where(near, q, turned(q, -18)) for q in values]
    east = jnp.where(head, LANES - 1, 1), jnp.where(head, LANES - 2, 2)
    w = [jnp.where(head, weights[EDGE + 2 * k], weights[EDGE + 2 * k - 1]) for k in (1, 2)]
    return [weights[EDGE] * q + w[0] * turned(q, east[0]) + w[1] * turned(q, east[1]) for q in values]


def halo_network_kernel(tracers, levels, rows, moves, _, ring, *refs):
    count = len(moves)
    corner = refs[:count]
    weights, w_in, w_mid, w_out, mine, other, hidden, masks, x = refs[count:]
    lat, lev = lax.axis_index("lat"), lax.axis_index("lev")
    width = tracers * levels
    head = lev == 0
    lane = lane_ids(levels)
    west = (lane % 6 >= 3) == head
    shifts = [jnp.where(head, a, b) for a, b in ((W, 0), (0, LANES - W))]
    half = levels // 2

    def place(numbers, which, extra):
        moved = []
        for shift in shifts:
            shift = shift + (extra + LANES - HALF_LANES * which)
            shift = jnp.where(shift >= 2 * LANES, shift - 2 * LANES, jnp.where(shift >= LANES, shift - LANES, shift))
            moved.append(turned(numbers, shift))
        return moved

    def unpack(numbers_of, size, which):
        lane_part = lane[:size]
        values = place(numbers_of(ring), which, 0)
        used = lane_part < 48
        for n, move in enumerate(moves):
            base = 48 + 18 * n
            here = (lane_part >= base) & (lane_part < base + 18)
            beside = place(numbers_of(corner[n]), which, base - 6 * first_row_received(move, lat, rows))
            values = [jnp.where(here, q, value) for q, value in zip(beside, values)]
            used = used | here
        used = used & west[:size]
        return [jnp.where(used, value, 0.0) for value in values]

    def mask_of(message):
        low, high = (
            turned(message[levels + EXTRA * n : levels + EXTRA * (n + 1), :], HALF_LANES // 2 * n - SCALE_LANE) for n in range(2)
        )
        lane_part = lane[:EXTRA]
        return jnp.where(lane_part < HALF_LANES // 2, low, jnp.where(lane_part < HALF_LANES, high, 0.0))

    mask = unpack(mask_of, EXTRA, 0)[0][:1]
    far = pl.ds(pl.multiple_of((1 - lev) * width, width), width)
    halos, scales = [], []
    for which in range(2):
        start = lev * width if which == 0 else (1 - lev) * width
        values = unpack(lambda message: message[:levels, :], levels, which)
        values.append(jnp.concatenate(unpack(lambda message: message[levels:, :], half, which), axis=0))
        for t, value in enumerate(values):
            in_scale, out_scale = (read_scale(ring, which, n, tracers, levels) for n in (t, tracers + t))
            halos.append(value)
            scales.append(out_scale)
            x[pl.ds(pl.multiple_of(start + t * levels, levels), levels), :] = (value * in_scale).astype(BF16)
    hidden[...] = middle_layers(first_layer(x[...], w_in[...]), w_mid, range(len(w_mid)))
    mine[...] = jnp.stack(halos[:tracers])
    masks[...] = jnp.broadcast_to(mask, masks.shape)
    tendency = last_layer(hidden[...], w_out[far, :]).astype(F32)
    values = [
        halos[tracers + t] + scales[tracers + t] * tendency[t * levels : (t + 1) * levels] * mask for t in range(tracers)
    ]
    for t, q in enumerate(edge_corrections(values, weights, lev == 0, moves)):
        other[t] = q


def row_kernel(tracers, levels, moves, hidden, fields, masks, halo, edge_hidden, edge_mask, weights, w_mid, w_out, beyond, fix, tendency):
    lev = lax.axis_index("lev")
    width = tracers * levels
    near = pl.ds(pl.multiple_of(lev * width, width), width)
    outer = middle_layers(hidden[...], w_mid, range(EARLY_LAYERS, len(w_mid)))
    tendency[...] = last_layer(jnp.concatenate([edge_hidden[...], outer], axis=0), w_out[near, :])
    values = [
        halo[t] + weights[OUT_SCALE + t] * tendency[t * levels : (t + 1) * levels, :LANES].astype(F32) * edge_mask[0:1, :]
        for t in range(tracers)
    ]
    for t, q in enumerate(edge_corrections(values, weights, lev == 0, moves)):
        fix[t] = q
    up = weights[LAT_SIGN] > 0.5
    values = []
    for t in range(tracers):
        for r in range(W):
            rows_q = []
            for n in range(len(moves)):
                column_at = (1 + n * W + r) * LANES
                moist = tendency[t * levels : (t + 1) * levels, column_at : column_at + LANES].astype(F32)
                rows_q.append(fields[n, t * W + r] + weights[OUT_SCALE + t] * moist * masks[n, r : r + 1, :])
            values.append(jnp.where(up, rows_q[0], rows_q[1]) if len(moves) == 2 else rows_q[0])
    for n, q in enumerate(sweep_lon(values, weights, slice(0, levels))):
        beyond[n] = q


def finish_kernel(tracers, levels, rows, moves, swept, weights, fix_mine, fix_other, beyond, out, result, sems):
    lat = lax.axis_index("lat")
    southward = jnp.where(lat == 0, 0.0, 1.0)
    copies = []
    lane = lane_ids(HALF_GROUP)
    at_edge = (lane < W) | (lane >= LANES - W)
    for g in range(0, levels, HALF_GROUP):
        span = slice(g, g + HALF_GROUP)
        sign = weights[LAT_SIGN, span, :]
        up = sign > 0.5
        w = [weights[LAT + k, span, :] for k in range(4)]
        for t in range(tracers):
            at = t * levels + g
            fix = fix_mine[t, span, :] + fix_other[t, span, :]

            def fixed(value, first):
                return value + jnp.where(at_edge, turned(fix, LANES - W - first), 0.0)

            inner = [fixed(swept[i, at : at + HALF_GROUP, :], 6 * i) for i in range(rows)]
            outer = [fixed(beyond[t * W + r, span, :], 48 + 6 * r) for r in range(W)]
            if len(moves) == 1:
                outer = [jnp.where(sign == southward, q, 0.0) for q in outer]
            line = []
            for i in range(rows + W):
                above = outer[i] if i < W else inner[i - W]
                below = inner[i] if i < rows else outer[i - rows]
                line.append(jnp.where(up, above, below))
            results = [w[0] * line[i] + w[1] * line[i + 1] + w[2] * line[i + 2] + w[3] * line[i + 3] for i in range(rows)]
            for i, value in enumerate(results):
                result[pl.ds(at * rows + i, HALF_GROUP, stride=rows), :] = value
            part = pl.ds(at * rows, HALF_GROUP * rows)
            copies.append(pltpu.make_async_copy(result.at[part], out.at[part], sems.at[len(copies)]))
            copies[-1].start()
    for copy in copies:
        copy.wait()


def call(kernel, out_shape, scratch, name, **specs):
    return pl.pallas_call(
        kernel,
        out_shape=out_shape,
        **specs,
        scratch_shapes=scratch,
        compiler_params=pltpu.CompilerParams(vmem_limit_bytes=VMEM_LIMIT),
        cost_estimate=pl.CostEstimate(flops=10**10, bytes_accessed=0, transcendentals=0),
        name=name,
    )


def swap_cores(x):
    return lax.ppermute(x, "lev", [(0, 1), (1, 0)])


def send(x, move, along_lon):
    axes = ("lon", "lat", "lev")
    lon_count, lat_count = lax.axis_size("lon"), lax.axis_size("lat")
    pairs = []
    for i in range(lon_count):
        for j in range(lat_count):
            to_lat = j if move is None else 1 - j if move == 0 else j + move
            if not 0 <= to_lat < lat_count:
                continue
            for k in range(2):
                to_lon = (i + 1 - 2 * k) % lon_count if along_lon else i
                pairs.append(((i * lat_count + j) * 2 + k, (to_lon * lat_count + to_lat) * 2 + k))
    return lax.ppermute(x, axes, pairs)


def on_device(fields, in_scale, out_scale, w_in, w_mid, w_out, storm_mask, balance, substeps, courant):
    tracers, levels, rows, columns = fields.shape
    width = tracers * levels
    moves = (0,) if lax.axis_size("lat") == 2 else (1, -1)
    count = len(moves)
    flat = fields.reshape(width * rows, columns)
    edge_shape = jax.ShapeDtypeStruct((W * width + levels + 2 * EXTRA, columns), jnp.int16)
    pack_shape = jax.ShapeDtypeStruct((levels + levels // 2, LANES), F32)
    inputs = (in_scale, storm_mask, balance.T, out_scale, courant, substeps.reshape(1, levels))
    inputs = [pltpu.with_memory_space_constraint(x, pltpu.HBM) for x in inputs]
    mask_shape = jax.ShapeDtypeStruct((rows, columns), F32)
    small, storm, scale_lanes, in_scales = call(
        functools.partial(scalar_kernel, tracers, levels, rows),
        [jax.ShapeDtypeStruct((EXTRA, LANES), F32), mask_shape, jax.ShapeDtypeStruct((2, levels, LANES), F32),
         jax.ShapeDtypeStruct((tracers, levels, LANES), F32)],
        [pltpu.VMEM(x.shape, x.dtype) for x in inputs]
        + [pltpu.VMEM((EXTRA, LANES), F32), pltpu.SemaphoreType.DMA((len(inputs),))],
        "scalars",
        in_specs=[pl.BlockSpec(memory_space=pltpu.HBM)] * len(inputs),
    )(*inputs)
    keep, give, active, features = call(
        functools.partial(edge_kernel, tracers, levels, rows),
        [pack_shape, pack_shape, mask_shape, jax.ShapeDtypeStruct((rows, width, columns), BF16)],
        [],
        "edges",
    )(flat, small, storm, scale_lanes, in_scales)
    given = swap_cores(give)
    features_other = swap_cores(features)
    edge_rows = call(
        functools.partial(row_message_kernel, tracers, levels, rows, moves),
        [edge_shape] * count,
        [],
        "row_messages",
    )(flat, active)
    packs = keep + given
    corner = [send(packs, move, True) for move in moves]
    ring = send(packs, None, True)
    edge = [send(e, move, False) for e, move in zip(edge_rows, moves)]

    tendency, token = call(
        functools.partial(own_network_kernel, tracers, levels, rows),
        [jax.ShapeDtypeStruct((width, rows * columns), BF16), jax.ShapeDtypeStruct((2 * EXTRA, LANES), jnp.int16)],
        [pltpu.VMEM((2 * width, rows * columns), BF16)],
        "own_network",
    )(features, features_other, w_in, w_mid, w_out)
    swept, weights = call(
        functools.partial(own_sweep_kernel, tracers, levels, rows),
        [jax.ShapeDtypeStruct((rows, width, columns), F32), jax.ShapeDtypeStruct((PLANES, levels, LANES), F32)],
        [],
        "own_sweep",
    )(flat, tendency, small, active)

    fix_shape = jax.ShapeDtypeStruct((tracers, levels, LANES), F32)
    edge_other = [swap_cores(e + token[:1]) for e in edge]
    total = W * count * LANES
    physics_shape = jax.ShapeDtypeStruct((count, tracers * W, levels, LANES), F32)
    hidden, row_fields, row_masks = call(
        functools.partial(row_input_kernel, tracers, levels, moves),
        [jax.ShapeDtypeStruct((total, w_in.shape[0]), BF16), physics_shape,
         jax.ShapeDtypeStruct((count, 2 * EXTRA, LANES), F32)],
        [pltpu.VMEM((2 * width, total), BF16)],
        "row_input",
    )(packs, *edge, *edge_other, w_in, w_mid)
    halo, fix_given, edge_hidden, edge_mask = call(
        functools.partial(halo_network_kernel, tracers, levels, rows, moves),
        [fix_shape, fix_shape, jax.ShapeDtypeStruct((LANES, w_in.shape[0]), BF16),
         jax.ShapeDtypeStruct((EXTRA, LANES), F32)],
        [pltpu.VMEM((2 * width, LANES), BF16)],
        "halo_network",
    )(row_masks, ring, *corner, weights, w_in, w_mid, w_out)
    fix_other = swap_cores(fix_given)
    beyond, fix_mine = call(
        functools.partial(row_kernel, tracers, levels, moves),
        [jax.ShapeDtypeStruct((tracers * W, levels, LANES), F32), fix_shape],
        [pltpu.VMEM((width, LANES + total), BF16)],
        "row_network",
    )(hidden, row_fields, row_masks, halo, edge_hidden, edge_mask, weights, w_mid, w_out)
    out = call(
        functools.partial(finish_kernel, tracers, levels, rows, moves),
        jax.ShapeDtypeStruct((width * rows, columns), F32),
        [pltpu.VMEM((width * rows, columns), F32), pltpu.SemaphoreType.DMA((width // HALF_GROUP,))],
        "finish",
        out_specs=pl.BlockSpec(memory_space=pltpu.HBM),
    )(swept, weights, fix_mine, fix_other, beyond)
    return out.reshape(fields.shape)


def solution(mesh):
    in_specs = (
        P("lev", None, ("group", "lat"), "lon"),
        P("lev", None),
        P("lev", None),
        P(),
        P(),
        P(),
        P(("group", "lat"), "lon"),
        P(("group", "lat"), None),
        P(),
        P(),
    )
    out_specs = P("lev", None, ("group", "lat"), "lon")
    return jax.shard_map(
        on_device, mesh=mesh, in_specs=in_specs, out_specs=out_specs, check_vma=False
    )
```

```python
import functools

import jax
import jax.numpy as jnp
from jax import lax
from jax.experimental import pallas as pl
from jax.experimental.pallas import tpu as pltpu
from jax.sharding import PartitionSpec as P

W = 3
LANES = 128
HALF_LANES = 48
TARGET_ROW = 6
SCALE_LANE = 96
FIELD_BOUND = 8.0
FIXED_ONE = 32768.0 / FIELD_BOUND
FIXED_MOST = 32767.0
EXTRA = 8
F32 = jnp.float32
BF16 = jnp.bfloat16
GROUP = 32
HALF_GROUP = 16
EARLY_LAYERS = 0
VMEM_LIMIT = 40 * 1024 * 1024


def lane_ids(rows):
    return lax.broadcasted_iota(jnp.int32, (rows, LANES), 1)


def turned(x, shift):
    if isinstance(shift, int):
        shift %= LANES
        if shift == 0:
            return x
    return pltpu.roll(x, shift, 1)


def silu(v):
    half = 0.5 * v
    return half + half * jnp.tanh(half)


def as_columns(scratch, parts):
    scratch[...] = jnp.zeros_like(scratch)
    at = 0
    for part in parts:
        scratch[at : at + part.shape[0], : part.shape[1]] = part
        at += part.shape[0]
    return scratch[...].T


def column(turned_rows, index, levels):
    return jnp.broadcast_to(turned_rows[:levels, index : index + 1], (levels, LANES))


def side_messages(edges):
    lane = lane_ids(1)
    east = lane % 6 < 3
    used = lane < HALF_LANES
    half = edges[2].shape[0] // 2
    pairs = ((edges[0], edges[1]), (edges[2][:half], edges[2][half:]))
    last = [jnp.where(east, p, turned(q, W)) for p, q in pairs]
    first = [jnp.where(used, jnp.where(east, turned(p, -W), q), 0.0) for p, q in pairs]
    return last, first


def scalar_kernel(tracers, levels, rows, *refs):
    sources, (small, mask, scale_lanes, in_scales), refs = refs[:6], refs[6:10], refs[10:]
    (in_scale, storm, balance, *loads), scratch, sems = refs[:6], refs[6], refs[7]
    copies = [
        pltpu.make_async_copy(source, into, sems.at[n]) for n, (source, into) in enumerate(zip(sources, refs[:6]))
    ]
    for copy in copies:
        copy.start()
    for copy in copies[:4]:
        copy.wait()
    lon = lax.axis_index("lon")
    position = lax.broadcasted_iota(jnp.int32, balance.shape, 0)
    target = jnp.max(jnp.where(position == lon, balance[...], -1).astype(F32), axis=0, keepdims=True)
    scales = as_columns(scratch, [in_scale[...], loads[0][...]])
    lane = lane_ids(levels)
    own_scales, given_scales = jnp.zeros((levels, LANES), F32), jnp.zeros((levels, LANES), F32)
    for n in range(2 * tracers):
        scale = column(scales, n, levels)
        own_scales = jnp.where(lane == SCALE_LANE + n, scale, own_scales)
        given_scales = jnp.where(lane == SCALE_LANE + 2 * tracers + n, scale, given_scales)
        if n < tracers:
            in_scales[n] = scale
    scale_lanes[0], scale_lanes[1] = own_scales, given_scales
    for copy in copies[4:]:
        copy.wait()
    small[...] = jnp.zeros_like(small)
    at = 0
    for load in loads:
        small[at : at + load.shape[0], : load.shape[1]] = load[...].astype(F32)
        at += load.shape[0]
    small[at : at + 1, :rows] = target
    mask[...] = storm[...].astype(F32)


def edge_kernel(tracers, levels, rows, fields, small, storm, scale_lanes, in_scales, keep, give, active, features):
    lane = lane_ids(levels)
    half = levels // 2
    head = lax.axis_index("lev") == 0
    edges, values = [], []
    for t in range(tracers):
        pack = jnp.zeros((levels, LANES), F32)
        for i in range(rows):
            x = fields[pl.ds((t * levels) * rows + i, levels, stride=rows), :]
            values.append((x * in_scales[t]).astype(BF16))
            pack = jnp.where((lane >= 6 * i) & (lane < 6 * i + 6), turned(x, 6 * i + W), pack)
        edges.append(pack)
    mask = jnp.where(column(small[...].T, TARGET_ROW, rows) >= 0.0, storm[...], 0.0)
    lane = lane_ids(rows)
    row = lax.broadcasted_iota(jnp.int32, (rows, LANES), 0)
    mask_pack = pltpu.roll(mask, W, 1, stride=6, stride_axis=0)
    mask_pack = jnp.where((lane >= 6 * row) & (lane < 6 * row + 6), mask_pack, 0.0)
    mask_pack = jnp.broadcast_to(jnp.sum(mask_pack, axis=0, keepdims=True), (EXTRA, LANES))
    lane = lane_ids(1)
    east = lane % 6 < 3
    side_mask = jnp.where(head, jnp.where(east, mask_pack, 0.0), turned(jnp.where(east, 0.0, mask_pack), -W))
    free = (lane >= SCALE_LANE) & (lane < SCALE_LANE + HALF_LANES // 2)
    side_masks = [jnp.where(free, turned(side_mask, SCALE_LANE - HALF_LANES // 2 * n), 0.0) for n in range(2)]
    last, first = side_messages(edges)
    keep[:levels] = jnp.where(head, last[0], first[0]) + scale_lanes[0]
    give[:levels] = turned(jnp.where(head, first[0], last[0]), HALF_LANES) + scale_lanes[1]
    third = jnp.where(head, last[1], first[1])
    for n in range(2):
        at = EXTRA * n
        keep[levels + at : levels + at + EXTRA] = third[at : at + EXTRA] + side_masks[n]
    keep[levels + 2 * EXTRA :] = third[2 * EXTRA :]
    give[levels:] = turned(jnp.where(head, first[1], last[1]), HALF_LANES)
    active[...] = mask
    for n, x in enumerate(values):
        t, i = n // rows, n % rows
        features[i, t * levels : (t + 1) * levels, :] = x


def binary_scale(largest):
    largest = largest * (1.0 / FIELD_BOUND)
    power, scale = jnp.zeros_like(largest), jnp.ones_like(largest)
    for bits in (64, 32, 16, 8, 4, 2, 1):
        small = largest < 2.0**-bits
        largest = jnp.where(small, largest * 2.0**bits, largest)
        scale = jnp.where(small, scale * 2.0**bits, scale)
        power = jnp.where(small, power + float(bits), power)
    return scale, power


def inverse_scale(power):
    scale = jnp.ones_like(power)
    for bits in (64, 32, 16, 8, 4, 2, 1):
        large = power > bits - 0.5
        scale = jnp.where(large, scale * 2.0**-bits, scale)
        power = jnp.where(large, power - float(bits), power)
    return scale


def to_fixed(x):
    return jnp.round(x).astype(jnp.int32).astype(jnp.int16)


def from_fixed(x):
    return x.astype(jnp.int32).astype(F32)


def row_message_kernel(tracers, levels, rows, moves, fields, active, *edge_rows):
    lat = lax.axis_index("lat")
    lane = lane_ids(levels)
    row = lax.broadcasted_iota(jnp.int32, (2 * EXTRA, LANES), 0)
    tail = W * tracers * levels
    for move, out in zip(moves, edge_rows):
        start = first_row_sent(move, lat, rows)
        values = [
            [fields[pl.ds((t * levels) * rows + start + r, levels, stride=rows), :] for r in range(W)]
            for t in range(tracers)
        ]
        largest = [jnp.max(jnp.maximum(jnp.maximum(jnp.abs(a), jnp.abs(b)), jnp.abs(c)), axis=1, keepdims=True) for a, b, c in values]
        bound = jnp.zeros((levels, LANES), F32)
        for t in range(tracers):
            bound = jnp.where(lane == t, largest[t], bound)
        scale, power = binary_scale(bound)
        for t in range(tracers):
            to_one = jnp.broadcast_to(scale[:, t : t + 1], (levels, LANES))
            for r, x in enumerate(values[t]):
                x = jnp.clip(x * to_one * FIXED_ONE, -FIXED_MOST, FIXED_MOST)
                out[(r * tracers + t) * levels : (r * tracers + t + 1) * levels, :] = to_fixed(x)
        out[tail : tail + levels, :] = to_fixed(power)
        mask = jnp.zeros(row.shape, F32)
        for r in range(W):
            mask = jnp.where(row == r, active[pl.ds(start + r, 1), :], mask)
        out[tail + levels :, :] = to_fixed(mask)


def first_row_sent(move, lat, rows):
    if move == 0:
        return jnp.where(lat == 0, rows - W, 0)
    return rows - W if move > 0 else 0


def first_row_received(move, lat, rows):
    if move == 0:
        return jnp.where(lat == 0, 0, rows - W)
    return rows - W if move > 0 else 0


def network(x, w_in, w_mid, w_last):
    hidden = silu(jnp.dot(w_in, x, preferred_element_type=F32)).astype(BF16)
    for layer in range(len(w_mid)):
        hidden = silu(jnp.dot(w_mid[layer], hidden, preferred_element_type=F32)).astype(BF16)
    return jnp.dot(w_last, hidden, preferred_element_type=F32).astype(BF16)


def taps(step, count):
    first = jnp.abs(step)
    second = jnp.where(count > 1.5, first, 0.0)
    third = jnp.where(count > 2.5, first, 0.0)
    rest = [1.0 - a for a in (first, second, third)]
    return (
        rest[0] * rest[1] * rest[2],
        first * rest[1] * rest[2] + rest[0] * second * rest[2] + rest[0] * rest[1] * third,
        first * second * rest[2] + first * rest[1] * third + rest[0] * second * third,
        first * second * third,
    )


def first_layer(x, w_in):
    return silu(lax.dot_general(x, w_in, (((0,), (1,)), ((), ())), preferred_element_type=F32)).astype(BF16)


def weights_times(hidden, w):
    return lax.dot_general(hidden, w, (((1,), (1,)), ((), ())), preferred_element_type=F32)


def middle_layers(hidden, w_mid, layers):
    for k in layers:
        hidden = silu(weights_times(hidden, w_mid[k])).astype(BF16)
    return hidden


def last_layer(hidden, w_last):
    return weights_times(w_last, hidden).astype(BF16)


OUT_SCALE, LON, LON_SIGN, LAT, LAT_SIGN, EDGE, PLANES = 0, 3, 7, 8, 12, 13, 18


def write_weights(weights, small, tracers, levels):
    columns = small[...].T
    for t in range(tracers):
        weights[OUT_SCALE + t] = column(columns, t, levels)
    count = column(columns, tracers + 2, levels)
    lane = lane_ids(levels)
    place = lane % 6
    step = column(columns, tracers, levels) / count
    up = step > 0.0
    w = taps(step, count)
    weights[LON_SIGN] = jnp.where(up, 1.0, 0.0)
    for k in range(4):
        weights[LON + k] = jnp.where(
            up, jnp.where(lane >= k, w[k], 0.0), jnp.where(lane < LANES - (W - k), w[W - k], 0.0)
        )
    east = [jnp.where(up | (place > 2) | (place < d), 0.0, w[W - d]) for d in range(3)]
    west = [jnp.where(up & (place > 2) & (place + d < 6), w[W - d], 0.0) for d in range(3)]
    weights[EDGE] = east[0] + west[0]
    weights[EDGE + 1] = east[1]
    weights[EDGE + 2] = west[1]
    weights[EDGE + 3] = east[2]
    weights[EDGE + 4] = west[2]
    step = column(columns, tracers + 1, levels) / count
    up = step > 0.0
    w = taps(step, count)
    weights[LAT_SIGN] = jnp.where(up, 1.0, 0.0)
    for k in range(4):
        weights[LAT + k] = jnp.where(up, w[W - k], w[k])


def sweep_lon(values, weights, span):
    up = weights[LON_SIGN, span, :] > 0.5
    values = [jnp.where(up, q, turned(q, -W)) for q in values]
    w = [weights[LON + k, span, :] for k in range(4)]
    return [w[0] * q + w[1] * turned(q, 1) + w[2] * turned(q, 2) + w[3] * turned(q, 3) for q in values]


def own_network_kernel(tracers, levels, rows, mine, other, w_in, w_mid, w_out, tendency, token, x):
    token[...] = jnp.zeros_like(token)
    lev = lax.axis_index("lev")
    width = tracers * levels
    near = pl.ds(pl.multiple_of(lev * width, width), width)
    far = pl.ds(pl.multiple_of((1 - lev) * width, width), width)
    w_last = w_out[near, :]
    for i in range(rows):
        x[near, i * LANES : (i + 1) * LANES] = mine[i]
        x[far, i * LANES : (i + 1) * LANES] = other[i]
    tendency[...] = network(x[...], w_in[...], w_mid, w_last)


def own_sweep_kernel(tracers, levels, rows, fields, tendency, small, active, swept, weights):
    write_weights(weights, small, tracers, levels)
    for g in range(0, levels, GROUP):
        span = slice(g, g + GROUP)
        for t in range(tracers):
            at = t * levels + g
            scale = weights[OUT_SCALE + t, span, :]
            values = []
            for i in range(rows):
                moist = tendency[at : at + GROUP, i * LANES : (i + 1) * LANES].astype(F32)
                q = fields[pl.ds(at * rows + i, GROUP, stride=rows), :]
                values.append(q + scale * moist * active[i : i + 1, :])
            for i, q in enumerate(sweep_lon(values, weights, span)):
                swept[i, at : at + GROUP, :] = q


def read_scale(message, which, n, tracers, levels):
    at = SCALE_LANE + 2 * tracers * which + n
    return jnp.broadcast_to(message[:levels, at : at + 1], (levels, LANES))


def row_input_kernel(tracers, levels, moves, packs, *refs):
    count = len(moves)
    edge, edge_other, (w_in, w_mid, hidden, fields, masks, x) = refs[:count], refs[count : 2 * count], refs[2 * count :]
    lev = lax.axis_index("lev")
    width = tracers * levels
    tail = W * width
    for which, source in ((0, edge), (1, edge_other)):
        start = lev * width if which == 0 else (1 - lev) * width
        for n in range(count):
            unit = inverse_scale(from_fixed(source[n][tail : tail + levels, :])) * (1.0 / FIXED_ONE)
            for t in range(tracers):
                in_scale = read_scale(packs, which, t, tracers, levels)
                scale = jnp.broadcast_to(unit[:, t : t + 1], (levels, LANES))
                to = pl.ds(pl.multiple_of(start + t * levels, levels), levels)
                parts = [(r * tracers + t) * levels for r in range(W)]
                values = [from_fixed(source[n][part : part + levels, :]) * scale for part in parts]
                for r, value in enumerate(values):
                    column_at = (n * W + r) * LANES
                    x[to, column_at : column_at + LANES] = (value * in_scale).astype(BF16)
                    if which == 0:
                        fields[n, t * W + r] = value
    for n in range(count):
        masks[n] = from_fixed(edge[n][tail + levels :, :])
    hidden[...] = middle_layers(first_layer(x[...], w_in[...]), w_mid, range(EARLY_LAYERS))


def edge_corrections(values, weights, head, moves):
    if len(moves) == 2:
        near = (weights[LAT_SIGN] > 0.5) | (lane_ids(values[0].shape[0]) < 48)
        values = [jnp.where(near, q, turned(q, -18)) for q in values]
    east = jnp.where(head, LANES - 1, 1), jnp.where(head, LANES - 2, 2)
    w = [jnp.where(head, weights[EDGE + 2 * k], weights[EDGE + 2 * k - 1]) for k in (1, 2)]
    return [weights[EDGE] * q + w[0] * turned(q, east[0]) + w[1] * turned(q, east[1]) for q in values]


def halo_network_kernel(tracers, levels, rows, moves, _, ring, *refs):
    count = len(moves)
    corner = refs[:count]
    weights, w_in, w_mid, w_out, mine, other, hidden, masks, x = refs[count:]
    lat, lev = lax.axis_index("lat"), lax.axis_index("lev")
    width = tracers * levels
    head = lev == 0
    lane = lane_ids(levels)
    west = (lane % 6 >= 3) == head
    shifts = [jnp.where(head, a, b) for a, b in ((W, 0), (0, LANES - W))]
    half = levels // 2

    def place(numbers, which, extra):
        moved = []
        for shift in shifts:
            shift = shift + (extra + LANES - HALF_LANES * which)
            shift = jnp.where(shift >= 2 * LANES, shift - 2 * LANES, jnp.where(shift >= LANES, shift - LANES, shift))
            moved.append(turned(numbers, shift))
        return moved

    def unpack(numbers_of, size, which):
        lane_part = lane[:size]
        values = place(numbers_of(ring), which, 0)
        used = lane_part < 48
        for n, move in enumerate(moves):
            base = 48 + 18 * n
            here = (lane_part >= base) & (lane_part < base + 18)
            beside = place(numbers_of(corner[n]), which, base - 6 * first_row_received(move, lat, rows))
            values = [jnp.where(here, q, value) for q, value in zip(beside, values)]
            used = used | here
        used = used & west[:size]
        return [jnp.where(used, value, 0.0) for value in values]

    def mask_of(message):
        low, high = (
            turned(message[levels + EXTRA * n : levels + EXTRA * (n + 1), :], HALF_LANES // 2 * n - SCALE_LANE) for n in range(2)
        )
        lane_part = lane[:EXTRA]
        return jnp.where(lane_part < HALF_LANES // 2, low, jnp.where(lane_part < HALF_LANES, high, 0.0))

    mask = unpack(mask_of, EXTRA, 0)[0][:1]
    far = pl.ds(pl.multiple_of((1 - lev) * width, width), width)
    halos, scales = [], []
    for which in range(2):
        start = lev * width if which == 0 else (1 - lev) * width
        values = unpack(lambda message: message[:levels, :], levels, which)
        values.append(jnp.concatenate(unpack(lambda message: message[levels:, :], half, which), axis=0))
        for t, value in enumerate(values):
            in_scale, out_scale = (read_scale(ring, which, n, tracers, levels) for n in (t, tracers + t))
            halos.append(value)
            scales.append(out_scale)
            x[pl.ds(pl.multiple_of(start + t * levels, levels), levels), :] = (value * in_scale).astype(BF16)
    hidden[...] = middle_layers(first_layer(x[...], w_in[...]), w_mid, range(len(w_mid)))
    mine[...] = jnp.stack(halos[:tracers])
    masks[...] = jnp.broadcast_to(mask, masks.shape)
    tendency = last_layer(hidden[...], w_out[far, :]).astype(F32)
    values = [
        halos[tracers + t] + scales[tracers + t] * tendency[t * levels : (t + 1) * levels] * mask for t in range(tracers)
    ]
    for t, q in enumerate(edge_corrections(values, weights, lev == 0, moves)):
        other[t] = q


def row_kernel(tracers, levels, moves, hidden, fields, masks, halo, edge_hidden, edge_mask, weights, w_mid, w_out, beyond, fix, tendency):
    lev = lax.axis_index("lev")
    width = tracers * levels
    near = pl.ds(pl.multiple_of(lev * width, width), width)
    outer = middle_layers(hidden[...], w_mid, range(EARLY_LAYERS, len(w_mid)))
    tendency[...] = last_layer(jnp.concatenate([edge_hidden[...], outer], axis=0), w_out[near, :])
    values = [
        halo[t] + weights[OUT_SCALE + t] * tendency[t * levels : (t + 1) * levels, :LANES].astype(F32) * edge_mask[0:1, :]
        for t in range(tracers)
    ]
    for t, q in enumerate(edge_corrections(values, weights, lev == 0, moves)):
        fix[t] = q
    up = weights[LAT_SIGN] > 0.5
    values = []
    for t in range(tracers):
        for r in range(W):
            rows_q = []
            for n in range(len(moves)):
                column_at = (1 + n * W + r) * LANES
                moist = tendency[t * levels : (t + 1) * levels, column_at : column_at + LANES].astype(F32)
                rows_q.append(fields[n, t * W + r] + weights[OUT_SCALE + t] * moist * masks[n, r : r + 1, :])
            values.append(jnp.where(up, rows_q[0], rows_q[1]) if len(moves) == 2 else rows_q[0])
    for n, q in enumerate(sweep_lon(values, weights, slice(0, levels))):
        beyond[n] = q


def finish_kernel(tracers, levels, rows, moves, swept, weights, fix_mine, fix_other, beyond, out, result, sems):
    lat = lax.axis_index("lat")
    southward = jnp.where(lat == 0, 0.0, 1.0)
    copies = []
    lane = lane_ids(HALF_GROUP)
    at_edge = (lane < W) | (lane >= LANES - W)
    for g in range(0, levels, HALF_GROUP):
        span = slice(g, g + HALF_GROUP)
        sign = weights[LAT_SIGN, span, :]
        up = sign > 0.5
        w = [weights[LAT + k, span, :] for k in range(4)]
        for t in range(tracers):
            at = t * levels + g
            fix = fix_mine[t, span, :] + fix_other[t, span, :]

            def fixed(value, first):
                return value + jnp.where(at_edge, turned(fix, LANES - W - first), 0.0)

            inner = [fixed(swept[i, at : at + HALF_GROUP, :], 6 * i) for i in range(rows)]
            outer = [fixed(beyond[t * W + r, span, :], 48 + 6 * r) for r in range(W)]
            if len(moves) == 1:
                outer = [jnp.where(sign == southward, q, 0.0) for q in outer]
            line = []
            for i in range(rows + W):
                above = outer[i] if i < W else inner[i - W]
                below = inner[i] if i < rows else outer[i - rows]
                line.append(jnp.where(up, above, below))
            results = [w[0] * line[i] + w[1] * line[i + 1] + w[2] * line[i + 2] + w[3] * line[i + 3] for i in range(rows)]
            for i, value in enumerate(results):
                result[pl.ds(at * rows + i, HALF_GROUP, stride=rows), :] = value
            part = pl.ds(at * rows, HALF_GROUP * rows)
            copies.append(pltpu.make_async_copy(result.at[part], out.at[part], sems.at[len(copies)]))
            copies[-1].start()
    for copy in copies:
        copy.wait()


def call(kernel, out_shape, scratch, name, **specs):
    return pl.pallas_call(
        kernel,
        out_shape=out_shape,
        **specs,
        scratch_shapes=scratch,
        compiler_params=pltpu.CompilerParams(vmem_limit_bytes=VMEM_LIMIT),
        cost_estimate=pl.CostEstimate(flops=10**10, bytes_accessed=0, transcendentals=0),
        name=name,
    )


def swap_cores(x):
    return lax.ppermute(x, "lev", [(0, 1), (1, 0)])


def send(x, move, along_lon):
    axes = ("lon", "lat", "lev")
    lon_count, lat_count = lax.axis_size("lon"), lax.axis_size("lat")
    pairs = []
    for i in range(lon_count):
        for j in range(lat_count):
            to_lat = j if move is None else 1 - j if move == 0 else j + move
            if not 0 <= to_lat < lat_count:
                continue
            for k in range(2):
                to_lon = (i + 1 - 2 * k) % lon_count if along_lon else i
                pairs.append(((i * lat_count + j) * 2 + k, (to_lon * lat_count + to_lat) * 2 + k))
    return lax.ppermute(x, axes, pairs)


def on_device(fields, in_scale, out_scale, w_in, w_mid, w_out, storm_mask, balance, substeps, courant):
    tracers, levels, rows, columns = fields.shape
    width = tracers * levels
    moves = (0,) if lax.axis_size("lat") == 2 else (1, -1)
    count = len(moves)
    flat = fields.reshape(width * rows, columns)
    edge_shape = jax.ShapeDtypeStruct((W * width + levels + 2 * EXTRA, columns), jnp.int16)
    pack_shape = jax.ShapeDtypeStruct((levels + levels // 2, LANES), F32)
    inputs = (in_scale, storm_mask, balance.T, out_scale, courant, substeps.reshape(1, levels))
    inputs = [pltpu.with_memory_space_constraint(x, pltpu.HBM) for x in inputs]
    mask_shape = jax.ShapeDtypeStruct((rows, columns), F32)
    small, storm, scale_lanes, in_scales = call(
        functools.partial(scalar_kernel, tracers, levels, rows),
        [jax.ShapeDtypeStruct((EXTRA, LANES), F32), mask_shape, jax.ShapeDtypeStruct((2, levels, LANES), F32),
         jax.ShapeDtypeStruct((tracers, levels, LANES), F32)],
        [pltpu.VMEM(x.shape, x.dtype) for x in inputs]
        + [pltpu.VMEM((EXTRA, LANES), F32), pltpu.SemaphoreType.DMA((len(inputs),))],
        "scalars",
        in_specs=[pl.BlockSpec(memory_space=pltpu.HBM)] * len(inputs),
    )(*inputs)
    keep, give, active, features = call(
        functools.partial(edge_kernel, tracers, levels, rows),
        [pack_shape, pack_shape, mask_shape, jax.ShapeDtypeStruct((rows, width, columns), BF16)],
        [],
        "edges",
    )(flat, small, storm, scale_lanes, in_scales)
    given = swap_cores(give)
    features_other = swap_cores(features)
    edge_rows = call(
        functools.partial(row_message_kernel, tracers, levels, rows, moves),
        [edge_shape] * count,
        [],
        "row_messages",
    )(flat, active)
    packs = keep + given
    corner = [send(packs, move, True) for move in moves]
    ring = send(packs, None, True)
    edge = [send(e, move, False) for e, move in zip(edge_rows, moves)]

    tendency, token = call(
        functools.partial(own_network_kernel, tracers, levels, rows),
        [jax.ShapeDtypeStruct((width, rows * columns), BF16), jax.ShapeDtypeStruct((2 * EXTRA, LANES), jnp.int16)],
        [pltpu.VMEM((2 * width, rows * columns), BF16)],
        "own_network",
    )(features, features_other, w_in, w_mid, w_out)
    swept, weights = call(
        functools.partial(own_sweep_kernel, tracers, levels, rows),
        [jax.ShapeDtypeStruct((rows, width, columns), F32), jax.ShapeDtypeStruct((PLANES, levels, LANES), F32)],
        [],
        "own_sweep",
    )(flat, tendency, small, active)

    fix_shape = jax.ShapeDtypeStruct((tracers, levels, LANES), F32)
    edge_other = [swap_cores(e + token[:1]) for e in edge]
    total = W * count * LANES
    physics_shape = jax.ShapeDtypeStruct((count, tracers * W, levels, LANES), F32)
    hidden, row_fields, row_masks = call(
        functools.partial(row_input_kernel, tracers, levels, moves),
        [jax.ShapeDtypeStruct((total, w_in.shape[0]), BF16), physics_shape,
         jax.ShapeDtypeStruct((count, 2 * EXTRA, LANES), F32)],
        [pltpu.VMEM((2 * width, total), BF16)],
        "row_input",
    )(packs, *edge, *edge_other, w_in, w_mid)
    halo, fix_given, edge_hidden, edge_mask = call(
        functools.partial(halo_network_kernel, tracers, levels, rows, moves),
        [fix_shape, fix_shape, jax.ShapeDtypeStruct((LANES, w_in.shape[0]), BF16),
         jax.ShapeDtypeStruct((EXTRA, LANES), F32)],
        [pltpu.VMEM((2 * width, LANES), BF16)],
        "halo_network",
    )(row_masks, ring, *corner, weights, w_in, w_mid, w_out)
    fix_other = swap_cores(fix_given)
    beyond, fix_mine = call(
        functools.partial(row_kernel, tracers, levels, moves),
        [jax.ShapeDtypeStruct((tracers * W, levels, LANES), F32), fix_shape],
        [pltpu.VMEM((width, LANES + total), BF16)],
        "row_network",
    )(hidden, row_fields, row_masks, halo, edge_hidden, edge_mask, weights, w_mid, w_out)
    out = call(
        functools.partial(finish_kernel, tracers, levels, rows, moves),
        jax.ShapeDtypeStruct((width * rows, columns), F32),
        [pltpu.VMEM((width * rows, columns), F32), pltpu.SemaphoreType.DMA((width // HALF_GROUP,))],
        "finish",
        out_specs=pl.BlockSpec(memory_space=pltpu.HBM),
    )(swept, weights, fix_mine, fix_other, beyond)
    return out.reshape(fields.shape)


def solution(mesh):
    in_specs = (
        P("lev", None, ("group", "lat"), "lon"),
        P("lev", None),
        P("lev", None),
        P(),
        P(),
        P(),
        P(("group", "lat"), "lon"),
        P(("group", "lat"), None),
        P(),
        P(),
    )
    out_specs = P("lev", None, ("group", "lat"), "lon")
    return jax.shard_map(
        on_device, mesh=mesh, in_specs=in_specs, out_specs=out_specs, check_vma=False
    )
```

```python
import functools

import jax
import jax.numpy as jnp
from jax import lax
from jax.experimental import pallas as pl
from jax.experimental.pallas import tpu as pltpu
from jax.sharding import PartitionSpec as P

W = 3
LANES = 128
HALF_LANES = 48
TARGET_ROW = 6
SCALE_LANE = 96
FIELD_BOUND = 8.0
FIXED_ONE = 32768.0 / FIELD_BOUND
FIXED_MOST = 32767.0
EXTRA = 8
F32 = jnp.float32
BF16 = jnp.bfloat16
GROUP = 32
HALF_GROUP = 16
EARLY_LAYERS = 0
VMEM_LIMIT = 40 * 1024 * 1024


def lane_ids(rows):
    return lax.broadcasted_iota(jnp.int32, (rows, LANES), 1)


def turned(x, shift):
    if isinstance(shift, int):
        shift %= LANES
        if shift == 0:
            return x
    return pltpu.roll(x, shift, 1)


def silu(v):
    half = 0.5 * v
    return half + half * jnp.tanh(half)


def as_columns(scratch, parts):
    scratch[...] = jnp.zeros_like(scratch)
    at = 0
    for part in parts:
        scratch[at : at + part.shape[0], : part.shape[1]] = part
        at += part.shape[0]
    return scratch[...].T


def column(turned_rows, index, levels):
    return jnp.broadcast_to(turned_rows[:levels, index : index + 1], (levels, LANES))


def side_message(edges, west, base):
    lane = lane_ids(1)
    east = lane % 6 < 3
    used = (lane >= base) & (lane < base + HALF_LANES)
    half = edges[2].shape[0] // 2
    even = jnp.where(west, base - W + LANES, base + LANES) % LANES
    odd = jnp.where(west, base, base + W)
    pairs = ((edges[0], edges[1]), (edges[2][:half], edges[2][half:]))
    return [jnp.where(used, jnp.where(east, turned(p, even), turned(q, odd)), 0.0) for p, q in pairs]


def scalar_kernel(tracers, levels, rows, *refs):
    sources, (small, mask, scale_lanes, in_scales), refs = refs[:6], refs[6:10], refs[10:]
    (in_scale, storm, balance, *loads), scratch, sems = refs[:6], refs[6], refs[7]
    copies = [
        pltpu.make_async_copy(source, into, sems.at[n]) for n, (source, into) in enumerate(zip(sources, refs[:6]))
    ]
    for copy in copies:
        copy.start()
    for copy in copies[:4]:
        copy.wait()
    lon = lax.axis_index("lon")
    position = lax.broadcasted_iota(jnp.int32, balance.shape, 0)
    target = jnp.max(jnp.where(position == lon, balance[...], -1).astype(F32), axis=0, keepdims=True)
    scales = as_columns(scratch, [in_scale[...], loads[0][...]])
    lane = lane_ids(levels)
    own_scales, given_scales = jnp.zeros((levels, LANES), F32), jnp.zeros((levels, LANES), F32)
    for n in range(2 * tracers):
        scale = column(scales, n, levels)
        own_scales = jnp.where(lane == SCALE_LANE + n, scale, own_scales)
        given_scales = jnp.where(lane == SCALE_LANE + 2 * tracers + n, scale, given_scales)
        if n < tracers:
            in_scales[n] = scale
    scale_lanes[0], scale_lanes[1] = own_scales, given_scales
    for copy in copies[4:]:
        copy.wait()
    small[...] = jnp.zeros_like(small)
    at = 0
    for load in loads:
        small[at : at + load.shape[0], : load.shape[1]] = load[...].astype(F32)
        at += load.shape[0]
    small[at : at + 1, :rows] = target
    mask[...] = storm[...].astype(F32)


def edge_kernel(tracers, levels, rows, fields, small, storm, scale_lanes, in_scales, keep, give, active, features):
    lane = lane_ids(levels)
    half = levels // 2
    head = lax.axis_index("lev") == 0
    edges, values = [], []
    for t in range(tracers):
        pack = jnp.zeros((levels, LANES), F32)
        for i in range(rows):
            x = fields[pl.ds((t * levels) * rows + i, levels, stride=rows), :]
            values.append((x * in_scales[t]).astype(BF16))
            pack = jnp.where((lane >= 6 * i) & (lane < 6 * i + 6), turned(x, 6 * i + W), pack)
        edges.append(pack)
    mask = jnp.where(column(small[...].T, TARGET_ROW, rows) >= 0.0, storm[...], 0.0)
    lane = lane_ids(rows)
    row = lax.broadcasted_iota(jnp.int32, (rows, LANES), 0)
    mask_pack = pltpu.roll(mask, W, 1, stride=6, stride_axis=0)
    mask_pack = jnp.where((lane >= 6 * row) & (lane < 6 * row + 6), mask_pack, 0.0)
    mask_pack = jnp.broadcast_to(jnp.sum(mask_pack, axis=0, keepdims=True), (EXTRA, LANES))
    lane = lane_ids(1)
    east = lane % 6 < 3
    side_mask = jnp.where(head, jnp.where(east, mask_pack, 0.0), turned(jnp.where(east, 0.0, mask_pack), -W))
    free = (lane >= SCALE_LANE) & (lane < SCALE_LANE + HALF_LANES // 2)
    side_masks = [jnp.where(free, turned(side_mask, SCALE_LANE - HALF_LANES // 2 * n), 0.0) for n in range(2)]
    kept, third = side_message(edges, ~head, 0)
    passed = side_message(edges, head, HALF_LANES)
    keep[:levels] = kept + scale_lanes[0]
    give[:levels] = passed[0] + scale_lanes[1]
    for n in range(2):
        at = EXTRA * n
        keep[levels + at : levels + at + EXTRA] = third[at : at + EXTRA] + side_masks[n]
    keep[levels + 2 * EXTRA :] = third[2 * EXTRA :]
    give[levels:] = passed[1]
    active[...] = mask
    for n, x in enumerate(values):
        t, i = n // rows, n % rows
        features[i, t * levels : (t + 1) * levels, :] = x


def binary_scale(largest):
    largest = largest * (1.0 / FIELD_BOUND)
    power, scale = jnp.zeros_like(largest), jnp.ones_like(largest)
    for bits in (64, 32, 16, 8, 4, 2, 1):
        small = largest < 2.0**-bits
        largest = jnp.where(small, largest * 2.0**bits, largest)
        scale = jnp.where(small, scale * 2.0**bits, scale)
        power = jnp.where(small, power + float(bits), power)
    return scale, power


def inverse_scale(power):
    scale = jnp.ones_like(power)
    for bits in (64, 32, 16, 8, 4, 2, 1):
        large = power > bits - 0.5
        scale = jnp.where(large, scale * 2.0**-bits, scale)
        power = jnp.where(large, power - float(bits), power)
    return scale


def to_fixed(x):
    return jnp.round(x).astype(jnp.int32).astype(jnp.int16)


def from_fixed(x):
    return x.astype(jnp.int32).astype(F32)


def row_message_kernel(tracers, levels, rows, moves, fields, active, *edge_rows):
    lat = lax.axis_index("lat")
    lane = lane_ids(levels)
    row = lax.broadcasted_iota(jnp.int32, (2 * EXTRA, LANES), 0)
    tail = W * tracers * levels
    for move, out in zip(moves, edge_rows):
        start = first_row_sent(move, lat, rows)
        values = [
            [fields[pl.ds((t * levels) * rows + start + r, levels, stride=rows), :] for r in range(W)]
            for t in range(tracers)
        ]
        largest = [jnp.max(jnp.maximum(jnp.maximum(jnp.abs(a), jnp.abs(b)), jnp.abs(c)), axis=1, keepdims=True) for a, b, c in values]
        bound = jnp.zeros((levels, LANES), F32)
        for t in range(tracers):
            bound = jnp.where(lane == t, largest[t], bound)
        scale, power = binary_scale(bound)
        for t in range(tracers):
            to_one = jnp.broadcast_to(scale[:, t : t + 1], (levels, LANES))
            for r, x in enumerate(values[t]):
                x = jnp.clip(x * to_one * FIXED_ONE, -FIXED_MOST, FIXED_MOST)
                out[(r * tracers + t) * levels : (r * tracers + t + 1) * levels, :] = to_fixed(x)
        out[tail : tail + levels, :] = to_fixed(power)
        mask = jnp.zeros(row.shape, F32)
        for r in range(W):
            mask = jnp.where(row == r, active[pl.ds(start + r, 1), :], mask)
        out[tail + levels :, :] = to_fixed(mask)


def first_row_sent(move, lat, rows):
    if move == 0:
        return jnp.where(lat == 0, rows - W, 0)
    return rows - W if move > 0 else 0


def first_row_received(move, lat, rows):
    if move == 0:
        return jnp.where(lat == 0, 0, rows - W)
    return rows - W if move > 0 else 0


def network(x, w_in, w_mid, w_last):
    hidden = silu(jnp.dot(w_in, x, preferred_element_type=F32)).astype(BF16)
    for layer in range(len(w_mid)):
        hidden = silu(jnp.dot(w_mid[layer], hidden, preferred_element_type=F32)).astype(BF16)
    return jnp.dot(w_last, hidden, preferred_element_type=F32).astype(BF16)


def taps(step, count):
    first = jnp.abs(step)
    second = jnp.where(count > 1.5, first, 0.0)
    third = jnp.where(count > 2.5, first, 0.0)
    rest = [1.0 - a for a in (first, second, third)]
    return (
        rest[0] * rest[1] * rest[2],
        first * rest[1] * rest[2] + rest[0] * second * rest[2] + rest[0] * rest[1] * third,
        first * second * rest[2] + first * rest[1] * third + rest[0] * second * third,
        first * second * third,
    )


def first_layer(x, w_in):
    return silu(lax.dot_general(x, w_in, (((0,), (1,)), ((), ())), preferred_element_type=F32)).astype(BF16)


def weights_times(hidden, w):
    return lax.dot_general(hidden, w, (((1,), (1,)), ((), ())), preferred_element_type=F32)


def middle_layers(hidden, w_mid, layers):
    for k in layers:
        hidden = silu(weights_times(hidden, w_mid[k])).astype(BF16)
    return hidden


def last_layer(hidden, w_last):
    return weights_times(w_last, hidden).astype(BF16)


OUT_SCALE, LON, LON_SIGN, LAT, LAT_SIGN, EDGE, PLANES = 0, 3, 7, 8, 12, 13, 18


def write_weights(weights, small, tracers, levels):
    columns = small[...].T
    for t in range(tracers):
        weights[OUT_SCALE + t] = column(columns, t, levels)
    count = column(columns, tracers + 2, levels)
    lane = lane_ids(levels)
    place = lane % 6
    step = column(columns, tracers, levels) / count
    up = step > 0.0
    w = taps(step, count)
    weights[LON_SIGN] = jnp.where(up, 1.0, 0.0)
    for k in range(4):
        weights[LON + k] = jnp.where(
            up, jnp.where(lane >= k, w[k], 0.0), jnp.where(lane < LANES - (W - k), w[W - k], 0.0)
        )
    east = [jnp.where(up | (place > 2) | (place < d), 0.0, w[W - d]) for d in range(3)]
    west = [jnp.where(up & (place > 2) & (place + d < 6), w[W - d], 0.0) for d in range(3)]
    weights[EDGE] = east[0] + west[0]
    weights[EDGE + 1] = east[1]
    weights[EDGE + 2] = west[1]
    weights[EDGE + 3] = east[2]
    weights[EDGE + 4] = west[2]
    step = column(columns, tracers + 1, levels) / count
    up = step > 0.0
    w = taps(step, count)
    weights[LAT_SIGN] = jnp.where(up, 1.0, 0.0)
    for k in range(4):
        weights[LAT + k] = jnp.where(up, w[W - k], w[k])


def sweep_lon(values, weights, span):
    up = weights[LON_SIGN, span, :] > 0.5
    values = [jnp.where(up, q, turned(q, -W)) for q in values]
    w = [weights[LON + k, span, :] for k in range(4)]
    return [w[0] * q + w[1] * turned(q, 1) + w[2] * turned(q, 2) + w[3] * turned(q, 3) for q in values]


def own_network_kernel(tracers, levels, rows, mine, other, w_in, w_mid, w_out, tendency, token, x):
    token[...] = jnp.zeros_like(token)
    lev = lax.axis_index("lev")
    width = tracers * levels
    near = pl.ds(pl.multiple_of(lev * width, width), width)
    far = pl.ds(pl.multiple_of((1 - lev) * width, width), width)
    w_last = w_out[near, :]
    for i in range(rows):
        x[near, i * LANES : (i + 1) * LANES] = mine[i]
        x[far, i * LANES : (i + 1) * LANES] = other[i]
    tendency[...] = network(x[...], w_in[...], w_mid, w_last)


def own_sweep_kernel(tracers, levels, rows, fields, tendency, small, active, swept, weights):
    write_weights(weights, small, tracers, levels)
    for g in range(0, levels, GROUP):
        span = slice(g, g + GROUP)
        for t in range(tracers):
            at = t * levels + g
            scale = weights[OUT_SCALE + t, span, :]
            values = []
            for i in range(rows):
                moist = tendency[at : at + GROUP, i * LANES : (i + 1) * LANES].astype(F32)
                q = fields[pl.ds(at * rows + i, GROUP, stride=rows), :]
                values.append(q + scale * moist * active[i : i + 1, :])
            for i, q in enumerate(sweep_lon(values, weights, span)):
                swept[i, at : at + GROUP, :] = q


def read_scale(message, which, n, tracers, levels):
    at = SCALE_LANE + 2 * tracers * which + n
    return jnp.broadcast_to(message[:levels, at : at + 1], (levels, LANES))


def row_input_kernel(tracers, levels, moves, packs, *refs):
    count = len(moves)
    edge, edge_other, (w_in, w_mid, hidden, fields, masks, x) = refs[:count], refs[count : 2 * count], refs[2 * count :]
    lev = lax.axis_index("lev")
    width = tracers * levels
    tail = W * width
    for which, source in ((0, edge), (1, edge_other)):
        start = lev * width if which == 0 else (1 - lev) * width
        for n in range(count):
            unit = inverse_scale(from_fixed(source[n][tail : tail + levels, :])) * (1.0 / FIXED_ONE)
            for t in range(tracers):
                in_scale = read_scale(packs, which, t, tracers, levels)
                scale = jnp.broadcast_to(unit[:, t : t + 1], (levels, LANES))
                to = pl.ds(pl.multiple_of(start + t * levels, levels), levels)
                parts = [(r * tracers + t) * levels for r in range(W)]
                values = [from_fixed(source[n][part : part + levels, :]) * scale for part in parts]
                for r, value in enumerate(values):
                    column_at = (n * W + r) * LANES
                    x[to, column_at : column_at + LANES] = (value * in_scale).astype(BF16)
                    if which == 0:
                        fields[n, t * W + r] = value
    for n in range(count):
        masks[n] = from_fixed(edge[n][tail + levels :, :])
    hidden[...] = middle_layers(first_layer(x[...], w_in[...]), w_mid, range(EARLY_LAYERS))


def edge_corrections(values, weights, head, moves):
    if len(moves) == 2:
        near = (weights[LAT_SIGN] > 0.5) | (lane_ids(values[0].shape[0]) < 48)
        values = [jnp.where(near, q, turned(q, -18)) for q in values]
    east = jnp.where(head, LANES - 1, 1), jnp.where(head, LANES - 2, 2)
    w = [jnp.where(head, weights[EDGE + 2 * k], weights[EDGE + 2 * k - 1]) for k in (1, 2)]
    return [weights[EDGE] * q + w[0] * turned(q, east[0]) + w[1] * turned(q, east[1]) for q in values]


def halo_network_kernel(tracers, levels, rows, moves, _, ring, *refs):
    count = len(moves)
    corner = refs[:count]
    weights, w_in, w_mid, w_out, mine, other, hidden, masks, x = refs[count:]
    lat, lev = lax.axis_index("lat"), lax.axis_index("lev")
    width = tracers * levels
    head = lev == 0
    lane = lane_ids(levels)
    west = (lane % 6 >= 3) == head
    shifts = [jnp.where(head, a, b) for a, b in ((W, 0), (0, LANES - W))]
    half = levels // 2

    def place(numbers, which, extra):
        moved = []
        for shift in shifts:
            shift = shift + (extra + LANES - HALF_LANES * which)
            shift = jnp.where(shift >= 2 * LANES, shift - 2 * LANES, jnp.where(shift >= LANES, shift - LANES, shift))
            moved.append(turned(numbers, shift))
        return moved

    def unpack(numbers_of, size, which):
        lane_part = lane[:size]
        values = place(numbers_of(ring), which, 0)
        used = lane_part < 48
        for n, move in enumerate(moves):
            base = 48 + 18 * n
            here = (lane_part >= base) & (lane_part < base + 18)
            beside = place(numbers_of(corner[n]), which, base - 6 * first_row_received(move, lat, rows))
            values = [jnp.where(here, q, value) for q, value in zip(beside, values)]
            used = used | here
        used = used & west[:size]
        return [jnp.where(used, value, 0.0) for value in values]

    def mask_of(message):
        low, high = (
            turned(message[levels + EXTRA * n : levels + EXTRA * (n + 1), :], HALF_LANES // 2 * n - SCALE_LANE) for n in range(2)
        )
        lane_part = lane[:EXTRA]
        return jnp.where(lane_part < HALF_LANES // 2, low, jnp.where(lane_part < HALF_LANES, high, 0.0))

    mask = unpack(mask_of, EXTRA, 0)[0][:1]
    far = pl.ds(pl.multiple_of((1 - lev) * width, width), width)
    halos, scales = [], []
    for which in range(2):
        start = lev * width if which == 0 else (1 - lev) * width
        values = unpack(lambda message: message[:levels, :], levels, which)
        values.append(jnp.concatenate(unpack(lambda message: message[levels:, :], half, which), axis=0))
        for t, value in enumerate(values):
            in_scale, out_scale = (read_scale(ring, which, n, tracers, levels) for n in (t, tracers + t))
            halos.append(value)
            scales.append(out_scale)
            x[pl.ds(pl.multiple_of(start + t * levels, levels), levels), :] = (value * in_scale).astype(BF16)
    hidden[...] = middle_layers(first_layer(x[...], w_in[...]), w_mid, range(len(w_mid)))
    mine[...] = jnp.stack(halos[:tracers])
    masks[...] = jnp.broadcast_to(mask, masks.shape)
    tendency = last_layer(hidden[...], w_out[far, :]).astype(F32)
    values = [
        halos[tracers + t] + scales[tracers + t] * tendency[t * levels : (t + 1) * levels] * mask for t in range(tracers)
    ]
    for t, q in enumerate(edge_corrections(values, weights, lev == 0, moves)):
        other[t] = q


def row_kernel(tracers, levels, moves, hidden, fields, masks, halo, edge_hidden, edge_mask, weights, w_mid, w_out, beyond, fix, tendency):
    lev = lax.axis_index("lev")
    width = tracers * levels
    near = pl.ds(pl.multiple_of(lev * width, width), width)
    outer = middle_layers(hidden[...], w_mid, range(EARLY_LAYERS, len(w_mid)))
    tendency[...] = last_layer(jnp.concatenate([edge_hidden[...], outer], axis=0), w_out[near, :])
    values = [
        halo[t] + weights[OUT_SCALE + t] * tendency[t * levels : (t + 1) * levels, :LANES].astype(F32) * edge_mask[0:1, :]
        for t in range(tracers)
    ]
    for t, q in enumerate(edge_corrections(values, weights, lev == 0, moves)):
        fix[t] = q
    up = weights[LAT_SIGN] > 0.5
    values = []
    for t in range(tracers):
        for r in range(W):
            rows_q = []
            for n in range(len(moves)):
                column_at = (1 + n * W + r) * LANES
                moist = tendency[t * levels : (t + 1) * levels, column_at : column_at + LANES].astype(F32)
                rows_q.append(fields[n, t * W + r] + weights[OUT_SCALE + t] * moist * masks[n, r : r + 1, :])
            values.append(jnp.where(up, rows_q[0], rows_q[1]) if len(moves) == 2 else rows_q[0])
    for n, q in enumerate(sweep_lon(values, weights, slice(0, levels))):
        beyond[n] = q


def finish_kernel(tracers, levels, rows, moves, swept, weights, fix_mine, fix_other, beyond, out, result, sems):
    lat = lax.axis_index("lat")
    southward = jnp.where(lat == 0, 0.0, 1.0)
    copies = []
    lane = lane_ids(HALF_GROUP)
    at_edge = (lane < W) | (lane >= LANES - W)
    for g in range(0, levels, HALF_GROUP):
        span = slice(g, g + HALF_GROUP)
        sign = weights[LAT_SIGN, span, :]
        up = sign > 0.5
        w = [weights[LAT + k, span, :] for k in range(4)]
        for t in range(tracers):
            at = t * levels + g
            fix = fix_mine[t, span, :] + fix_other[t, span, :]

            def fixed(value, first):
                return value + jnp.where(at_edge, turned(fix, LANES - W - first), 0.0)

            inner = [fixed(swept[i, at : at + HALF_GROUP, :], 6 * i) for i in range(rows)]
            outer = [fixed(beyond[t * W + r, span, :], 48 + 6 * r) for r in range(W)]
            if len(moves) == 1:
                outer = [jnp.where(sign == southward, q, 0.0) for q in outer]
            line = []
            for i in range(rows + W):
                above = outer[i] if i < W else inner[i - W]
                below = inner[i] if i < rows else outer[i - rows]
                line.append(jnp.where(up, above, below))
            results = [w[0] * line[i] + w[1] * line[i + 1] + w[2] * line[i + 2] + w[3] * line[i + 3] for i in range(rows)]
            for i, value in enumerate(results):
                result[pl.ds(at * rows + i, HALF_GROUP, stride=rows), :] = value
            part = pl.ds(at * rows, HALF_GROUP * rows)
            copies.append(pltpu.make_async_copy(result.at[part], out.at[part], sems.at[len(copies)]))
            copies[-1].start()
    for copy in copies:
        copy.wait()


def call(kernel, out_shape, scratch, name, **specs):
    return pl.pallas_call(
        kernel,
        out_shape=out_shape,
        **specs,
        scratch_shapes=scratch,
        compiler_params=pltpu.CompilerParams(vmem_limit_bytes=VMEM_LIMIT),
        cost_estimate=pl.CostEstimate(flops=10**10, bytes_accessed=0, transcendentals=0),
        name=name,
    )


def swap_cores(x):
    return lax.ppermute(x, "lev", [(0, 1), (1, 0)])


def send(x, move, along_lon):
    axes = ("lon", "lat", "lev")
    lon_count, lat_count = lax.axis_size("lon"), lax.axis_size("lat")
    pairs = []
    for i in range(lon_count):
        for j in range(lat_count):
            to_lat = j if move is None else 1 - j if move == 0 else j + move
            if not 0 <= to_lat < lat_count:
                continue
            for k in range(2):
                to_lon = (i + 1 - 2 * k) % lon_count if along_lon else i
                pairs.append(((i * lat_count + j) * 2 + k, (to_lon * lat_count + to_lat) * 2 + k))
    return lax.ppermute(x, axes, pairs)


def on_device(fields, in_scale, out_scale, w_in, w_mid, w_out, storm_mask, balance, substeps, courant):
    tracers, levels, rows, columns = fields.shape
    width = tracers * levels
    moves = (0,) if lax.axis_size("lat") == 2 else (1, -1)
    count = len(moves)
    flat = fields.reshape(width * rows, columns)
    edge_shape = jax.ShapeDtypeStruct((W * width + levels + 2 * EXTRA, columns), jnp.int16)
    pack_shape = jax.ShapeDtypeStruct((levels + levels // 2, LANES), F32)
    inputs = (in_scale, storm_mask, balance.T, out_scale, courant, substeps.reshape(1, levels))
    inputs = [pltpu.with_memory_space_constraint(x, pltpu.HBM) for x in inputs]
    mask_shape = jax.ShapeDtypeStruct((rows, columns), F32)
    small, storm, scale_lanes, in_scales = call(
        functools.partial(scalar_kernel, tracers, levels, rows),
        [jax.ShapeDtypeStruct((EXTRA, LANES), F32), mask_shape, jax.ShapeDtypeStruct((2, levels, LANES), F32),
         jax.ShapeDtypeStruct((tracers, levels, LANES), F32)],
        [pltpu.VMEM(x.shape, x.dtype) for x in inputs]
        + [pltpu.VMEM((EXTRA, LANES), F32), pltpu.SemaphoreType.DMA((len(inputs),))],
        "scalars",
        in_specs=[pl.BlockSpec(memory_space=pltpu.HBM)] * len(inputs),
    )(*inputs)
    keep, give, active, features = call(
        functools.partial(edge_kernel, tracers, levels, rows),
        [pack_shape, pack_shape, mask_shape, jax.ShapeDtypeStruct((rows, width, columns), BF16)],
        [],
        "edges",
    )(flat, small, storm, scale_lanes, in_scales)
    given = swap_cores(give)
    features_other = swap_cores(features)
    edge_rows = call(
        functools.partial(row_message_kernel, tracers, levels, rows, moves),
        [edge_shape] * count,
        [],
        "row_messages",
    )(flat, active)
    packs = keep + given
    corner = [send(packs, move, True) for move in moves]
    ring = send(packs, None, True)
    edge = [send(e, move, False) for e, move in zip(edge_rows, moves)]

    tendency, token = call(
        functools.partial(own_network_kernel, tracers, levels, rows),
        [jax.ShapeDtypeStruct((width, rows * columns), BF16), jax.ShapeDtypeStruct((2 * EXTRA, LANES), jnp.int16)],
        [pltpu.VMEM((2 * width, rows * columns), BF16)],
        "own_network",
    )(features, features_other, w_in, w_mid, w_out)
    swept, weights = call(
        functools.partial(own_sweep_kernel, tracers, levels, rows),
        [jax.ShapeDtypeStruct((rows, width, columns), F32), jax.ShapeDtypeStruct((PLANES, levels, LANES), F32)],
        [],
        "own_sweep",
    )(flat, tendency, small, active)

    fix_shape = jax.ShapeDtypeStruct((tracers, levels, LANES), F32)
    edge_other = [swap_cores(e + token[:1]) for e in edge]
    total = W * count * LANES
    physics_shape = jax.ShapeDtypeStruct((count, tracers * W, levels, LANES), F32)
    hidden, row_fields, row_masks = call(
        functools.partial(row_input_kernel, tracers, levels, moves),
        [jax.ShapeDtypeStruct((total, w_in.shape[0]), BF16), physics_shape,
         jax.ShapeDtypeStruct((count, 2 * EXTRA, LANES), F32)],
        [pltpu.VMEM((2 * width, total), BF16)],
        "row_input",
    )(packs, *edge, *edge_other, w_in, w_mid)
    halo, fix_given, edge_hidden, edge_mask = call(
        functools.partial(halo_network_kernel, tracers, levels, rows, moves),
        [fix_shape, fix_shape, jax.ShapeDtypeStruct((LANES, w_in.shape[0]), BF16),
         jax.ShapeDtypeStruct((EXTRA, LANES), F32)],
        [pltpu.VMEM((2 * width, LANES), BF16)],
        "halo_network",
    )(row_masks, ring, *corner, weights, w_in, w_mid, w_out)
    fix_other = swap_cores(fix_given)
    beyond, fix_mine = call(
        functools.partial(row_kernel, tracers, levels, moves),
        [jax.ShapeDtypeStruct((tracers * W, levels, LANES), F32), fix_shape],
        [pltpu.VMEM((width, LANES + total), BF16)],
        "row_network",
    )(hidden, row_fields, row_masks, halo, edge_hidden, edge_mask, weights, w_mid, w_out)
    out = call(
        functools.partial(finish_kernel, tracers, levels, rows, moves),
        jax.ShapeDtypeStruct((width * rows, columns), F32),
        [pltpu.VMEM((width * rows, columns), F32), pltpu.SemaphoreType.DMA((width // HALF_GROUP,))],
        "finish",
        out_specs=pl.BlockSpec(memory_space=pltpu.HBM),
    )(swept, weights, fix_mine, fix_other, beyond)
    return out.reshape(fields.shape)


def solution(mesh):
    in_specs = (
        P("lev", None, ("group", "lat"), "lon"),
        P("lev", None),
        P("lev", None),
        P(),
        P(),
        P(),
        P(("group", "lat"), "lon"),
        P(("group", "lat"), None),
        P(),
        P(),
    )
    out_specs = P("lev", None, ("group", "lat"), "lon")
    return jax.shard_map(
        on_device, mesh=mesh, in_specs=in_specs, out_specs=out_specs, check_vma=False
    )
```
